32 devices in a mesh: rows: 4 (over y, x), cols: 8 (over z, core).
Axes of the slice: x: 2, y: 2, z: 4, core: 2. Of those that a mesh axis runs over, the one named last changes fastest.
Arguments:
- features: bfloat16 [2, 4096, 100], P(None, ('rows', 'cols')), may hold values from -6 to 6
- adjacency: bfloat16 [2, 4096, 4, 8, 128], P(None, 'rows', None, 'cols'), may hold values from -0.125 to 0.125
- block_mask: int32 [2, 32, 4, 8, 1], P(None, 'rows', None, 'cols'), may hold values 0 or 1
- diagonal: float32 [2, 4096], P(None, ('rows', 'cols')), may hold values from 0.2 to 1
- labels: int32 [2, 4096], P(None, ('rows', 'cols')), may hold values from 0 to 46
- train_mask: int32 [2, 4096], P(None, ('rows', 'cols')), may hold values from 0 to 1, as said below
- params: float32 [4501504], P(('rows', 'cols')), as said below
- first_moment: float32 [4501504], P(('rows', 'cols'))
- second_moment: float32 [4501504], P(('rows', 'cols')), as said below
Outputs:
- new_params: float32 [4501504], P(('rows', 'cols'))
- new_first: float32 [4501504], P(('rows', 'cols'))
- new_second: float32 [4501504], P(('rows', 'cols'))
- grad_norm: float32 [], replicated
- loss_sum: float32 [], replicated
- node_total: float32 [], replicated
- class_bias_grad: float32 [47], replicated
The draws below stay inside these ranges and needn't reach their ends.
Inputs may be any that keep to these rules, and one draw needn't show every extreme that they name: `train_mask`: the share of ones rises with the node's index within a micro-batch. `params`: entries beyond 4499503 are padding. `second_moment`: positive.
All inputs are finite; a program needn't handle non-finite values. No bound on the sum of `block_mask` on one device may be relied on, other than what follows from the above.
Results may differ from the reference program's by a relative error of at most 0.0068.
Values may be sent and summed in bfloat16 or wider, within the bound.
No kernel may reach another device: no remote copies, remote signals or barrier semaphores. Data moves between devices by JAX's collectives and lax.ppermute only.
A program may use at most 192 MiB of HBM per device.

```python
import math
import jax
import jax.numpy as jnp
from jax import lax

FIN = 100
HID = 2048
NCLS = 47
NS = 128
BLK = 128
MB = 2
STEP = 10
NODES = 4096
PARAMS = 4499503
PTOTAL = 4501504
N_ROWS = 4
N_COLS = 8


def entry_scales():
    position = jnp.arange(PTOTAL, dtype=jnp.int32)
    offset_two = FIN * HID
    offset_three = offset_two + HID * HID
    offset_bias = offset_three + HID * NCLS
    return jnp.where(position < offset_two, FIN ** (-0.5), jnp.where(position < offset_three, HID ** (-0.5), jnp.where(position < offset_bias, (3 * NCLS) ** (-0.5), jnp.where(position < PARAMS, 0.3, 0.05)))).astype(jnp.float32)


def draw_params(key, part):
    key = jax.random.fold_in(key, 11)
    return jax.random.normal(key, (PTOTAL,), jnp.float32) * entry_scales()


def draw_first_moment(key, part):
    key = jax.random.fold_in(key, 23)
    typical = 0.01 / math.sqrt(PARAMS)
    return jax.random.normal(key, (PTOTAL,), jnp.float32) * (typical * 0.1 / 0.9)


def draw_second_moment(key, part):
    key = jax.random.fold_in(key, 37)
    typical = 0.01 / math.sqrt(PARAMS)
    factor = jax.random.uniform(key, (PTOTAL,), jnp.float32, 1.0, 4.0)
    return factor * (typical * typical * 0.05 / 0.95)


def draw_train_mask(key, part):
    key = jax.random.fold_in(key, 53)
    position = jnp.arange(NODES, dtype=jnp.int32)
    threshold = 250 + 500 * position // NODES
    random_rolls = jax.random.randint(key, (MB, NODES), 0, 1000)
    return (random_rolls < threshold[None, :]).astype(jnp.int32)


def with_ends(result, stream_key, smallest, high):
    index_at = [jax.random.randint(jax.random.fold_in(stream_key, axis), (), 0, length) for axis, length in enumerate(result.shape)]
    main_axis = result.shape.index(max(result.shape))
    beside = index_at[:main_axis] + [(index_at[main_axis] + 1) % result.shape[main_axis]] + index_at[main_axis + 1:]
    return result.at[tuple(index_at)].set(smallest).at[tuple(beside)].set(high)


def level_of(own_key, shape, cuts, smallest, largest):
    gain = 1.0
    for dim, shards_of in cuts:
        draws = jax.random.uniform(jax.random.fold_in(jax.random.fold_in(own_key, 6), dim), (shards_of,), jnp.float32, smallest / len(cuts), largest / len(cuts))
        gain = gain * jnp.repeat(jnp.exp(draws), shape[dim] // shards_of).reshape((-1,) + (1,) * (len(shape) - 1 - dim))
    return gain


def centred(own_key, shape, spread, bound, shards=(), kind=jnp.bfloat16):
    gain = level_of(own_key, shape, shards, -0.22, 0.18) if shards else 1.0
    entries = jax.random.normal(own_key, shape, jnp.float32) * spread * gain
    return jnp.minimum(jnp.maximum(entries, -bound), bound).astype(kind)


def setup_inputs(seed: int = 0) -> dict:
    key_list = jax.random.split(jax.random.key(seed), 10)
    return {
        "features": centred(key_list[0], (MB, NODES, FIN), 1.0, 6.0, ((1, 32),)),
        "adjacency": centred(key_list[1], (MB, NODES, N_ROWS, N_COLS, NS), (NODES // 2) ** -0.5, 0.125, ((1, 4), (3, 8))),
        "block_mask": with_ends((jax.random.randint(key_list[2], (MB, NODES // BLK, N_ROWS, N_COLS, NS // BLK), 0, 2) < 1).astype(jnp.int32), jax.random.fold_in(key_list[2], 1), 0, 1),
        "diagonal": jnp.clip(0.2 + 0.8 * jax.random.uniform(key_list[3], (MB, NODES), jnp.float32) ** level_of(key_list[3], (MB, NODES), ((1, 32),), -0.2, 0.2), 0.2, 1.0),
        "labels": with_ends(jax.random.randint(key_list[4], (MB, NODES), 0, NCLS), jax.random.fold_in(key_list[4], 1), 0, NCLS - 1).astype(jnp.int32),
        "train_mask": draw_train_mask(jax.random.fold_in(key_list[9], 71), 0),
        "params": draw_params(jax.random.fold_in(key_list[9], 71), 0),
        "first_moment": draw_first_moment(jax.random.fold_in(key_list[9], 71), 0),
        "second_moment": draw_second_moment(jax.random.fold_in(key_list[9], 71), 0),
    }


@jax.custom_vjp
def low(v):
    return lax.optimization_barrier(v.astype(jnp.bfloat16)).astype(jnp.float32)

@jax.custom_vjp
def low_back(v):
    return v

def low_keep(v):
    return (low(v), None)

def low_pass(kept, grad):
    return (grad,)

def back_keep(v):
    return (v, None)

def back_low(kept, grad):
    return (low(grad),)
low.defvjp(low_keep, low_pass)
low_back.defvjp(back_keep, back_low)
PRECISE = lax.Precision.HIGHEST
LAMBDA = 1.0
CLIP_NORM = 0.01
BETA_ONE = 0.9
BETA_TWO = 0.95
EPSILON = 1e-08
WEIGHT_DECAY = 0.1
LEARN_RATE = 0.02

def unpack(flat_params):
    offset_two = FIN * HID
    offset_three = offset_two + HID * HID
    offset_bias = offset_three + HID * NCLS
    w_first = flat_params[:offset_two].reshape(FIN, HID)
    w_second = flat_params[offset_two:offset_three].reshape(HID, HID)
    w_third = flat_params[offset_three:offset_bias].reshape(HID, NCLS)
    b_first = flat_params[offset_bias:offset_bias + HID]
    b_second = flat_params[offset_bias + HID:offset_bias + 2 * HID]
    b_third = flat_params[offset_bias + 2 * HID:offset_bias + 2 * HID + NCLS]
    return (w_first, w_second, w_third, b_first, b_second, b_third)

def expand_blocks(blocks):
    grown = jnp.repeat(jnp.repeat(blocks, BLK, axis=0), BLK, axis=3)
    return grown.reshape(NODES, NODES).astype(jnp.float32)

def aggregate(matrix, diag_vals, values):
    return jnp.dot(matrix, values, precision=PRECISE) + LAMBDA * diag_vals[:, None] * values

def layer_first(matrix, diag_vals, hidden, weight, bias_row):
    inputs = low(hidden)
    summed = low(low_back(aggregate(matrix, diag_vals, inputs)))
    return low_back(jnp.dot(summed, weight, precision=PRECISE)) + bias_row

def layer_last(matrix, diag_vals, hidden, weight, bias_row):
    inputs = low(hidden)
    projected = low(low_back(jnp.dot(inputs, weight, precision=PRECISE)))
    return low_back(aggregate(matrix, diag_vals, projected)) + bias_row

def reference(features, adjacency, block_mask, diagonal, labels, train_mask, params, first_moment, second_moment):
    feats = features.astype(jnp.float32)
    edges = adjacency.astype(jnp.float32)
    node_total = jnp.sum(train_mask.astype(jnp.float32))

    def objective(flat_params):
        w_first, w_second, w_third, b_first, b_second, b_third = unpack(low(flat_params))
        loss_total = jnp.float32(0.0)
        for batch_index in range(MB):
            matrix = edges[batch_index].reshape(NODES, NODES) * expand_blocks(block_mask[batch_index])
            diag_vals = diagonal[batch_index]
            hidden = jax.nn.gelu(layer_first(matrix, diag_vals, feats[batch_index], w_first, b_first))
            hidden = jax.nn.gelu(layer_first(matrix, diag_vals, hidden, w_second, b_second))
            logits = layer_last(matrix, diag_vals, hidden, w_third, b_third)
            log_total = jax.nn.logsumexp(logits, axis=1)
            label_hits = labels[batch_index][:, None] == jnp.arange(NCLS, dtype=jnp.int32)[None, :]
            picked = lax.optimization_barrier(jnp.sum(jnp.where(label_hits, logits, 0.0), axis=1))
            loss_total = loss_total + jnp.sum(train_mask[batch_index].astype(jnp.float32) * (log_total - picked))
        return (loss_total / node_total, loss_total)
    value, pullback, loss_sum = jax.vjp(objective, params, has_aux=True)
    gradient = pullback(jnp.ones_like(value))[0]
    grad_norm = jnp.sqrt(jnp.sum(gradient * gradient))
    clip_scale = jnp.minimum(1.0, CLIP_NORM / (grad_norm + 1e-06))
    clipped = gradient * clip_scale
    class_start = FIN * HID + HID * HID + HID * NCLS + 2 * HID
    class_bias_grad = clipped[class_start:class_start + NCLS]
    new_first = BETA_ONE * first_moment + (1.0 - BETA_ONE) * clipped
    new_second = BETA_TWO * second_moment + (1.0 - BETA_TWO) * clipped * clipped
    correct_one = 1.0 - BETA_ONE ** STEP
    correct_two = 1.0 - BETA_TWO ** STEP
    step_size = new_first / correct_one / (jnp.sqrt(new_second / correct_two) + EPSILON)
    new_params = params - LEARN_RATE * (step_size + WEIGHT_DECAY * params)
    return (new_params, new_first, new_second, grad_norm, loss_sum, node_total, class_bias_grad)
```

```python
import jax
import jax.numpy as jnp
from jax import lax
from jax.sharding import PartitionSpec as P

FIN = 100
HID = 2048
NCLS = 47
BLK = 128
MB = 2
STEP = 10
PARAMS = FIN * HID + HID * HID + HID * NCLS + 2 * HID + NCLS

LAMBDA = 1.0
CLIP_NORM = 0.01
BETA_ONE = 0.9
BETA_TWO = 0.95
EPSILON = 1e-08
WEIGHT_DECAY = 0.1
LEARN_RATE = 0.02

LANES = 128
UNIT = HID // LANES
BOTH = ("rows", "cols")
F32 = jnp.float32
BF16 = jnp.bfloat16


def swap(x, axis, bit):
    size = lax.axis_size(axis)
    return lax.ppermute(x, axis, [(i, i ^ bit) for i in range(size)])


def bits_of(size):
    return [1 << i for i in range(size.bit_length() - 1)]


def mm(left, right):
    return jnp.dot(left, right, preferred_element_type=F32)


def mm_t(left, right):
    return lax.dot_general(left, right, (((0,), (0,)), ((), ())), preferred_element_type=F32)


def mm_nt(left, right):
    return lax.dot_general(left, right, (((1,), (1,)), ((), ())), preferred_element_type=F32)


def take(x, axis, picks):
    return jnp.concatenate([lax.slice_in_dim(x, p, p + 1, axis=axis) for p in picks], axis)


def split_bit(x, axis, order, bit):
    keep = [j for j in order if not j & bit]
    at = {j: i for i, j in enumerate(order)}
    return (
        take(x, axis, [at[j] for j in keep]),
        take(x, axis, [at[j | bit] for j in keep]),
        keep,
    )


def gelu_back(pre_act, upstream):
    return jax.vjp(jax.nn.gelu, pre_act)[1](upstream)[0]


def total_over_all(row):
    count = lax.axis_size(BOTH)
    sent = jnp.broadcast_to(row[None, :, :], (count,) + row.shape)
    return jnp.sum(lax.all_to_all(sent, BOTH, split_axis=0, concat_axis=0, tiled=True), axis=0)


def per_device(features, adjacency, block_mask, diagonal, labels, train_mask, params, first_moment, second_moment):
    n_rows, n_cols = lax.axis_size("rows"), lax.axis_size("cols")
    n_z = n_cols // 2
    n_dev = n_rows * n_cols
    my_row, my_col = lax.axis_index("rows"), lax.axis_index("cols")
    me = my_row * n_cols + my_col
    ns = features.shape[1]
    z_bits, row_bits = bits_of(n_z), bits_of(n_rows)
    z_order = [0]
    for bit in reversed(z_bits):
        z_order = z_order + [j ^ bit for j in z_order]
    z_at = {j: i for i, j in enumerate(z_order)}

    n_own = params.shape[0] // LANES
    slot = -(-((n_own + UNIT - 2) // UNIT + 1) // 8) * 8
    shift = lax.rem(n_own * me, UNIT)
    own = lax.dynamic_update_slice(
        jnp.zeros((slot * UNIT, LANES), BF16), params.reshape(n_own, LANES).astype(BF16), (shift, 0)
    ).reshape(1, 1, slot, HID)
    for bit in reversed(z_bits):
        own = jnp.concatenate([own, swap(own, "cols", 2 * bit)], 1)
    halves = []
    for half, order_of in ((0, row_bits), (1, row_bits[1:] + row_bits[:1])):
        part = own[..., half * (HID // 2) : (half + 1) * (HID // 2)]
        order = [0]
        for bit in order_of:
            part = jnp.concatenate([part, swap(part, "rows", bit)], 0)
            order = order + [j ^ bit for j in order]
        at = {j: i for i, j in enumerate(order)}
        halves.append(take(part, 0, [at[j] for j in range(n_rows)]))
    near = jnp.concatenate(halves, -1).reshape(n_rows * n_z * slot, HID)
    far = swap(near, "cols", 1)

    def units_of(core):
        owner = (my_row ^ jnp.arange(n_rows))[:, None] * n_cols + (
            my_col ^ (2 * jnp.array(z_order) + core)
        )[None, :]
        start = (n_own * owner) // UNIT
        return (start[:, :, None] + jnp.arange(slot)[None, None, :]).reshape(-1)

    units = jnp.concatenate([units_of(0), units_of(1)])
    expand = (jnp.arange(HID)[:, None] == (units - FIN)[None, :]).astype(BF16)
    per_small = -(-(FIN + NCLS + 3) // n_dev)
    n_small = per_small * n_dev
    small_unit = jnp.arange(n_small)
    small_unit = jnp.where(small_unit < FIN, small_unit, small_unit + HID)
    n_near = near.shape[0]
    pick = (small_unit[:, None] == units[None, :]).astype(BF16)
    small = (mm(pick[:, :n_near], near) + mm(pick[:, n_near:], far)).astype(BF16)
    w_first = small[:FIN]
    w_third = small[FIN : FIN + NCLS].reshape(HID, NCLS)
    b_first, b_second, b_third = (small[FIN + NCLS + i].astype(F32) for i in range(3))
    b_third = b_third[:NCLS]

    counted = train_mask.astype(F32)
    node_total = jnp.sum(total_over_all(jnp.broadcast_to(jnp.sum(counted), (1, LANES)))[0, :1])

    tile = adjacency.reshape(MB, n_cols, ns, n_rows, ns) * block_mask.reshape(
        MB, n_cols, 1, n_rows, 1
    ).astype(BF16)
    tile = jnp.concatenate(
        [
            lax.dynamic_slice_in_dim(tile, my_col ^ (2 * j + core), 1, 1)
            for core in (0, 1)
            for j in z_order
        ],
        1,
    )
    tile = jnp.concatenate(
        [lax.dynamic_slice_in_dim(tile, my_row ^ j, 1, 3) for j in range(n_rows)], 3
    )
    tile = lax.optimization_barrier(tile.reshape(MB, n_cols * ns, n_rows * ns))
    by_z = tile.reshape(MB, 2, n_z, ns, n_rows * ns)
    strip = [by_z[:, :, 0]]
    for j in z_order[1:]:
        strip.append(swap(by_z[:, :, z_at[j]], "cols", 2 * j))
    strip = jnp.concatenate(strip, -1).reshape(MB, 2 * ns, n_z * n_rows * ns)

    def over_z(x):
        return jnp.stack([x] + [swap(x, "cols", 2 * j) for j in z_order[1:]])

    def over_rows(x):
        return [x] + [swap(x, "rows", j) for j in range(1, n_rows)]

    feats = jnp.concatenate(over_rows(features), 1)
    partial = jnp.einsum("mik,mkf->mif", tile, feats, preferred_element_type=F32)
    partial = partial.reshape(MB, 2, n_z, ns, FIN)
    partial = partial[:, 0] + swap(partial[:, 1], "cols", 1)
    g_one = partial[:, 0] + LAMBDA * diagonal[:, :, None] * features.astype(F32)
    for i, j in enumerate(z_order[1:], 1):
        g_one = g_one + swap(partial[:, i], "cols", 2 * j)
    g_one = g_one.astype(BF16)
    all_one = jnp.stack(over_rows(over_z(g_one)))
    all_one = all_one.transpose(2, 1, 0, 3, 4).reshape(MB * n_z * n_rows * ns, FIN)
    h_one = jax.nn.gelu(mm(all_one, w_first) + b_first).astype(BF16)
    h_one = h_one.reshape(MB, n_z * n_rows * ns, HID)
    g_one = g_one.reshape(MB * ns, FIN)
    z_one = mm(g_one, w_first) + b_first

    diag = diagonal.reshape(MB * ns, 1)
    partial = jnp.einsum("mik,mkf->mif", strip, h_one, preferred_element_type=F32)
    g_two = (
        partial[:, :ns]
        + swap(partial[:, ns:].astype(BF16), "cols", 1).astype(F32)
        + LAMBDA * diagonal[:, :, None] * h_one[:, :ns].astype(F32)
    )
    g_two = g_two.reshape(MB * ns, HID).astype(BF16)
    g_spread = mm(g_two, expand).astype(BF16)
    z_two = mm(g_spread[:, :n_near], near) + mm(g_spread[:, n_near:], far) + b_second
    h_two = jax.nn.gelu(z_two).astype(BF16)

    def side_by_side(x):
        return jnp.concatenate([x[:ns], x[ns:]], 1)

    q = mm(h_two, w_third).astype(BF16)
    all_q = jnp.stack(over_rows(over_z(side_by_side(q))))
    all_q = all_q.transpose(1, 0, 2, 3).reshape(n_z * n_rows * ns, MB, NCLS)
    partial = jnp.stack([mm(strip[m], all_q[:, m]) for m in range(MB)], 1)
    partial = partial.reshape(2 * ns, MB * NCLS)
    logits = partial[:ns] + swap(partial[ns:], "cols", 1)
    logits = jnp.concatenate([logits[:, :NCLS], logits[:, NCLS:]], 0)
    logits = logits + LAMBDA * diag * q.astype(F32) + b_third
    log_total = jax.nn.logsumexp(logits, axis=1)
    hits = labels.reshape(-1, 1) == jnp.arange(NCLS, dtype=jnp.int32)[None, :]
    picked = jnp.sum(jnp.where(hits, logits, 0.0), axis=1)
    counted = counted.reshape(-1)
    loss = jnp.sum(counted * (log_total - picked))
    d_logits = counted[:, None] * (jnp.exp(logits - log_total[:, None]) - hits.astype(F32)) / node_total
    d_bias_three = jnp.sum(d_logits, axis=0)
    d_s = d_logits.astype(BF16)

    pair = side_by_side(d_s)
    all_s = jnp.concatenate([over_z(pair), over_z(swap(pair, "cols", 1))], 0)
    all_s = all_s.reshape(n_cols * ns, MB, NCLS)
    partial = jnp.stack([mm_t(tile[m], all_s[:, m]) for m in range(MB)], 1)
    partial = partial.reshape(n_rows, ns, MB * NCLS)
    d_q = partial[0]
    for j in range(1, n_rows):
        d_q = d_q + swap(partial[j], "rows", j)
    d_q = jnp.concatenate([d_q[:, :NCLS], d_q[:, NCLS:]], 0)
    d_q = (d_q + LAMBDA * diag * d_s.astype(F32)).astype(BF16)
    d_w_three = mm_t(h_two, d_q)
    d_z = gelu_back(z_two, mm_nt(d_q, w_third))
    d_bias_two = jnp.sum(d_z, axis=0)
    d_zb = d_z.astype(BF16)

    d_g = jnp.concatenate([mm_nt(d_zb, near), mm_nt(d_zb, far)], 1).astype(BF16)
    d_g = mm_nt(d_g, expand).astype(BF16)

    d_w_one, d_bias_one = [], []
    n_cut = 2
    wide = HID // n_cut
    for cut in range(n_cut):
        d_w_cut = 0.0
        d_bias_cut = 0.0
        for m in range(MB):
            up = d_g[m * ns : (m + 1) * ns, cut * wide : (cut + 1) * wide]
            got = up[None]
            for bit in reversed(z_bits):
                got = jnp.concatenate([got, swap(got, "cols", 2 * bit)], 0)
            got = jnp.concatenate([got, swap(got, "cols", 1)], 0).reshape(n_cols * ns, wide)
            partial = mm_t(tile[m], got).reshape(n_rows, ns, wide)
            low = partial.astype(BF16)
            d_h = partial[0] + LAMBDA * diagonal[m][:, None] * up.astype(F32)
            for j in range(1, n_rows):
                d_h = d_h + swap(low[j], "rows", j).astype(F32)
            d_one = gelu_back(z_one[m * ns : (m + 1) * ns, cut * wide : (cut + 1) * wide], d_h)
            d_bias_cut = d_bias_cut + jnp.sum(d_one, axis=0)
            d_w_cut = d_w_cut + mm_t(g_one[m * ns : (m + 1) * ns], d_one.astype(BF16))
        d_w_one.append(d_w_cut)
        d_bias_one.append(d_bias_cut)
    d_w_one = jnp.concatenate(d_w_one, 1)
    d_bias_one = jnp.concatenate(d_bias_one)

    d_w = mm_t(g_spread, d_zb).reshape(2, n_rows, n_z, slot, HID)
    d_w = d_w[0] + swap(d_w[1].astype(BF16), "cols", 1).astype(F32)
    halves = []
    for half, order_of in ((0, row_bits), (1, row_bits[1:] + row_bits[:1])):
        part = d_w[..., half * (HID // 2) : (half + 1) * (HID // 2)]
        order = list(range(n_rows))
        for bit in order_of:
            kept, sent, order = split_bit(part, 0, order, bit)
            part = kept + swap(sent.astype(BF16), "rows", bit).astype(F32)
        halves.append(part[0])
    part = jnp.concatenate(halves, -1)
    order = z_order
    for bit in z_bits:
        kept, sent, order = split_bit(part, 0, order, bit)
        part = kept + swap(sent.astype(BF16), "cols", 2 * bit).astype(F32)
    own_grad = part[0]

    pad_bias = jnp.pad(d_bias_three, (0, HID - NCLS))
    d_small = jnp.concatenate(
        [
            d_w_one,
            d_w_three.reshape(NCLS, HID),
            d_bias_one[None],
            d_bias_two[None],
            pad_bias[None],
            jnp.zeros((n_small - FIN - NCLS - 3, HID), F32),
        ],
        0,
    ).astype(BF16)
    d_small = d_small.reshape(n_dev, per_small * UNIT, LANES)
    got = lax.all_to_all(d_small, BOTH, split_axis=0, concat_axis=0, tiled=True)
    got = jnp.sum(got.astype(F32), axis=0)
    low = got.astype(BF16)
    sent = jnp.broadcast_to(low[None], d_small.shape)
    d_small = lax.all_to_all(sent, BOTH, split_axis=0, concat_axis=0, tiled=True)
    d_small = d_small.reshape(n_small, HID)

    own_flat = lax.dynamic_slice(own_grad.reshape(slot * UNIT, LANES), (shift, 0), (n_own, LANES))
    squares = jnp.sum(own_flat * own_flat) + jnp.sum(low.astype(F32) ** 2)
    row = jnp.concatenate([squares[None], loss[None], d_bias_three, jnp.zeros((LANES - NCLS - 2,), F32)])
    row = total_over_all(row[None])[0]
    squares, loss_sum, class_sum = row[0], row[1], row[2 : 2 + NCLS]

    mine = (n_own * me) // UNIT + jnp.arange(slot)
    place = (mine[:, None] == small_unit[None, :]).astype(BF16)
    small_flat = lax.dynamic_slice(
        mm(place, d_small).reshape(slot * UNIT, LANES), (shift, 0), (n_own, LANES)
    )
    reduced = (own_flat + small_flat).reshape(-1)

    grad_norm = jnp.sqrt(squares)
    clip_scale = jnp.minimum(1.0, CLIP_NORM / (grad_norm + 1e-06))
    clipped = reduced * clip_scale
    class_bias_grad = class_sum * clip_scale
    new_first = BETA_ONE * first_moment + (1.0 - BETA_ONE) * clipped
    new_second = BETA_TWO * second_moment + (1.0 - BETA_TWO) * clipped * clipped
    correct_one = 1.0 - BETA_ONE**STEP
    correct_two = 1.0 - BETA_TWO**STEP
    step_size = new_first / correct_one / (jnp.sqrt(new_second / correct_two) + EPSILON)
    new_params = params - LEARN_RATE * (step_size + WEIGHT_DECAY * params)
    return (new_params, new_first, new_second, grad_norm, loss_sum, node_total, class_bias_grad)


def solution(mesh):
    in_specs = (
        P(None, ("rows", "cols"), None),
        P(None, "rows", None, "cols", None),
        P(None, "rows", None, "cols", None),
        P(None, ("rows", "cols")),
        P(None, ("rows", "cols")),
        P(None, ("rows", "cols")),
        P(("rows", "cols")),
        P(("rows", "cols")),
        P(("rows", "cols")),
    )
    out_specs = (P(("rows", "cols")), P(("rows", "cols")), P(("rows", "cols")), P(), P(), P(), P())
    return jax.shard_map(
        per_device, mesh=mesh, in_specs=in_specs, out_specs=out_specs, check_vma=False
    )
```

```python
import jax
import jax.numpy as jnp
from jax import lax
from jax.experimental import pallas as pl
from jax.experimental.pallas import tpu as pltpu
from jax.sharding import PartitionSpec as P

FIN = 100
HID = 2048
NCLS = 47
BLK = 128
MB = 2
STEP = 10
PARAMS = FIN * HID + HID * HID + HID * NCLS + 2 * HID + NCLS

LAMBDA = 1.0
CLIP_NORM = 0.01
BETA_ONE = 0.9
BETA_TWO = 0.95
EPSILON = 1e-08
WEIGHT_DECAY = 0.1
LEARN_RATE = 0.02

LANES = 128
UNIT = HID // LANES
BOTH = ("rows", "cols")
GELU_ONE = 0.7978845608028654
GELU_THREE = GELU_ONE * 0.044715
F32 = jnp.float32
FAR_BYTES = 1 << 17
BF16 = jnp.bfloat16


def swap(x, axis, bit):
    size = lax.axis_size(axis)
    return lax.ppermute(x, axis, [(i, i ^ bit) for i in range(size)])


def bits_of(size):
    return [1 << i for i in range(size.bit_length() - 1)]


def mm(left, right):
    return jnp.dot(left, right, preferred_element_type=F32)


def mm_t(left, right):
    return lax.dot_general(left, right, (((0,), (0,)), ((), ())), preferred_element_type=F32)


def mm_nt(left, right):
    return lax.dot_general(left, right, (((1,), (1,)), ((), ())), preferred_element_type=F32)


def take(x, axis, picks):
    return jnp.concatenate([lax.slice_in_dim(x, p, p + 1, axis=axis) for p in picks], axis)


def split_bit(x, axis, order, bit):
    keep = [j for j in order if not j & bit]
    run = next(i for i, j in enumerate(order) if j & bit)
    if any(bool(j & bit) != bool(i // run % 2) or j & ~bit != order[i - i // run % 2 * run] & ~bit for i, j in enumerate(order)):
        at = {j: i for i, j in enumerate(order)}
        return take(x, axis, [at[j] for j in keep]), take(x, axis, [at[j | bit] for j in keep]), keep
    shape = x.shape[:axis] + (len(order) // (2 * run), 2, run) + x.shape[axis + 1 :]
    kept_shape = x.shape[:axis] + (len(keep),) + x.shape[axis + 1 :]
    x = x.reshape(shape)
    pair = [lax.index_in_dim(x, i, axis + 1, keepdims=False).reshape(kept_shape) for i in (0, 1)]
    return pair[0], pair[1], keep


def total_over_all(row):
    count = lax.axis_size(BOTH)
    sent = jnp.broadcast_to(row[None, :, :], (count,) + row.shape)
    return jnp.sum(lax.all_to_all(sent, BOTH, split_axis=0, concat_axis=0, tiled=True), axis=0)


ANYWHERE = pl.BlockSpec(memory_space=pl.ANY)
IN_VMEM = pl.BlockSpec(memory_space=pltpu.VMEM)
IN_SMEM = pl.BlockSpec(memory_space=pltpu.SMEM)


def tip(x):
    while x.ndim > 2:
        x = x[0]
    return x[:8, :128].astype(F32)


def after_kernel(*refs):
    pass


def after(x, *earlier):
    earlier = [tip(e) for e in earlier]
    return pl.pallas_call(
        after_kernel,
        out_shape=jax.ShapeDtypeStruct(x.shape, x.dtype),
        in_specs=[ANYWHERE] * (1 + len(earlier)),
        out_specs=ANYWHERE,
        input_output_aliases={0: 0},
        name="after",
    )(x, *earlier)


def padded_bytes(shape, dtype):
    *front, rows, lanes = (1, 1, *shape)
    size = -(-rows // 16) * 16 * -(-lanes // LANES) * LANES * jnp.dtype(dtype).itemsize
    for n in front:
        size *= n
    return size


def call(kernel, name, out_shape, in_specs, out_specs, grid=None, room=4, scratch=()):
    more = {} if grid is None else {"grid": grid}

    def run(*args):
        outs = out_shape if isinstance(out_shape, tuple) else (out_shape,)
        specs = (*in_specs, *(out_specs if isinstance(out_specs, tuple) else (out_specs,)))
        total = room << 20
        for spec, x in zip(specs, (*args, *outs)):
            if spec.block_shape is not None:
                total += 2 * padded_bytes(spec.block_shape, x.dtype)
            elif spec.memory_space == pltpu.VMEM:
                total += padded_bytes(x.shape, x.dtype)
        args = [
            pltpu.with_memory_space_constraint(x, pltpu.HBM) if x.size * x.dtype.itemsize >= FAR_BYTES else x
            for x in args
        ]
        return pl.pallas_call(
            kernel,
            out_shape=out_shape,
            in_specs=in_specs,
            out_specs=out_specs,
            scratch_shapes=list(scratch),
            compiler_params=pltpu.CompilerParams(vmem_limit_bytes=total),
            cost_estimate=pl.CostEstimate(flops=0, bytes_accessed=0, transcendentals=0),
            name=name,
            **more,
        )(*args)

    return run


def shaped(shape, dtype=F32):
    return jax.ShapeDtypeStruct(shape, dtype)


def lane_of(shape):
    return lax.broadcasted_iota(jnp.int32, shape, len(shape) - 1)


def masked_tile_kernel(row_order, n_across, n_pieces, where_ref, mask_ref, tile_ref, *refs):
    out_refs, wide_ref = refs[:-1], refs[-1]
    col, row = where_ref[0], where_ref[1]
    tall = BLK * n_across
    per_piece = len(row_order) // n_pieces
    for m in range(MB):
        for i, j in enumerate(row_order):
            block = col ^ j
            wide_ref[...] = tile_ref[m, pl.ds(pl.multiple_of(block * tall, tall), tall), :].astype(F32)
            piece, low = i // per_piece, i % per_piece * BLK
            for k in range(n_across):
                keep = mask_ref[(m * len(row_order) + block) * n_across + k].astype(F32)
                part = (wide_ref[pl.ds(k, BLK, n_across), :] * keep).astype(BF16)
                lanes = pl.ds(pl.multiple_of((row ^ k) * BLK, BLK), BLK)
                out_refs[m * n_pieces + piece][low : low + BLK, lanes] = part
                if piece:
                    at = MB * n_pieces + m * (n_pieces - 1) + piece - 1
                    out_refs[at][low : low + BLK, lanes] = part


def masked_tile(adjacency, block_mask, row_order, my_col, my_row):
    n_across = adjacency.shape[2]
    n_pieces = len(row_order) // 2
    piece = pltpu.HBM((2 * BLK, n_across * BLK), BF16)
    n_out = MB * (2 * n_pieces - 1)
    out = call(
        lambda *refs: masked_tile_kernel(row_order, n_across, n_pieces, *refs),
        "masked_tile",
        (piece,) * n_out,
        [IN_SMEM, IN_SMEM, pl.BlockSpec((MB, adjacency.shape[1] * n_across, LANES), lambda i: (0, 0, 0))],
        (pl.BlockSpec((2 * BLK, n_across * BLK), lambda i: (0, 0)),) * n_out,
        grid=(1,),
        room=4,
        scratch=[pltpu.VMEM((n_across * BLK, LANES), F32)],
    )(
        jnp.stack([my_col, my_row]).astype(jnp.int32),
        block_mask.reshape(-1),
        adjacency.reshape(MB, -1, LANES),
    )
    tile = [out[m * n_pieces : (m + 1) * n_pieces] for m in range(MB)]
    leave = out[MB * n_pieces :]
    return tile, [leave[m * (n_pieces - 1) : (m + 1) * (n_pieces - 1)] for m in range(MB)]


def layer_one_kernel(n_z, *refs):
    tile_refs, feat_refs, (near_ref, far_ref) = refs[: MB * n_z], refs[MB * n_z : -2], refs[-2:]
    ns = near_ref.shape[2]
    for m in range(MB):
        feats = jnp.concatenate([f[m] for f in feat_refs], 0)
        for i in range(n_z):
            out = mm(tile_refs[m * n_z + i][...], feats)
            near_ref[i, m] = out[:ns]
            far_ref[i, m] = out[ns:]


def layer_one(tile, feats):
    n_z = len(tile[0])
    half, across = tile[0][0].shape
    out = shaped((n_z, MB, half // 2, LANES))
    return call(
        lambda *refs: layer_one_kernel(n_z, *refs),
        "layer_one",
        (out, out),
        [pl.BlockSpec((half, across), lambda i: (0, 0))] * (MB * n_z) + [IN_VMEM] * len(feats),
        (IN_VMEM, IN_VMEM),
        grid=(1,),
    )(*tile[0], *tile[1], *feats)


def twice_gelu(z):
    return z + z * jnp.tanh(z * (GELU_ONE + GELU_THREE * (z * z)))


def twice_gelu_slope(z):
    square = z * z
    inner = z * (GELU_ONE + GELU_THREE * square)
    t = jnp.tanh(inner)
    slope = z * (GELU_ONE + (3 * GELU_THREE) * square)
    return (1.0 + t) * (1.0 + (1.0 - t) * slope)


def forward_kernel(n_z, n_rows, m, *refs):
    g_refs, strip_refs = refs[:n_rows], refs[n_rows : n_rows + n_z]
    w_ref, near_ref, far_ref = refs[n_rows + n_z :]
    half = near_ref.shape[0]
    total = None
    for i in range(n_z):
        g = jnp.concatenate([g_ref[i, m] for g_ref in g_refs], 0)
        h = twice_gelu(mm(g, w_ref[...])).astype(BF16)
        part = mm(strip_refs[i][...], h)
        total = part if total is None else total + part
    near_ref[...] = 0.5 * total[:half]
    far_ref[...] = (0.5 * total[half:]).astype(BF16)


def forward_two(g_all, w_wide, strip, m, wide=256):
    n_rows, n_z = len(g_all), len(strip)
    rows, across = strip[0].shape
    span = w_wide.shape[1]
    return call(
        lambda *refs: forward_kernel(n_z, n_rows, m, *refs),
        "forward_two",
        (shaped((rows // 2, span)), shaped((rows // 2, span), BF16)),
        [pl.BlockSpec(g_all[0].shape, lambda f: (0, 0, 0, 0))] * n_rows
        + [pl.BlockSpec((rows, across), lambda f: (0, 0))] * n_z
        + [pl.BlockSpec((LANES, wide), lambda f: (0, f))],
        (pl.BlockSpec((rows // 2, wide), lambda f: (0, f)),) * 2,
        grid=(span // wide,),
        room=2 + 8 * across // 1024,
    )(*g_all, *strip, w_wide)


def layer_two_kernel(n_m, *refs):
    near_parts, far_parts = refs[:n_m], refs[n_m : 2 * n_m]
    g_one_ref, w_wide_ref, diag_ref, wn_ref, wf_ref, b_ref, w3_ref, here_ref = refs[2 * n_m : -6]
    gn_ref, gf_ref, z_ref, h_ref, q_ref, sum_ref = refs[-6:]
    ns = near_parts[0].shape[0]
    n_near = wn_ref.shape[0]

    @pl.when(pl.program_id(0) == 0)
    def _():
        step = 384 if n_near % 384 == 0 else LANES
        for at in range(0, 2 * n_near, step):
            cut = slice(at, at + step)
            turned = slice((at + n_near) % (2 * n_near), (at + n_near) % (2 * n_near) + step)
            g_ref, base = (gn_ref, at) if at < n_near else (gf_ref, at - n_near)
            h = (0.5 * twice_gelu(mm(g_one_ref[...], w_wide_ref[:, cut]))).astype(BF16)
            for m in range(n_m):
                g_ref[m * ns : (m + 1) * ns, base : base + step] = (
                    near_parts[m][:, cut]
                    + far_parts[m][:, turned].astype(F32)
                    + LAMBDA * diag_ref[:, m : m + 1] * h[m * ns : (m + 1) * ns].astype(F32)
                ).astype(BF16)
        sum_ref[...] = jnp.zeros_like(sum_ref)

    z = mm(gn_ref[...], wn_ref[...]) + mm(gf_ref[...], wf_ref[...]) + b_ref[...]
    z_ref[...] = z
    h = (0.5 * twice_gelu(z)).astype(BF16)
    h_ref[...] = h
    q = mm(h, w3_ref[...])
    lane = lane_of(sum_ref.shape)
    sum_ref[...] += jnp.where(lane < LANES // 2, q[:ns], q[ns:])

    @pl.when(pl.program_id(0) == pl.num_programs(0) - 1)
    def _():
        q_ref[...] = jnp.where(lane == LANES - 1, here_ref[...], sum_ref[...]).astype(BF16)


def layer_two(near_parts, far_parts, g_one, w_wide, diag, near, far, b_second, w3, here, wide=512):
    ns, span = near_parts[0].shape
    n_m = len(near_parts)
    n_near = near.shape[0]
    whole = lambda f: (0, 0)
    part = pl.BlockSpec((ns, span), whole)
    rows = n_m * ns
    return call(
        lambda *refs: layer_two_kernel(n_m, *refs),
        "layer_two",
        (
            shaped((rows, n_near), BF16),
            shaped((rows, n_near), BF16),
            shaped((rows, HID)),
            shaped((rows, HID), BF16),
            shaped((ns, LANES), BF16),
        ),
        [part] * (2 * n_m)
        + [
            pl.BlockSpec((rows, LANES), whole),
            pl.BlockSpec((LANES, span), whole),
            pl.BlockSpec((ns, n_m), whole),
            pl.BlockSpec((n_near, wide), lambda f: (0, f)),
            pl.BlockSpec((n_near, wide), lambda f: (0, f)),
            pl.BlockSpec((1, wide), lambda f: (0, f)),
            pl.BlockSpec((wide, LANES), lambda f: (f, 0)),
            pl.BlockSpec((1, LANES), whole),
        ],
        (
            pl.BlockSpec((rows, n_near), whole),
            pl.BlockSpec((rows, n_near), whole),
            pl.BlockSpec((rows, wide), lambda f: (0, f)),
            pl.BlockSpec((rows, wide), lambda f: (0, f)),
            pl.BlockSpec((ns, LANES), whole),
        ),
        grid=(HID // wide,),
        scratch=[pltpu.VMEM((ns, LANES), F32)],
        room=4,
    )(*near_parts, *far_parts, g_one, w_wide, diag, near, far, b_second, w3, here)


def logits_kernel(n_z, *refs):
    strips, q_refs, (near_ref, far_ref) = refs[: MB * n_z], refs[MB * n_z : -2], refs[-2:]
    half = near_ref.shape[0]
    lane = lane_of((2 * half, LANES))
    sums = [None] * MB
    for i in range(n_z):
        all_q = jnp.concatenate([q[i] for q in q_refs], 0)
        for m in range(MB):
            part = mm(strips[m * n_z + i][...], all_q)
            sums[m] = part if sums[m] is None else sums[m] + part
    out = jnp.where(lane < LANES // 2, sums[0], sums[1])
    count = sum(jnp.sum(q[:, 0:1, :].astype(F32), axis=0) for q in q_refs)
    out = jnp.where(lane == LANES - 1, count, out)
    near_ref[...] = out[:half]
    far_ref[...] = out[half:]


def logits_parts(strips, q_rows):
    n_z = len(strips[0])
    rows, across = strips[0][0].shape
    out = shaped((rows // 2, LANES))
    return call(
        lambda *refs: logits_kernel(n_z, *refs),
        "logits_parts",
        (out, out),
        [pl.BlockSpec((rows, across), lambda i: (0, 0))] * (MB * n_z) + [IN_VMEM] * len(q_rows),
        (IN_VMEM, IN_VMEM),
        grid=(1,),
    )(*strips[0], *strips[1], *q_rows)


def loss_kernel(near_ref, got_ref, q_ref, diag_ref, bias_ref, labels_ref, counted_ref, ds_ref, row_ref):
    total = near_ref[...] + got_ref[...]
    node_total = total[0:1, LANES - 1 :]
    lane = lane_of(total.shape)
    low = lane < LANES // 2
    at = jnp.where(low, lane, lane - LANES // 2)
    real = at < NCLS
    pick = lambda ref: jnp.where(low, ref[:, 0:1], ref[:, 1:2])
    logits = total + LAMBDA * pick(diag_ref) * q_ref[...].astype(F32) + bias_ref[...]
    least = jnp.float32(-3.0e38)
    hits = jnp.logical_and(real, at == pick(labels_ref))
    counted = pick(counted_ref)
    parts = []
    for side in (jnp.logical_and(real, low), jnp.logical_and(real, jnp.logical_not(low))):
        top = jnp.max(jnp.where(side, logits, least), axis=1, keepdims=True)
        powers = jnp.where(side, jnp.exp(jnp.where(side, logits - top, 0.0)), 0.0)
        parts.append((top, jnp.sum(powers, axis=1, keepdims=True)))
    log_total = jnp.where(
        low, parts[0][0] + jnp.log(parts[0][1]), parts[1][0] + jnp.log(parts[1][1])
    )
    loss = jnp.where(hits, counted * (log_total - logits), 0.0)
    soft = jnp.exp(jnp.where(real, logits - log_total, 0.0))
    d_logits = jnp.where(real, counted * (soft - hits.astype(F32)) / node_total, 0.0)
    ds_ref[...] = d_logits.astype(BF16)
    row_ref[0:1] = jnp.sum(d_logits, axis=0, keepdims=True)
    row_ref[1:2] = jnp.broadcast_to(jnp.sum(jnp.sum(loss, axis=0, keepdims=True), axis=1, keepdims=True), (1, LANES))
    row_ref[2:3] = jnp.broadcast_to(node_total, (1, LANES))
    row_ref[3:8] = jnp.zeros((5, LANES), F32)


def d_q_kernel(n_z, *refs):
    tile_refs, s_refs, out_refs = refs[: MB * n_z], refs[MB * n_z : (MB + 1) * n_z], refs[(MB + 1) * n_z :]
    side = out_refs[0].shape[0]
    lane = lane_of((side * len(out_refs), LANES))
    sums = [None] * MB
    for i in range(n_z):
        all_s = jnp.concatenate([s_refs[i][core] for core in (0, 1)], 0)
        for m in range(MB):
            part = mm_t(tile_refs[m * n_z + i][...], all_s)
            sums[m] = part if sums[m] is None else sums[m] + part
    out = jnp.where(lane < LANES // 2, sums[0], sums[1])
    for k, out_ref in enumerate(out_refs):
        out_ref[...] = out[k * side : (k + 1) * side]


def d_q_parts(tile, pieces):
    n_z = len(pieces)
    rows, across = tile[0][0].shape
    n = across // BLK
    return call(
        lambda *refs: d_q_kernel(n_z, *refs),
        "d_q_parts",
        (shaped((BLK, LANES)),) * n,
        [pl.BlockSpec((rows, across), lambda i: (0, 0))] * (MB * n_z) + [IN_VMEM] * n_z,
        (IN_VMEM,) * n,
        grid=(1,),
    )(*tile[0], *tile[1], *pieces)


def d_two_kernel(n_q, *refs):
    q_refs = refs[:n_q]
    ds_ref, diag_ref, z_ref, h_ref, w3_ref, gn_ref, gf_ref, dz_ref, db_ref, dw3_ref, near_ref, far_ref = refs[n_q:]
    ns = ds_ref.shape[0]
    d_q = q_refs[0][...]
    for q in q_refs[1:]:
        d_q = d_q + q[...]
    low = lane_of(d_q.shape) < LANES // 2
    d_q = d_q + LAMBDA * jnp.where(low, diag_ref[:, 0:1], diag_ref[:, 1:2]) * ds_ref[...].astype(F32)
    d_q = jnp.concatenate([jnp.where(low, d_q, 0.0), jnp.where(low, 0.0, d_q)], 0).astype(BF16)
    d_z = mm_nt(d_q, w3_ref[...]) * (0.5 * twice_gelu_slope(z_ref[...]))
    db_ref[...] = jnp.sum(d_z.reshape(-1, 8, d_z.shape[1]), axis=0)
    d_zb = d_z.astype(BF16)
    dz_ref[...] = d_zb
    dw3_ref[...] = mm_t(h_ref[...], d_q)
    far_ref[...] = mm_t(gf_ref[...], d_zb).astype(BF16)
    near_ref[...] = mm_t(gn_ref[...], d_zb)


def d_two(d_q, d_s, diag, z_two, h_two, w3, g_near, g_far, lo, hi, wide=256):
    rows = z_two.shape[0]
    ns, n_far = d_s.shape[0], g_far.shape[1]
    whole = lambda f: (0, 0)
    start = lo // wide
    small = pl.BlockSpec((ns, LANES), whole)
    column = pl.BlockSpec((rows, wide), lambda f: (0, start + f))
    span = hi - lo
    return call(
        lambda *refs: d_two_kernel(len(d_q), *refs),
        "d_two",
        (
            shaped((rows, span), BF16),
            shaped((8, span)),
            shaped((span, LANES)),
            shaped((n_far, span)),
            shaped((n_far, span), BF16),
        ),
        [small] * (len(d_q) + 1)
        + [
            pl.BlockSpec((ns, MB), whole),
            column,
            column,
            pl.BlockSpec((wide, LANES), lambda f: (start + f, 0)),
            pl.BlockSpec((rows, n_far), whole),
            pl.BlockSpec((rows, n_far), whole),
        ],
        (
            pl.BlockSpec((rows, wide), lambda f: (0, f)),
            pl.BlockSpec((8, wide), lambda f: (0, f)),
            pl.BlockSpec((wide, LANES), lambda f: (f, 0)),
            pl.BlockSpec((n_far, wide), lambda f: (0, f)),
            pl.BlockSpec((n_far, wide), lambda f: (0, f)),
        ),
        grid=(span // wide,),
        room=4,
    )(*d_q, d_s, diag, z_two, h_two, w3, g_near, g_far)


def backward_kernel(n_z, n_rows, *refs):
    g_refs, strip_refs = refs[:n_rows], refs[n_rows : n_rows + MB * n_z]
    w_ref, dgn_ref, dgf_ref, diag_ref, dw_ref = refs[n_rows + MB * n_z :]
    own = dgn_ref.shape[1]
    total = None
    for m in range(MB):
        d_g = jnp.concatenate([dgn_ref[m], dgf_ref[m]], 0)
        for i in range(n_z):
            d_h = mm_t(strip_refs[m * n_z + i][...], d_g)
            if i == 0:
                more = LAMBDA * diag_ref[:, m : m + 1] * dgn_ref[m].astype(F32)
                d_h = jnp.concatenate([d_h[:own] + more, d_h[own:]], 0)
            g = jnp.concatenate([g_ref[i, m] for g_ref in g_refs], 0)
            d_z = d_h * twice_gelu_slope(mm(g, w_ref[...]))
            part = mm_t(g, d_z.astype(BF16))
            total = part if total is None else total + part
    dw_ref[...] = (0.5 * total).astype(BF16)


def backward_one(g_all, w_wide, strips, d_g_near, d_g_far, diag, lo, hi, wide=256):
    n_rows, n_z = len(g_all), len(strips[0])
    rows, across = strips[0][0].shape
    span = hi - lo
    start = lo // wide
    column = pl.BlockSpec((MB, rows // 2, wide), lambda f: (0, 0, start + f))
    return call(
        lambda *refs: backward_kernel(n_z, n_rows, *refs),
        "backward_one",
        shaped((LANES, span), BF16),
        [pl.BlockSpec(g_all[0].shape, lambda f: (0, 0, 0, 0))] * n_rows
        + [pl.BlockSpec((rows, across), lambda f: (0, 0))] * (MB * n_z)
        + [
            pl.BlockSpec((LANES, wide), lambda f: (0, start + f)),
            column,
            column,
            pl.BlockSpec((rows // 2, MB), lambda f: (0, 0)),
        ],
        pl.BlockSpec((LANES, wide), lambda f: (0, f)),
        grid=(span // wide,),
        room=2 + 12 * across // 1024,
    )(*g_all, *strips[0], *strips[1], w_wide, d_g_near, d_g_far, diag)


def d_g_kernel(n_blocks, cuts, *refs):
    dz_refs, (wn_ref, wf_ref, out_ref, turned_ref) = refs[: len(cuts)], refs[len(cuts) :]
    near = pl.program_id(0) < n_blocks

    def product(w_ref):
        return sum(mm_nt(dz[...], w_ref[:, lo:hi]) for dz, (lo, hi) in zip(dz_refs, cuts)).astype(BF16)

    @pl.when(near)
    def _():
        out_ref[...] = product(wn_ref)

    @pl.when(jnp.logical_not(near))
    def _():
        out_ref[...] = product(wf_ref)

    turned_ref[...] = out_ref[...]


def d_g_wide(d_zb, cuts, near, far):
    rows, n_near = d_zb[0].shape[0], near.shape[0]
    wide = 384 if n_near % 384 == 0 else LANES
    n = n_near // wide
    out = shaped((rows, 2 * n_near), BF16)
    return call(
        lambda *refs: d_g_kernel(n, cuts, *refs),
        "d_g_wide",
        (out, out),
        [IN_VMEM] * len(cuts)
        + [
            pl.BlockSpec((wide, HID), lambda k: (jnp.minimum(k, n - 1), 0)),
            pl.BlockSpec((wide, HID), lambda k: (jnp.maximum(k - n, 0), 0)),
        ],
        (
            pl.BlockSpec((rows, wide), lambda k: (0, k)),
            pl.BlockSpec((rows, wide), lambda k: (0, lax.rem(k + n, 2 * n))),
        ),
        grid=(2 * n,),
        room=4,
    )(*d_zb, near, far)


def join_kernel(sizes, *refs):
    pieces, out_ref, sems = refs[: len(sizes)], refs[len(sizes)], refs[-1]
    at, copies = 0, []
    for i, (piece, size) in enumerate(zip(pieces, sizes)):
        copies.append(pltpu.make_async_copy(piece, out_ref.at[pl.ds(at, size)], sems.at[i]))
        copies[-1].start()
        at += size
    for copy in copies:
        copy.wait()


def join(pieces):
    sizes = [p.shape[0] for p in pieces]
    return call(
        lambda *refs: join_kernel(sizes, *refs),
        "join",
        shaped((sum(sizes),) + pieces[0].shape[1:], pieces[0].dtype),
        [ANYWHERE] * len(pieces),
        IN_VMEM,
        room=2,
        scratch=[pltpu.SemaphoreType.DMA((len(pieces),))],
    )(*pieces)


def per_device(features, adjacency, block_mask, diagonal, labels, train_mask, params, first_moment, second_moment):
    n_rows, n_cols = lax.axis_size("rows"), lax.axis_size("cols")
    n_z = n_cols // 2
    n_dev = n_rows * n_cols
    my_row, my_col = lax.axis_index("rows"), lax.axis_index("cols")
    me = my_row * n_cols + my_col
    ns = features.shape[1]
    z_bits, row_bits = bits_of(n_z), bits_of(n_rows)
    turned = row_bits[1:] + row_bits[:1]
    single = z_bits[::-1]
    several = [j for j in range(1, n_z) if j not in single]
    z_order = [0] + single + several

    def over_z(x):
        return [x] + [swap(x, "cols", 2 * j) for j in z_order[1:]]

    def over_rows(x):
        return [x] + [swap(x, "rows", j) for j in range(1, n_rows)]

    n_own = params.shape[0] // LANES
    slot = -(-((n_own + UNIT - 2) // UNIT + 1) // 8) * 8
    shift = lax.rem(n_own * me, UNIT)
    own = lax.dynamic_update_slice(
        jnp.zeros((slot * UNIT, LANES), BF16), params.reshape(n_own, LANES).astype(BF16), (shift, 0)
    ).reshape(1, slot, HID)
    wide_feats = jnp.pad(features, ((0, 0), (0, 0), (0, LANES - FIN)))
    ones = lax.broadcasted_iota(jnp.int32, (1, 1, LANES), 2) == FIN
    feats = over_rows(wide_feats)
    tile, leave = masked_tile(
        adjacency.reshape(MB, -1, n_rows, LANES), block_mask, [2 * j + core for j in z_order for core in (0, 1)], my_col, my_row
    )

    part_near, part_far = layer_one(tile, feats)
    own = after(own, part_far)
    by_z = {0: own}
    for j in single:
        by_z[j] = swap(own, "cols", 2 * j)
    partial = part_near + swap(part_far, "cols", 1)
    g_one = partial[0] + LAMBDA * diagonal[:, :, None] * wide_feats.astype(F32)
    low = partial.astype(BF16)
    for i, j in enumerate(z_order[1:], 1):
        g_one = g_one + swap(low[i], "cols", 2 * j).astype(F32)
    g_one = jnp.where(ones, 1.0, g_one).astype(BF16)

    middle = after(join([by_z[j] for j in single]), g_one)
    for j in several:
        bit = j & -j
        by_z[j] = swap(by_z[j - bit], "cols", 2 * bit)
    last = by_z[several[0]] if len(several) == 1 else join([by_z[j] for j in several])
    g_z = over_z(g_one)
    last = after(last, *g_z[1:])
    groups = [own, middle, last]
    g_all = over_rows(jnp.stack(g_z))
    passed = {0: groups}
    for j in range(1, n_rows):
        lowest = j & -j
        highest = 1 << (j.bit_length() - 1)
        hop = [passed[j - bit][i] for i, bit in enumerate((highest, lowest, highest))]
        if lowest != highest:
            hop = [after(h, *g_all[1:]) for h in hop]
        passed[j] = [swap(h, "rows", bit) for h, bit in zip(hop, (highest, lowest, highest))]
    strips = [[tile[m][0]] for m in range(MB)]
    for i, j in enumerate(z_order[1:]):
        strips[0].append(swap(after(leave[0][i], last), "cols", 2 * j))
    passed[0][0] = after(passed[0][0], *strips[0][1:])
    near = join([g.reshape(-1, HID) for j in range(n_rows) for g in passed[j]])
    far = swap(near, "cols", 1)
    n_near = near.shape[0]

    def units_of(core):
        owner = (my_row ^ jnp.arange(n_rows))[:, None] * n_cols + (
            my_col ^ (2 * jnp.array(z_order) + core)
        )[None, :]
        start = (n_own * owner) // UNIT
        return (start[:, :, None] + jnp.arange(slot)[None, None, :]).reshape(-1)

    near_units = units_of(0)
    units = jnp.concatenate([near_units, units_of(1)])
    expand = lax.optimization_barrier((jnp.arange(HID)[:, None] == (units - FIN)[None, :]).astype(BF16))

    per_small = -(-(FIN + NCLS + 3) // n_dev)
    n_small = per_small * n_dev
    small_unit = jnp.arange(n_small)
    small_unit = jnp.where(small_unit < FIN, small_unit, small_unit + HID)
    pick = (small_unit[:, None] == near_units[None, :]).astype(BF16)
    small = mm(pick, near).astype(BF16)
    small = small + swap(small, "cols", 1)
    w_pad = jnp.concatenate(
        [small[:FIN], small[FIN + NCLS : FIN + NCLS + 1], jnp.zeros((LANES - FIN - 1, HID), BF16)], 0
    )
    w_third = small[FIN : FIN + NCLS].reshape(HID, NCLS)
    gap = jnp.zeros((HID, LANES // 2 - NCLS), BF16)
    w_third = jnp.concatenate([w_third, gap, w_third, gap], 1)
    b_second = small[FIN + NCLS + 1].astype(F32)[None]
    b_third = small[FIN + NCLS + 2].astype(F32)[: LANES // 2]
    b_third = jnp.concatenate([b_third, b_third])[None]
    w_wide = mm(w_pad, expand).astype(BF16)

    near_parts, far_parts = [], []
    for m in range(MB):
        if m:
            for i, j in enumerate(z_order[1:]):
                strips[m].append(swap(after(leave[m][i], *strips[m - 1][1:]), "cols", 2 * j))
        if m == MB - 1:
            w_wide = after(w_wide, w_third)
        part_near, part_far = forward_two(g_all, w_wide, strips[m], m)
        near_parts.append(part_near)
        far_parts.append(swap(part_far, "cols", 1))

    diag = diagonal.T
    counted = train_mask.T.astype(F32)
    here = jnp.broadcast_to(jnp.sum(counted), (1, LANES))
    g_near, g_far, z_two, h_two, q = layer_two(
        near_parts, far_parts, g_one.reshape(MB * ns, LANES), w_wide, diag, near, far,
        b_second, w_third, here,
    )

    part_near, part_far = logits_parts(strips, over_rows(jnp.stack(over_z(q))))
    d_s, sums = call(
        loss_kernel,
        "loss",
        (shaped((ns, LANES), BF16), shaped((8, LANES))),
        [IN_VMEM] * 7,
        (IN_VMEM, IN_VMEM),
    )(part_near, swap(part_far, "cols", 1), q, diag, b_third, labels.T, counted)
    d_bias_three = sums[0, :NCLS] + sums[0, LANES // 2 : LANES // 2 + NCLS]
    loss, node_total = sums[1, 0], sums[2, 0]

    d_q = d_q_parts(tile, over_z(jnp.stack([d_s, swap(d_s, "cols", 1)])))
    d_q = [d_q[0]] + [swap(d_q[j], "rows", j) for j in range(1, n_rows)]

    def split(item, axis, bit):
        dim = 0 if axis == "rows" else 1
        kept, send, item["orders"][axis] = split_bit(item["part"], dim, item["orders"][axis], bit)
        item["kept"], item["send"] = kept, send.astype(BF16)
        item["to"] = (axis, bit * (dim + 1))

    half = HID // 2
    work = []
    for k, bits in enumerate((row_bits, turned)):
        lo, hi = k * half, (k + 1) * half
        wait = d_s if k == 0 else after(d_s, work[0]["dz"])
        d_zb, d_b, d_w3, d_near, d_far = d_two(
            d_q, wait, diag, z_two, h_two, w_third, g_near, g_far, lo, hi
        )
        item = {"bits": bits, "dz": d_zb, "db": d_b, "dw3": d_w3}
        item["orders"] = {"rows": list(range(n_rows)), "cols": z_order}
        part = d_near + swap(d_far, "cols", 1).astype(F32)
        item["part"] = part.reshape(n_rows, n_z, slot, half)
        split(item, "rows", bits[0])
        work.append(item)
    d_zb = [item["dz"] for item in work]
    d_bias_two = jnp.concatenate([jnp.sum(item["db"], axis=0) for item in work])
    d_w_three = jnp.concatenate([item["dw3"] for item in work], 0)
    d_w_three = d_w_three[:, :NCLS] + d_w_three[:, LANES // 2 : LANES // 2 + NCLS]

    span = 2 * n_near
    n_cuts = 3
    cuts = [span // LANES // 2 * i // n_cuts * 2 * LANES for i in range(n_cuts + 1)]
    d_zb[0] = after(d_zb[0], *[item["send"] for item in work])
    d_g_near, d_g_far = d_g_wide(d_zb, [(0, half), (half, HID)], near, far)
    d_g_near = d_g_near.reshape(MB, ns, span)
    d_g_far = swap(d_g_far.reshape(MB, ns, span), "cols", 1)
    d_first = []

    def another_cut():
        i = len(d_first)
        if i < n_cuts:
            d_first.append(
                backward_one(g_all, w_wide, strips, d_g_near, d_g_far, diag, cuts[i], cuts[i + 1])
            )

    another_cut()
    for i in range(len(row_bits)):
        for item in work:
            item["part"] = item["kept"] + swap(item["send"], *item["to"]).astype(F32)
            if i + 1 < len(row_bits):
                split(item, "rows", item["bits"][i + 1])
        if i + 1 < len(row_bits):
            d_g_near = after(d_g_near, *[item["send"] for item in work])
            another_cut()
    item = {"orders": {"cols": z_order}, "part": jnp.concatenate([item["part"] for item in work], 3)}
    for bit in z_bits:
        split(item, "cols", bit)
        if bit == z_bits[0]:
            d_g_near = after(d_g_near, item["send"])
            another_cut()
        item["part"] = item["kept"] + swap(item["send"], *item["to"]).astype(F32)
    own_grad = item["part"][0, 0]
    d_first = mm_nt(jnp.concatenate(d_first, 1), expand)
    d_w_one, d_bias_one = d_first[:FIN], d_first[FIN]

    pad_bias = jnp.pad(d_bias_three, (0, HID - NCLS))
    d_small = jnp.concatenate(
        [
            d_w_one,
            d_w_three.reshape(NCLS, HID),
            d_bias_one[None],
            d_bias_two[None],
            pad_bias[None],
            jnp.zeros((n_small - FIN - NCLS - 3, HID), F32),
        ],
        0,
    ).astype(BF16)
    d_small = d_small.reshape(n_dev, per_small * UNIT, LANES)
    got = lax.all_to_all(d_small, BOTH, split_axis=0, concat_axis=0, tiled=True)
    got = jnp.sum(got.astype(F32), axis=0)
    low = got.astype(BF16)
    sent = jnp.broadcast_to(low[None], d_small.shape)
    d_small = lax.all_to_all(sent, BOTH, split_axis=0, concat_axis=0, tiled=True)
    d_small = d_small.reshape(n_small, HID)

    own_flat = lax.dynamic_slice(own_grad.reshape(slot * UNIT, LANES), (shift, 0), (n_own, LANES))
    squares = jnp.sum(own_flat * own_flat) + jnp.sum(low.astype(F32) ** 2)
    row = jnp.concatenate([squares[None], loss[None], d_bias_three, jnp.zeros((LANES - NCLS - 2,), F32)])
    row = total_over_all(after(row[None], d_small))[0]
    squares, loss_sum, class_sum = row[0], row[1], row[2 : 2 + NCLS]

    mine = (n_own * me) // UNIT + jnp.arange(slot)
    place = (mine[:, None] == small_unit[None, :]).astype(BF16)
    small_flat = lax.dynamic_slice(
        mm(place, d_small).reshape(slot * UNIT, LANES), (shift, 0), (n_own, LANES)
    )
    reduced = (own_flat + small_flat).reshape(-1)

    grad_norm = jnp.sqrt(squares)
    clip_scale = jnp.minimum(1.0, CLIP_NORM / (grad_norm + 1e-06))
    clipped = reduced * clip_scale
    class_bias_grad = class_sum * clip_scale
    new_first = BETA_ONE * first_moment + (1.0 - BETA_ONE) * clipped
    new_second = BETA_TWO * second_moment + (1.0 - BETA_TWO) * clipped * clipped
    correct_one = 1.0 - BETA_ONE**STEP
    correct_two = 1.0 - BETA_TWO**STEP
    step_size = new_first / correct_one / (jnp.sqrt(new_second / correct_two) + EPSILON)
    new_params = params - LEARN_RATE * (step_size + WEIGHT_DECAY * params)
    return (new_params, new_first, new_second, grad_norm, loss_sum, node_total, class_bias_grad)


def solution(mesh):
    in_specs = (
        P(None, ("rows", "cols"), None),
        P(None, "rows", None, "cols", None),
        P(None, "rows", None, "cols", None),
        P(None, ("rows", "cols")),
        P(None, ("rows", "cols")),
        P(None, ("rows", "cols")),
        P(("rows", "cols")),
        P(("rows", "cols")),
        P(("rows", "cols")),
    )
    out_specs = (P(("rows", "cols")), P(("rows", "cols")), P(("rows", "cols")), P(), P(), P(), P())
    return jax.shard_map(
        per_device, mesh=mesh, in_specs=in_specs, out_specs=out_specs, check_vma=False
    )
```

```python
import math

import jax
import jax.numpy as jnp
from jax import lax
from jax.experimental import pallas as pl
from jax.experimental.pallas import tpu as pltpu
from jax.sharding import PartitionSpec as P

FIN = 100
HID = 2048
NCLS = 47
BLK = 128
MB = 2
STEP = 10
PARAMS = FIN * HID + HID * HID + HID * NCLS + 2 * HID + NCLS

LAMBDA = 1.0
CLIP_NORM = 0.01
BETA_ONE = 0.9
BETA_TWO = 0.95
EPSILON = 1e-08
WEIGHT_DECAY = 0.1
LEARN_RATE = 0.02

LANES = 128
UNIT = HID // LANES
BOTH = ("rows", "cols")
GELU_ONE = 0.7978845608028654
GELU_THREE = GELU_ONE * 0.044715
F32 = jnp.float32
FAR_BYTES = 1 << 17
BF16 = jnp.bfloat16


def swap(x, axis, bit):
    size = lax.axis_size(axis)
    return lax.ppermute(x, axis, [(i, i ^ bit) for i in range(size)])


def bits_of(size):
    return [1 << i for i in range(size.bit_length() - 1)]


def mm(left, right):
    return jnp.dot(left, right, preferred_element_type=F32)


def mm_t(left, right):
    return lax.dot_general(left, right, (((0,), (0,)), ((), ())), preferred_element_type=F32)


def mm_nt(left, right):
    return lax.dot_general(left, right, (((1,), (1,)), ((), ())), preferred_element_type=F32)


def take(x, axis, picks):
    return jnp.concatenate([lax.slice_in_dim(x, p, p + 1, axis=axis) for p in picks], axis)


def split_bit(x, axis, order, bit):
    keep = [j for j in order if not j & bit]
    run = next(i for i, j in enumerate(order) if j & bit)
    if any(bool(j & bit) != bool(i // run % 2) or j & ~bit != order[i - i // run % 2 * run] & ~bit for i, j in enumerate(order)):
        at = {j: i for i, j in enumerate(order)}
        return take(x, axis, [at[j] for j in keep]), take(x, axis, [at[j | bit] for j in keep]), keep
    shape = x.shape[:axis] + (len(order) // (2 * run), 2, run) + x.shape[axis + 1 :]
    kept_shape = x.shape[:axis] + (len(keep),) + x.shape[axis + 1 :]
    x = x.reshape(shape)
    pair = [lax.index_in_dim(x, i, axis + 1, keepdims=False).reshape(kept_shape) for i in (0, 1)]
    return pair[0], pair[1], keep


ANYWHERE = pl.BlockSpec(memory_space=pl.ANY)
IN_VMEM = pl.BlockSpec(memory_space=pltpu.VMEM)
IN_SMEM = pl.BlockSpec(memory_space=pltpu.SMEM)


def tip(x):
    while x.ndim > 2:
        x = x[0]
    return x[:8, :128].astype(F32)


def after_kernel(*refs):
    pass


def after(x, *earlier):
    earlier = [tip(e) for e in earlier]
    return pl.pallas_call(
        after_kernel,
        out_shape=jax.ShapeDtypeStruct(x.shape, x.dtype),
        in_specs=[ANYWHERE] * (1 + len(earlier)),
        out_specs=ANYWHERE,
        input_output_aliases={0: 0},
        name="after",
    )(x, *earlier)


def padded_bytes(shape, dtype):
    *front, rows, lanes = (1, 1, *shape)
    size = -(-rows // 16) * 16 * -(-lanes // LANES) * LANES * jnp.dtype(dtype).itemsize
    for n in front:
        size *= n
    return size


def call(kernel, name, out_shape, in_specs, out_specs, grid=None, room=4, scratch=()):
    more = {} if grid is None else {"grid": grid}

    def run(*args):
        outs = out_shape if isinstance(out_shape, tuple) else (out_shape,)
        specs = (*in_specs, *(out_specs if isinstance(out_specs, tuple) else (out_specs,)))
        total = room << 20
        for spec, x in zip(specs, (*args, *outs)):
            if spec.block_shape is not None:
                total += 2 * padded_bytes(spec.block_shape, x.dtype)
            elif spec.memory_space == pltpu.VMEM:
                total += padded_bytes(x.shape, x.dtype)
        large = lambda x: math.prod(x.shape) * x.dtype.itemsize >= FAR_BYTES
        args = [pltpu.with_memory_space_constraint(x, pltpu.HBM) if large(x) else x for x in args]
        placed = [
            pltpu.HBM(x.shape, x.dtype) if large(x) and spec.block_shape is not None else x
            for spec, x in zip(specs[len(args) :], outs)
        ]
        return pl.pallas_call(
            kernel,
            out_shape=tuple(placed) if isinstance(out_shape, tuple) else placed[0],
            in_specs=in_specs,
            out_specs=out_specs,
            scratch_shapes=list(scratch),
            compiler_params=pltpu.CompilerParams(vmem_limit_bytes=total),
            cost_estimate=pl.CostEstimate(flops=0, bytes_accessed=0, transcendentals=0),
            name=name,
            **more,
        )(*args)

    return run


def shaped(shape, dtype=F32):
    return jax.ShapeDtypeStruct(shape, dtype)


def lane_of(shape):
    return lax.broadcasted_iota(jnp.int32, shape, len(shape) - 1)


def masked_tile_kernel(row_order, n_across, n_pieces, where_ref, mask_ref, tile_ref, *refs):
    out_refs, wide_ref = refs[:-1], refs[-1]
    col, row = where_ref[0], where_ref[1]
    tall = BLK * n_across
    per_piece = len(row_order) // n_pieces
    for m in range(MB):
        for i, j in enumerate(row_order):
            block = col ^ j
            wide_ref[...] = tile_ref[m, pl.ds(pl.multiple_of(block * tall, tall), tall), :].astype(F32)
            piece, low = i // per_piece, i % per_piece * BLK
            for k in range(n_across):
                keep = mask_ref[(m * len(row_order) + block) * n_across + k].astype(F32)
                part = (wide_ref[pl.ds(k, BLK, n_across), :] * keep).astype(BF16)
                lanes = pl.ds(pl.multiple_of((row ^ k) * BLK, BLK), BLK)
                out_refs[m * n_pieces + piece][low : low + BLK, lanes] = part
                if piece:
                    at = MB * n_pieces + m * (n_pieces - 1) + piece - 1
                    out_refs[at][low : low + BLK, lanes] = part


def masked_tile(adjacency, block_mask, row_order, my_col, my_row):
    n_across = adjacency.shape[2]
    n_pieces = len(row_order) // 2
    piece = shaped((2 * BLK, n_across * BLK), BF16)
    n_out = MB * (2 * n_pieces - 1)
    out = call(
        lambda *refs: masked_tile_kernel(row_order, n_across, n_pieces, *refs),
        "masked_tile",
        (piece,) * n_out,
        [IN_SMEM, IN_SMEM, pl.BlockSpec((MB, adjacency.shape[1] * n_across, LANES), lambda i: (0, 0, 0))],
        (pl.BlockSpec((2 * BLK, n_across * BLK), lambda i: (0, 0)),) * n_out,
        grid=(1,),
        room=4,
        scratch=[pltpu.VMEM((n_across * BLK, LANES), F32)],
    )(
        jnp.stack([my_col, my_row]).astype(jnp.int32),
        block_mask.reshape(-1),
        adjacency.reshape(MB, -1, LANES),
    )
    tile = [out[m * n_pieces : (m + 1) * n_pieces] for m in range(MB)]
    leave = out[MB * n_pieces :]
    return tile, [leave[m * (n_pieces - 1) : (m + 1) * (n_pieces - 1)] for m in range(MB)]


def layer_one_kernel(n_z, *refs):
    tile_refs, feat_refs, (near_ref, far_ref) = refs[: MB * n_z], refs[MB * n_z : -2], refs[-2:]
    ns = near_ref.shape[2]
    for m in range(MB):
        feats = jnp.concatenate([f[m] for f in feat_refs], 0)
        for i in range(n_z):
            out = mm(tile_refs[m * n_z + i][...], feats)
            near_ref[i, m] = out[:ns]
            far_ref[i, m] = out[ns:]


def layer_one(tile, feats):
    n_z = len(tile[0])
    half, across = tile[0][0].shape
    out = shaped((n_z, MB, half // 2, LANES))
    return call(
        lambda *refs: layer_one_kernel(n_z, *refs),
        "layer_one",
        (out, out),
        [pl.BlockSpec((half, across), lambda i: (0, 0))] * (MB * n_z) + [IN_VMEM] * len(feats),
        (IN_VMEM, IN_VMEM),
        grid=(1,),
    )(*tile[0], *tile[1], *feats)


def twice_gelu(z):
    return z + z * jnp.tanh(z * (GELU_ONE + GELU_THREE * (z * z)))


def twice_gelu_both(z):
    square = z * z
    t = jnp.tanh(z * (GELU_ONE + GELU_THREE * square))
    slope = z * (GELU_ONE + (3 * GELU_THREE) * square)
    return z + z * t, (1.0 + t) * (1.0 + (1.0 - t) * slope)


def forward_kernel(n_z, n_rows, m, *refs):
    g_refs, strip_refs = refs[:n_rows], refs[n_rows : n_rows + n_z]
    w_ref, near_ref, far_ref, slope_ref = refs[n_rows + n_z :]
    half = near_ref.shape[0]
    total = None
    for i in range(n_z):
        g = jnp.concatenate([g_ref[i, m] for g_ref in g_refs], 0)
        h, slope = twice_gelu_both(mm(g, w_ref[...]))
        n = g.shape[0]
        slope_ref[i * n : (i + 1) * n] = slope.astype(BF16)
        part = mm(strip_refs[i][...], h.astype(BF16))
        total = part if total is None else total + part
    near_ref[...] = 0.5 * total[:half]
    far_ref[...] = (0.5 * total[half:]).astype(BF16)


def forward_two(g_all, w_pad, strip, m, wide=256):
    n_rows, n_z = len(g_all), len(strip)
    rows, across = strip[0].shape
    span = w_pad.shape[1]
    n = n_z * across
    return call(
        lambda *refs: forward_kernel(n_z, n_rows, m, *refs),
        "forward_two",
        (shaped((rows // 2, span)), shaped((rows // 2, span), BF16), shaped((n, span), BF16)),
        [pl.BlockSpec(g_all[0].shape, lambda f: (0, 0, 0, 0))] * n_rows
        + [pl.BlockSpec((rows, across), lambda f: (0, 0))] * n_z
        + [pl.BlockSpec((LANES, wide), lambda f: (0, f))],
        (pl.BlockSpec((rows // 2, wide), lambda f: (0, f)),) * 2 + (pl.BlockSpec((n, wide), lambda f: (0, f)),),
        grid=(span // wide,),
        room=2 + 8 * across // 1024,
    )(*g_all, *strip, w_pad)


def one_hot(here, there):
    return jnp.where(here == there, 1.0, 0.0).astype(BF16)


def spread_kernel(n_m, n_blocks, *refs):
    near_parts, far_parts = refs[:n_m], refs[n_m : 2 * n_m]
    g_one_ref, w_ref, diag_ref, which_ref, gn_ref, gf_ref, g_ref = refs[2 * n_m :]
    ns = near_parts[0].shape[0]

    @pl.when(pl.program_id(0) == 0)
    def _():
        step = 256
        for at in range(0, HID, step):
            cut = slice(at, at + step)
            h = (0.5 * twice_gelu(mm(g_one_ref[...], w_ref[:, cut]))).astype(BF16)
            for m in range(n_m):
                g_ref[m * ns : (m + 1) * ns, cut] = (
                    near_parts[m][:, cut]
                    + far_parts[m][:, cut].astype(F32)
                    + LAMBDA * diag_ref[:, m : m + 1] * h[m * ns : (m + 1) * ns].astype(F32)
                ).astype(BF16)

    which = which_ref[...]
    hot = one_hot(lax.broadcasted_iota(jnp.int32, (HID, which.shape[1]), 0), which)
    out = mm(g_ref[...], hot).astype(BF16)

    @pl.when(pl.program_id(0) < n_blocks)
    def _():
        gn_ref[...] = out

    @pl.when(pl.program_id(0) >= n_blocks)
    def _():
        gf_ref[...] = out


def block_width(n):
    return 384 if n % 384 == 0 else LANES


def spread_two(near_parts, far_parts, g_one, w_pad, diag, which):
    ns = near_parts[0].shape[0]
    n_m = len(near_parts)
    n_near = which.shape[1] // 2
    rows = n_m * ns
    wide = block_width(n_near)
    n = n_near // wide
    whole = lambda k: (0, 0)
    out = shaped((rows, n_near), BF16)
    return call(
        lambda *refs: spread_kernel(n_m, n, *refs),
        "spread_two",
        (out, out),
        [pl.BlockSpec((ns, HID), whole)] * (2 * n_m)
        + [
            pl.BlockSpec((rows, LANES), whole),
            pl.BlockSpec((LANES, HID), whole),
            pl.BlockSpec((ns, n_m), whole),
            pl.BlockSpec((1, wide), lambda k: (0, k)),
        ],
        (
            pl.BlockSpec((rows, wide), lambda k: (0, jnp.minimum(k, n - 1))),
            pl.BlockSpec((rows, wide), lambda k: (0, jnp.maximum(k - n, 0))),
        ),
        grid=(2 * n,),
        scratch=[pltpu.VMEM((rows, HID), BF16)],
        room=8,
    )(*near_parts, *far_parts, g_one, w_pad, diag, which)


def layer_two_kernel(gn_ref, gf_ref, wn_ref, wf_ref, b_ref, w3_ref, here_ref, z_ref, h_ref, q_ref, sum_ref):
    ns = sum_ref.shape[0]

    @pl.when(pl.program_id(0) == 0)
    def _():
        sum_ref[...] = jnp.zeros_like(sum_ref)

    z = mm(gn_ref[...], wn_ref[...]) + mm(gf_ref[...], wf_ref[...]) + b_ref[...]
    z_ref[...] = z
    h = (0.5 * twice_gelu(z)).astype(BF16)
    h_ref[...] = h
    q = mm(h, w3_ref[...])
    lane = lane_of(sum_ref.shape)
    sum_ref[...] += jnp.where(lane < LANES // 2, q[:ns], q[ns:])

    @pl.when(pl.program_id(0) == pl.num_programs(0) - 1)
    def _():
        q_ref[...] = jnp.where(lane == LANES - 1, here_ref[...], sum_ref[...]).astype(BF16)


def layer_two(g_near, g_far, near, far, b_second, w3, here, wide=512):
    rows, n_near = g_near.shape
    ns = rows // MB
    whole = lambda f: (0, 0)
    return call(
        layer_two_kernel,
        "layer_two",
        (shaped((rows, HID)), shaped((rows, HID), BF16), shaped((ns, LANES), BF16)),
        [
            pl.BlockSpec((rows, n_near), whole),
            pl.BlockSpec((rows, n_near), whole),
            pl.BlockSpec((n_near, wide), lambda f: (0, f)),
            pl.BlockSpec((n_near, wide), lambda f: (0, f)),
            pl.BlockSpec((1, wide), lambda f: (0, f)),
            pl.BlockSpec((wide, LANES), lambda f: (f, 0)),
            pl.BlockSpec((1, LANES), whole),
        ],
        (
            pl.BlockSpec((rows, wide), lambda f: (0, f)),
            pl.BlockSpec((rows, wide), lambda f: (0, f)),
            pl.BlockSpec((ns, LANES), whole),
        ),
        grid=(HID // wide,),
        scratch=[pltpu.VMEM((ns, LANES), F32)],
    )(g_near, g_far, near, far, b_second, w3, here)


def logits_kernel(n_z, *refs):
    strips, q_refs, (near_ref, far_ref) = refs[: MB * n_z], refs[MB * n_z : -2], refs[-2:]
    half = near_ref.shape[0]
    lane = lane_of((2 * half, LANES))
    sums = [None] * MB
    for i in range(n_z):
        all_q = jnp.concatenate([q[i] for q in q_refs], 0)
        for m in range(MB):
            part = mm(strips[m * n_z + i][...], all_q)
            sums[m] = part if sums[m] is None else sums[m] + part
    out = jnp.where(lane < LANES // 2, sums[0], sums[1])
    count = sum(jnp.sum(q[:, 0:1, :].astype(F32), axis=0) for q in q_refs)
    out = jnp.where(lane == LANES - 1, count, out)
    near_ref[...] = out[:half]
    far_ref[...] = out[half:]


def logits_parts(strips, q_rows):
    n_z = len(strips[0])
    rows, across = strips[0][0].shape
    out = shaped((rows // 2, LANES))
    return call(
        lambda *refs: logits_kernel(n_z, *refs),
        "logits_parts",
        (out, out),
        [pl.BlockSpec((rows, across), lambda i: (0, 0))] * (MB * n_z) + [IN_VMEM] * len(q_rows),
        (IN_VMEM, IN_VMEM),
        grid=(1,),
    )(*strips[0], *strips[1], *q_rows)


def loss_kernel(near_ref, got_ref, q_ref, diag_ref, bias_ref, labels_ref, counted_ref, ds_ref, row_ref):
    total = near_ref[...] + got_ref[...]
    node_total = total[0:1, LANES - 1 :]
    lane = lane_of(total.shape)
    low = lane < LANES // 2
    at = jnp.where(low, lane, lane - LANES // 2)
    real = at < NCLS
    pick = lambda ref: jnp.where(low, ref[:, 0:1], ref[:, 1:2])
    logits = total + LAMBDA * pick(diag_ref) * q_ref[...].astype(F32) + bias_ref[...]
    least = jnp.float32(-3.0e38)
    hits = jnp.logical_and(real, at == pick(labels_ref))
    counted = pick(counted_ref)
    parts = []
    for side in (jnp.logical_and(real, low), jnp.logical_and(real, jnp.logical_not(low))):
        top = jnp.max(jnp.where(side, logits, least), axis=1, keepdims=True)
        powers = jnp.where(side, jnp.exp(jnp.where(side, logits - top, 0.0)), 0.0)
        parts.append((top, jnp.sum(powers, axis=1, keepdims=True)))
    log_total = jnp.where(
        low, parts[0][0] + jnp.log(parts[0][1]), parts[1][0] + jnp.log(parts[1][1])
    )
    loss = jnp.where(hits, counted * (log_total - logits), 0.0)
    soft = jnp.exp(jnp.where(real, logits - log_total, 0.0))
    d_logits = jnp.where(real, counted * (soft - hits.astype(F32)) / node_total, 0.0)
    ds_ref[...] = d_logits.astype(BF16)
    row_ref[0:1] = jnp.sum(d_logits, axis=0, keepdims=True)
    row_ref[1:2] = jnp.broadcast_to(jnp.sum(jnp.sum(loss, axis=0, keepdims=True), axis=1, keepdims=True), (1, LANES))
    row_ref[2:3] = jnp.broadcast_to(node_total, (1, LANES))
    row_ref[3:8] = jnp.zeros((5, LANES), F32)


def d_q_kernel(n_z, *refs):
    tile_refs, s_refs, out_refs = refs[: MB * n_z], refs[MB * n_z : (MB + 1) * n_z], refs[(MB + 1) * n_z :]
    side = out_refs[0].shape[0]
    lane = lane_of((side * len(out_refs), LANES))
    sums = [None] * MB
    for i in range(n_z):
        all_s = jnp.concatenate([s_refs[i][core] for core in (0, 1)], 0)
        for m in range(MB):
            part = mm_t(tile_refs[m * n_z + i][...], all_s)
            sums[m] = part if sums[m] is None else sums[m] + part
    out = jnp.where(lane < LANES // 2, sums[0], sums[1])
    for k, out_ref in enumerate(out_refs):
        out_ref[...] = out[k * side : (k + 1) * side]


def d_q_parts(tile, pieces):
    n_z = len(pieces)
    rows, across = tile[0][0].shape
    n = across // BLK
    return call(
        lambda *refs: d_q_kernel(n_z, *refs),
        "d_q_parts",
        (shaped((BLK, LANES)),) * n,
        [pl.BlockSpec((rows, across), lambda i: (0, 0))] * (MB * n_z) + [IN_VMEM] * n_z,
        (IN_VMEM,) * n,
        grid=(1,),
    )(*tile[0], *tile[1], *pieces)


def d_two_kernel(n_q, *refs):
    q_refs = refs[:n_q]
    ds_ref, diag_ref, z_ref, h_ref, w3_ref, g_ref, dz_ref, db_ref, dw3_ref, far_ref = refs[n_q:]
    ns = ds_ref.shape[0]
    d_q = q_refs[0][...]
    for q in q_refs[1:]:
        d_q = d_q + q[...]
    low = lane_of(d_q.shape) < LANES // 2
    d_q = d_q + LAMBDA * jnp.where(low, diag_ref[:, 0:1], diag_ref[:, 1:2]) * ds_ref[...].astype(F32)
    d_q = jnp.concatenate([jnp.where(low, d_q, 0.0), jnp.where(low, 0.0, d_q)], 0).astype(BF16)
    d_z = mm_nt(d_q, w3_ref[...]) * (0.5 * twice_gelu_both(z_ref[...])[1])
    db_ref[...] = jnp.sum(d_z.reshape(-1, 8, d_z.shape[1]), axis=0)
    d_zb = d_z.astype(BF16)
    dz_ref[...] = d_zb
    dw3_ref[...] = mm_t(h_ref[...], d_q)
    far_ref[...] = mm_t(g_ref[...], d_zb).astype(BF16)


def d_two(d_q, d_s, diag, z_two, h_two, w3, g_far, lo, hi, wide=256):
    rows = z_two.shape[0]
    ns, n_far = d_s.shape[0], g_far.shape[1]
    whole = lambda f: (0, 0)
    start = lo // wide
    small = pl.BlockSpec((ns, LANES), whole)
    column = pl.BlockSpec((rows, wide), lambda f: (0, start + f))
    span = hi - lo
    return call(
        lambda *refs: d_two_kernel(len(d_q), *refs),
        "d_two",
        (
            shaped((rows, span), BF16),
            shaped((8, span)),
            shaped((span, LANES)),
            shaped((n_far, span), BF16),
        ),
        [small] * (len(d_q) + 1)
        + [
            pl.BlockSpec((ns, MB), whole),
            column,
            column,
            pl.BlockSpec((wide, LANES), lambda f: (start + f, 0)),
            pl.BlockSpec((rows, n_far), whole),
        ],
        (
            pl.BlockSpec((rows, wide), lambda f: (0, f)),
            pl.BlockSpec((8, wide), lambda f: (0, f)),
            pl.BlockSpec((wide, LANES), lambda f: (f, 0)),
            pl.BlockSpec((n_far, wide), lambda f: (0, f)),
        ),
        grid=(span // wide,),
        room=4,
    )(*d_q, d_s, diag, z_two, h_two, w3, g_far)


def near_kernel(keep, send, rows, g_ref, dz_ref, got_ref, keep_ref, send_ref):
    total = mm_t(g_ref[...], dz_ref[...]) + got_ref[...].astype(F32)
    for out_ref, picks in ((keep_ref, keep), (send_ref, send)):
        for i, j in enumerate(picks):
            out_ref[i * rows : (i + 1) * rows] = total[j * rows : (j + 1) * rows].astype(out_ref.dtype)


def near_part(g_near, d_zb, got, n_rows, bit, wide=256):
    n_near, span = got.shape
    rows = n_near // n_rows
    keep = [j for j in range(n_rows) if not j & bit]
    send = [j | bit for j in keep]
    column = lambda n: pl.BlockSpec((n, wide), lambda f: (0, f))
    return call(
        lambda *refs: near_kernel(keep, send, rows, *refs),
        "near_part",
        (shaped((n_near // 2, span)), shaped((n_near // 2, span), BF16)),
        [pl.BlockSpec(g_near.shape, lambda f: (0, 0)), column(g_near.shape[0]), column(n_near)],
        (column(n_near // 2), column(n_near // 2)),
        grid=(span // wide,),
    )(g_near, d_zb, got)


def backward_kernel(n_z, n_rows, *refs):
    g_refs, strip_refs = refs[:n_rows], refs[n_rows : n_rows + MB * n_z]
    slope_refs, (dgn_ref, dgf_ref, diag_ref, dw_ref) = refs[-4 - MB : -4], refs[-4:]
    own = dgn_ref.shape[1]
    total = None
    for m in range(MB):
        d_g = jnp.concatenate([dgn_ref[m], dgf_ref[m]], 0)
        for i in range(n_z):
            d_h = mm_t(strip_refs[m * n_z + i][...], d_g)
            n = d_h.shape[0]
            if i == 0:
                more = LAMBDA * diag_ref[:, m : m + 1] * dgn_ref[m].astype(F32)
                d_h = jnp.concatenate([d_h[:own] + more, d_h[own:]], 0)
            g = jnp.concatenate([g_ref[i, m] for g_ref in g_refs], 0)
            d_z = d_h * slope_refs[m][i * n : (i + 1) * n].astype(F32)
            part = mm_t(g, d_z.astype(BF16))
            total = part if total is None else total + part
    dw_ref[...] = (0.5 * total).astype(BF16)


def backward_one(g_all, strips, slopes, d_g_near, d_g_far, diag, lo, hi, wide=256):
    n_rows, n_z = len(g_all), len(strips[0])
    rows, across = strips[0][0].shape
    span = hi - lo
    start = lo // wide
    column = pl.BlockSpec((MB, rows // 2, wide), lambda f: (0, 0, start + f))
    return call(
        lambda *refs: backward_kernel(n_z, n_rows, *refs),
        "backward_one",
        shaped((LANES, span), BF16),
        [pl.BlockSpec(g_all[0].shape, lambda f: (0, 0, 0, 0))] * n_rows
        + [pl.BlockSpec((rows, across), lambda f: (0, 0))] * (MB * n_z)
        + [pl.BlockSpec((n_z * across, wide), lambda f: (0, start + f))] * MB
        + [column, column, pl.BlockSpec((rows // 2, MB), lambda f: (0, 0))],
        pl.BlockSpec((LANES, wide), lambda f: (0, f)),
        grid=(span // wide,),
        room=2 + 8 * across // 1024,
    )(*g_all, *strips[0], *strips[1], *slopes, d_g_near, d_g_far, diag)


def d_g_kernel(n_blocks, cuts, *refs):
    dz_refs, (which_ref, wn_ref, wf_ref, out_ref, sum_ref) = refs[: len(cuts)], refs[len(cuts) :]
    step = pl.program_id(0)

    @pl.when(step == 0)
    def _():
        sum_ref[...] = jnp.zeros_like(sum_ref)

    def add(w_ref):
        part = sum(mm_nt(dz[...], w_ref[:, lo:hi]) for dz, (lo, hi) in zip(dz_refs, cuts)).astype(BF16)
        which = which_ref[...]
        hot = one_hot(lax.broadcasted_iota(jnp.int32, (which.shape[0], HID), 1), which)
        sum_ref[...] += mm(part, hot)

    @pl.when(step < n_blocks)
    def _():
        add(wn_ref)

    @pl.when(step >= n_blocks)
    def _():
        add(wf_ref)

    @pl.when(step == pl.num_programs(0) - 1)
    def _():
        out_ref[...] = sum_ref[...].astype(BF16)


def d_g_two(d_zb, cuts, which, near, far):
    rows, n_near = d_zb[0].shape[0], near.shape[0]
    wide = block_width(n_near)
    n = n_near // wide
    return call(
        lambda *refs: d_g_kernel(n, cuts, *refs),
        "d_g_two",
        shaped((rows, HID), BF16),
        [pl.BlockSpec(d.shape, lambda k: (0, 0)) for d in d_zb]
        + [
            pl.BlockSpec((wide, 1), lambda k: (k, 0)),
            pl.BlockSpec((wide, HID), lambda k: (jnp.minimum(k, n - 1), 0)),
            pl.BlockSpec((wide, HID), lambda k: (jnp.maximum(k - n, 0), 0)),
        ],
        pl.BlockSpec((rows, HID), lambda k: (0, 0)),
        grid=(2 * n,),
        scratch=[pltpu.VMEM((rows, HID), F32)],
        room=8,
    )(*d_zb, which, near, far)


def thirds_kernel(row_ref, out_ref):
    rest = row_ref[...]
    out_ref[...] = jnp.zeros_like(out_ref)
    for i in range(3):
        low = rest.astype(BF16)
        out_ref[i : i + 1] = low
        rest = rest - low.astype(F32)


def thirds(row):
    return call(thirds_kernel, "thirds", shaped((16, LANES), BF16), [IN_VMEM], IN_VMEM)(row)


def join_kernel(sizes, *refs):
    pieces, out_ref, sems = refs[: len(sizes)], refs[len(sizes)], refs[-1]
    at, copies = 0, []
    for i, (piece, size) in enumerate(zip(pieces, sizes)):
        copies.append(pltpu.make_async_copy(piece, out_ref.at[pl.ds(at, size)], sems.at[i]))
        copies[-1].start()
        at += size
    for copy in copies:
        copy.wait()


def join(pieces):
    sizes = [p.shape[0] for p in pieces]
    return call(
        lambda *refs: join_kernel(sizes, *refs),
        "join",
        shaped((sum(sizes),) + pieces[0].shape[1:], pieces[0].dtype),
        [ANYWHERE] * len(pieces),
        IN_VMEM,
        room=2,
        scratch=[pltpu.SemaphoreType.DMA((len(pieces),))],
    )(*pieces)


def per_device(features, adjacency, block_mask, diagonal, labels, train_mask, params, first_moment, second_moment):
    n_rows, n_cols = lax.axis_size("rows"), lax.axis_size("cols")
    n_z = n_cols // 2
    n_dev = n_rows * n_cols
    my_row, my_col = lax.axis_index("rows"), lax.axis_index("cols")
    me = my_row * n_cols + my_col
    ns = features.shape[1]
    z_bits, row_bits = bits_of(n_z), bits_of(n_rows)
    turned = row_bits[1:] + row_bits[:1]
    single = z_bits[::-1]
    several = [j for j in range(1, n_z) if j not in single]
    z_order = [0] + single + several

    def over_z(x):
        return [x] + [swap(x, "cols", 2 * j) for j in z_order[1:]]

    def over_rows(x):
        return [x] + [swap(x, "rows", j) for j in range(1, n_rows)]

    n_own = params.shape[0] // LANES
    slot = -(-((n_own + UNIT - 2) // UNIT + 1) // 8) * 8
    shift = lax.rem(n_own * me, UNIT)
    own = lax.dynamic_update_slice(
        jnp.zeros((slot * UNIT, LANES), BF16), params.reshape(n_own, LANES).astype(BF16), (shift, 0)
    ).reshape(1, slot, HID)
    wide_feats = jnp.pad(features, ((0, 0), (0, 0), (0, LANES - FIN)))
    ones = lax.broadcasted_iota(jnp.int32, (1, 1, LANES), 2) == FIN
    feats = over_rows(wide_feats)
    tile, leave = masked_tile(
        adjacency.reshape(MB, -1, n_rows, LANES), block_mask, [2 * j + core for j in z_order for core in (0, 1)], my_col, my_row
    )

    part_near, part_far = layer_one(tile, feats)
    own = after(own, part_far)
    by_z = {0: own}
    for j in single:
        by_z[j] = swap(own, "cols", 2 * j)
    partial = part_near + swap(part_far, "cols", 1)
    g_one = partial[0] + LAMBDA * diagonal[:, :, None] * wide_feats.astype(F32)
    low = partial.astype(BF16)
    for i, j in enumerate(z_order[1:], 1):
        g_one = g_one + swap(low[i], "cols", 2 * j).astype(F32)
    g_one = jnp.where(ones, 1.0, g_one).astype(BF16)

    def units_of(core):
        owner = (my_row ^ jnp.arange(n_rows))[:, None] * n_cols + (
            my_col ^ (2 * jnp.array(z_order) + core)
        )[None, :]
        start = (n_own * owner) // UNIT
        return (start[:, :, None] + jnp.arange(slot)[None, None, :]).reshape(-1)

    near_units = units_of(0)
    units = jnp.concatenate([near_units, units_of(1)])
    which = units - FIN

    middle = after(join([by_z[j] for j in single]), g_one)
    for j in several:
        bit = j & -j
        by_z[j] = swap(by_z[j - bit], "cols", 2 * bit)
    last = by_z[several[0]] if len(several) == 1 else join([by_z[j] for j in several])
    g_z = over_z(g_one)
    last = after(last, *g_z[1:])
    groups = [own, middle, last]
    g_all = over_rows(jnp.stack(g_z))
    strips = [[tile[m][0]] for m in range(MB)]
    for i, j in enumerate(z_order[1:]):
        strips[0].append(swap(after(leave[0][i], *g_all[1:]), "cols", 2 * j))
    passed = {0: groups}
    for j in range(1, n_rows):
        lowest = j & -j
        highest = 1 << (j.bit_length() - 1)
        hop = [passed[j - bit][i] for i, bit in enumerate((highest, lowest, highest))]
        if lowest != highest:
            hop = [after(h, *g_all[1:]) for h in hop]
        passed[j] = [swap(h, "rows", bit) for h, bit in zip(hop, (highest, lowest, highest))]
    for m in range(1, MB):
        for i, j in enumerate(z_order[1:]):
            strips[m].append(swap(after(leave[m][i], *strips[m - 1][1:]), "cols", 2 * j))
    passed[0][0] = after(passed[0][0], *strips[0][1:])
    near = join([g.reshape(-1, HID) for j in range(n_rows) for g in passed[j]])
    far = swap(near, "cols", 1)
    n_near = near.shape[0]

    per_small = -(-(FIN + NCLS + 3) // n_dev)
    n_small = per_small * n_dev
    small_unit = jnp.arange(n_small)
    small_unit = jnp.where(small_unit < FIN, small_unit, small_unit + HID)
    pick = (small_unit[:, None] == near_units[None, :]).astype(BF16)
    small = mm(pick, near).astype(BF16)
    small = small + swap(small, "cols", 1)
    w_pad = jnp.concatenate(
        [small[:FIN], small[FIN + NCLS : FIN + NCLS + 1], jnp.zeros((LANES - FIN - 1, HID), BF16)], 0
    )
    w_third = small[FIN : FIN + NCLS].reshape(HID, NCLS)
    gap = jnp.zeros((HID, LANES // 2 - NCLS), BF16)
    w_third = jnp.concatenate([w_third, gap, w_third, gap], 1)
    b_second = small[FIN + NCLS + 1].astype(F32)[None]
    b_third = small[FIN + NCLS + 2].astype(F32)[: LANES // 2]
    b_third = jnp.concatenate([b_third, b_third])[None]

    near_parts, far_parts, slopes = [], [], []
    for m in range(MB):
        if m == MB - 1:
            w_pad = after(w_pad, w_third)
        part_near, part_far, slope = forward_two(g_all, w_pad, strips[m], m)
        slopes.append(slope)
        near_parts.append(part_near)
        far_parts.append(swap(part_far, "cols", 1))

    diag = diagonal.T
    counted = train_mask.T.astype(F32)
    here = jnp.broadcast_to(jnp.sum(counted), (1, LANES))
    g_near, g_far = spread_two(
        near_parts, far_parts, g_one.reshape(MB * ns, LANES), w_pad, diag, which[None]
    )
    z_two, h_two, q = layer_two(g_near, g_far, near, far, b_second, w_third, here)

    part_near, part_far = logits_parts(strips, over_rows(jnp.stack(over_z(q))))
    d_s, sums = call(
        loss_kernel,
        "loss",
        (shaped((ns, LANES), BF16), shaped((8, LANES))),
        [IN_VMEM] * 7,
        (IN_VMEM, IN_VMEM),
    )(part_near, swap(part_far, "cols", 1), q, diag, b_third, labels.T, counted)
    d_bias_three = sums[0, :NCLS] + sums[0, LANES // 2 : LANES // 2 + NCLS]
    loss, node_total = sums[1, 0], sums[2, 0]

    d_q = d_q_parts(tile, over_z(jnp.stack([d_s, swap(d_s, "cols", 1)])))
    d_q = [d_q[0]] + [swap(d_q[j], "rows", j) for j in range(1, n_rows)]

    def split(item, axis, bit):
        dim = 0 if axis == "rows" else 1
        kept, send, item["orders"][axis] = split_bit(item["part"], dim, item["orders"][axis], bit)
        item["kept"], item["send"] = kept, send.astype(BF16)
        item["to"] = (axis, bit * (dim + 1))

    half = HID // 2
    work = []
    for k, bits in enumerate((row_bits, turned)):
        lo, hi = k * half, (k + 1) * half
        wait = d_s if k == 0 else after(d_s, work[0]["dz"])
        d_zb, d_b, d_w3, d_far = d_two(d_q, wait, diag, z_two, h_two, w_third, g_far, lo, hi)
        item = {"bits": bits, "dz": d_zb, "db": d_b, "dw3": d_w3}
        item["got"] = swap(d_far, "cols", 1)
        item["orders"] = {"rows": [j for j in range(n_rows) if not j & bits[0]], "cols": z_order}
        item["to"] = ("rows", bits[0])
        work.append(item)
    for item in work:
        kept, send = near_part(g_near, item["dz"], item["got"], n_rows, item["bits"][0])
        item["kept"], item["send"] = (x.reshape(n_rows // 2, n_z, slot, half) for x in (kept, send))
    d_zb = [item["dz"] for item in work]
    d_bias_two = jnp.concatenate([jnp.sum(item["db"], axis=0) for item in work])
    d_w_three = jnp.concatenate([item["dw3"] for item in work], 0)
    d_w_three = d_w_three[:, :NCLS] + d_w_three[:, LANES // 2 : LANES // 2 + NCLS]

    n_cuts = 3
    cuts = [0, 3 * (HID // 8), 6 * (HID // 8), HID]
    d_zb[0] = after(d_zb[0], *[item["send"] for item in work])
    d_g_near = d_g_two(d_zb, [(0, half), (half, HID)], which[:, None], near, far).reshape(MB, ns, HID)
    d_g_far = swap(d_g_near, "cols", 1)
    d_first = []

    def another_cut():
        i = len(d_first)
        if i < n_cuts:
            d_first.append(
                backward_one(g_all, strips, slopes, d_g_near, d_g_far, diag, cuts[i], cuts[i + 1])
            )

    for i in range(len(row_bits)):
        for item in work:
            item["part"] = item["kept"] + swap(item["send"], *item["to"]).astype(F32)
            if i + 1 < len(row_bits):
                split(item, "rows", item["bits"][i + 1])
        if i + 1 < len(row_bits):
            d_g_near = after(d_g_near, *[item["send"] for item in work])
            another_cut()
    item = {"orders": {"cols": z_order}, "part": jnp.concatenate([item["part"] for item in work], 3)}
    for bit in z_bits:
        split(item, "cols", bit)
        d_g_near = after(d_g_near, item["send"])
        another_cut()
        item["part"] = item["kept"] + swap(item["send"], *item["to"]).astype(F32)
        if bit == z_bits[0]:
            early = item["part"]
    own_grad = item["part"][0, 0]
    d_first = jnp.concatenate(d_first, 1)
    d_w_one, d_bias_one = d_first[:FIN], d_first[FIN].astype(F32)

    d_small = jnp.concatenate(
        [
            d_w_one.astype(BF16),
            d_w_three.astype(BF16).reshape(NCLS, HID),
            jnp.stack([d_bias_one, d_bias_two, jnp.pad(d_bias_three, (0, HID - NCLS))]).astype(BF16),
            jnp.zeros((n_small - FIN - NCLS - 3, HID), BF16),
        ],
        0,
    )
    d_small = after(d_small.reshape(n_dev, per_small * UNIT, LANES), early)
    got = lax.all_to_all(d_small, BOTH, split_axis=0, concat_axis=0, tiled=True)
    got = jnp.sum(got.astype(F32), axis=0)
    low = got.astype(BF16)

    own_flat = lax.dynamic_slice(own_grad.reshape(slot * UNIT, LANES), (shift, 0), (n_own, LANES))
    squares = jnp.sum(own_flat * own_flat) + jnp.sum(low.astype(F32) ** 2)
    row = jnp.concatenate([squares[None], loss[None], d_bias_three, jnp.zeros((LANES - NCLS - 2,), F32)])
    sent = jnp.concatenate([low, thirds(row[None])], 0)
    sent = jnp.broadcast_to(sent[None], (n_dev,) + sent.shape)
    got = lax.all_to_all(sent, BOTH, split_axis=0, concat_axis=0, tiled=True)
    d_small = got[:, : per_small * UNIT].reshape(n_small, HID)
    row = jnp.sum(got[:, per_small * UNIT : per_small * UNIT + 3].astype(F32), axis=(0, 1))
    squares, loss_sum, class_sum = row[0], row[1], row[2 : 2 + NCLS]

    mine = (n_own * me) // UNIT + jnp.arange(slot)
    place = (mine[:, None] == small_unit[None, :]).astype(BF16)
    small_flat = lax.dynamic_slice(
        mm(place, d_small).reshape(slot * UNIT, LANES), (shift, 0), (n_own, LANES)
    )
    reduced = (own_flat + small_flat).reshape(-1)

    grad_norm = jnp.sqrt(squares)
    clip_scale = jnp.minimum(1.0, CLIP_NORM / (grad_norm + 1e-06))
    clipped = reduced * clip_scale
    class_bias_grad = class_sum * clip_scale
    new_first = BETA_ONE * first_moment + (1.0 - BETA_ONE) * clipped
    new_second = BETA_TWO * second_moment + (1.0 - BETA_TWO) * clipped * clipped
    correct_one = 1.0 - BETA_ONE**STEP
    correct_two = 1.0 - BETA_TWO**STEP
    step_size = new_first / correct_one / (jnp.sqrt(new_second / correct_two) + EPSILON)
    new_params = params - LEARN_RATE * (step_size + WEIGHT_DECAY * params)
    return (new_params, new_first, new_second, grad_norm, loss_sum, node_total, class_bias_grad)


def solution(mesh):
    in_specs = (
        P(None, ("rows", "cols"), None),
        P(None, "rows", None, "cols", None),
        P(None, "rows", None, "cols", None),
        P(None, ("rows", "cols")),
        P(None, ("rows", "cols")),
        P(None, ("rows", "cols")),
        P(("rows", "cols")),
        P(("rows", "cols")),
        P(("rows", "cols")),
    )
    out_specs = (P(("rows", "cols")), P(("rows", "cols")), P(("rows", "cols")), P(), P(), P(), P())
    return jax.shard_map(
        per_device, mesh=mesh, in_specs=in_specs, out_specs=out_specs, check_vma=False
    )
```

```python
import math

import jax
import jax.numpy as jnp
from jax import lax
from jax.experimental import pallas as pl
from jax.experimental.pallas import tpu as pltpu
from jax.sharding import PartitionSpec as P

FIN = 100
HID = 2048
NCLS = 47
BLK = 128
MB = 2
STEP = 10
PARAMS = FIN * HID + HID * HID + HID * NCLS + 2 * HID + NCLS

LAMBDA = 1.0
CLIP_NORM = 0.01
BETA_ONE = 0.9
BETA_TWO = 0.95
EPSILON = 1e-08
WEIGHT_DECAY = 0.1
LEARN_RATE = 0.02

LANES = 128
UNIT = HID // LANES
BOTH = ("rows", "cols")
GELU_ONE = 0.7978845608028654
GELU_THREE = GELU_ONE * 0.044715
F32 = jnp.float32
FAR_BYTES = 1 << 17
BF16 = jnp.bfloat16


def swap(x, axis, bit):
    size = lax.axis_size(axis)
    return lax.ppermute(x, axis, [(i, i ^ bit) for i in range(size)])


def bits_of(size):
    return [1 << i for i in range(size.bit_length() - 1)]


def mm(left, right):
    return jnp.dot(left, right, preferred_element_type=F32)


def mm_t(left, right):
    return lax.dot_general(left, right, (((0,), (0,)), ((), ())), preferred_element_type=F32)


def mm_nt(left, right):
    return lax.dot_general(left, right, (((1,), (1,)), ((), ())), preferred_element_type=F32)


def take(x, axis, picks):
    return jnp.concatenate([lax.slice_in_dim(x, p, p + 1, axis=axis) for p in picks], axis)


def split_bit(x, axis, order, bit):
    keep = [j for j in order if not j & bit]
    run = next(i for i, j in enumerate(order) if j & bit)
    if any(bool(j & bit) != bool(i // run % 2) or j & ~bit != order[i - i // run % 2 * run] & ~bit for i, j in enumerate(order)):
        at = {j: i for i, j in enumerate(order)}
        return take(x, axis, [at[j] for j in keep]), take(x, axis, [at[j | bit] for j in keep]), keep
    shape = x.shape[:axis] + (len(order) // (2 * run), 2, run) + x.shape[axis + 1 :]
    kept_shape = x.shape[:axis] + (len(keep),) + x.shape[axis + 1 :]
    x = x.reshape(shape)
    pair = [lax.index_in_dim(x, i, axis + 1, keepdims=False).reshape(kept_shape) for i in (0, 1)]
    return pair[0], pair[1], keep


ANYWHERE = pl.BlockSpec(memory_space=pl.ANY)
IN_VMEM = pl.BlockSpec(memory_space=pltpu.VMEM)
IN_SMEM = pl.BlockSpec(memory_space=pltpu.SMEM)


def tip(x):
    while x.ndim > 2:
        x = x[0]
    return x[:8, :128].astype(F32)


def after_kernel(*refs):
    pass


def after(x, *earlier):
    earlier = [tip(e) for e in earlier]
    return pl.pallas_call(
        after_kernel,
        out_shape=jax.ShapeDtypeStruct(x.shape, x.dtype),
        in_specs=[ANYWHERE] * (1 + len(earlier)),
        out_specs=ANYWHERE,
        input_output_aliases={0: 0},
        name="after",
    )(x, *earlier)


def padded_bytes(shape, dtype):
    *front, rows, lanes = (1, 1, *shape)
    size = -(-rows // 16) * 16 * -(-lanes // LANES) * LANES * jnp.dtype(dtype).itemsize
    for n in front:
        size *= n
    return size


def call(kernel, name, out_shape, in_specs, out_specs, grid=None, room=4, scratch=()):
    more = {} if grid is None else {"grid": grid}

    def run(*args):
        outs = out_shape if isinstance(out_shape, tuple) else (out_shape,)
        specs = (*in_specs, *(out_specs if isinstance(out_specs, tuple) else (out_specs,)))
        total = room << 20
        for spec, x in zip(specs, (*args, *outs)):
            if spec.block_shape is not None:
                total += 2 * padded_bytes(spec.block_shape, x.dtype)
            elif spec.memory_space == pltpu.VMEM:
                total += padded_bytes(x.shape, x.dtype)
        large = lambda x: math.prod(x.shape) * x.dtype.itemsize >= FAR_BYTES
        args = [pltpu.with_memory_space_constraint(x, pltpu.HBM) if large(x) else x for x in args]
        placed = [
            pltpu.HBM(x.shape, x.dtype) if large(x) and spec.block_shape is not None else x
            for spec, x in zip(specs[len(args) :], outs)
        ]
        return pl.pallas_call(
            kernel,
            out_shape=tuple(placed) if isinstance(out_shape, tuple) else placed[0],
            in_specs=in_specs,
            out_specs=out_specs,
            scratch_shapes=list(scratch),
            compiler_params=pltpu.CompilerParams(vmem_limit_bytes=total),
            cost_estimate=pl.CostEstimate(flops=0, bytes_accessed=0, transcendentals=0),
            name=name,
            **more,
        )(*args)

    return run


def shaped(shape, dtype=F32):
    return jax.ShapeDtypeStruct(shape, dtype)


def lane_of(shape):
    return lax.broadcasted_iota(jnp.int32, shape, len(shape) - 1)


def masked_tile_kernel(row_order, n_across, n_pieces, where_ref, mask_ref, tile_ref, *refs):
    out_refs, wide_ref = refs[:-1], refs[-1]
    col, row = where_ref[0], where_ref[1]
    tall = BLK * n_across
    per_piece = len(row_order) // n_pieces
    for m in range(MB):
        for i, j in enumerate(row_order):
            block = col ^ j
            wide_ref[...] = tile_ref[m, pl.ds(pl.multiple_of(block * tall, tall), tall), :].astype(F32)
            piece, low = i // per_piece, i % per_piece * BLK
            for k in range(n_across):
                keep = mask_ref[(m * len(row_order) + block) * n_across + k].astype(F32)
                part = (wide_ref[pl.ds(k, BLK, n_across), :] * keep).astype(BF16)
                lanes = pl.ds(pl.multiple_of((row ^ k) * BLK, BLK), BLK)
                out_refs[m * n_pieces + piece][low : low + BLK, lanes] = part
                if piece:
                    at = MB * n_pieces + m * (n_pieces - 1) + piece - 1
                    out_refs[at][low : low + BLK, lanes] = part


def masked_tile(adjacency, block_mask, row_order, my_col, my_row):
    n_across = adjacency.shape[2]
    n_pieces = len(row_order) // 2
    piece = shaped((2 * BLK, n_across * BLK), BF16)
    n_out = MB * (2 * n_pieces - 1)
    out = call(
        lambda *refs: masked_tile_kernel(row_order, n_across, n_pieces, *refs),
        "masked_tile",
        (piece,) * n_out,
        [IN_SMEM, IN_SMEM, pl.BlockSpec((MB, adjacency.shape[1] * n_across, LANES), lambda i: (0, 0, 0))],
        (pl.BlockSpec((2 * BLK, n_across * BLK), lambda i: (0, 0)),) * n_out,
        grid=(1,),
        room=4,
        scratch=[pltpu.VMEM((n_across * BLK, LANES), F32)],
    )(
        jnp.stack([my_col, my_row]).astype(jnp.int32),
        block_mask.reshape(-1),
        adjacency.reshape(MB, -1, LANES),
    )
    tile = [out[m * n_pieces : (m + 1) * n_pieces] for m in range(MB)]
    leave = out[MB * n_pieces :]
    return tile, [leave[m * (n_pieces - 1) : (m + 1) * (n_pieces - 1)] for m in range(MB)]


def layer_one_kernel(n_z, *refs):
    tile_refs, feat_refs, (near_ref, far_ref) = refs[: MB * n_z], refs[MB * n_z : -2], refs[-2:]
    ns = near_ref.shape[2]
    for m in range(MB):
        feats = jnp.concatenate([f[m] for f in feat_refs], 0)
        for i in range(n_z):
            out = mm(tile_refs[m * n_z + i][...], feats)
            near_ref[i, m] = out[:ns]
            far_ref[i, m] = out[ns:]


def layer_one(tile, feats):
    n_z = len(tile[0])
    half, across = tile[0][0].shape
    out = shaped((n_z, MB, half // 2, LANES))
    return call(
        lambda *refs: layer_one_kernel(n_z, *refs),
        "layer_one",
        (out, out),
        [pl.BlockSpec((half, across), lambda i: (0, 0))] * (MB * n_z) + [IN_VMEM] * len(feats),
        (IN_VMEM, IN_VMEM),
        grid=(1,),
    )(*tile[0], *tile[1], *feats)


def twice_gelu(z):
    return z + z * jnp.tanh(z * (GELU_ONE + GELU_THREE * (z * z)))


def twice_gelu_both(z):
    square = z * z
    t = jnp.tanh(z * (GELU_ONE + GELU_THREE * square))
    slope = z * (GELU_ONE + (3 * GELU_THREE) * square)
    return z + z * t, (1.0 + t) * (1.0 + (1.0 - t) * slope)


def forward_kernel(n_z, n_rows, m, *refs):
    g_refs, strip_refs = refs[:n_rows], refs[n_rows : n_rows + n_z]
    w_ref, near_ref, far_ref, slope_ref = refs[n_rows + n_z :]
    half = near_ref.shape[0]
    total = None
    for i in range(n_z):
        g = jnp.concatenate([g_ref[i, m] for g_ref in g_refs], 0)
        h, slope = twice_gelu_both(mm(g, w_ref[...]))
        n = g.shape[0]
        slope_ref[i * n : (i + 1) * n] = slope.astype(BF16)
        part = mm(strip_refs[i][...], h.astype(BF16))
        total = part if total is None else total + part
    near_ref[...] = 0.5 * total[:half]
    far_ref[...] = (0.5 * total[half:]).astype(BF16)


def forward_two(g_all, w_pad, strip, m, wide=256):
    n_rows, n_z = len(g_all), len(strip)
    rows, across = strip[0].shape
    span = w_pad.shape[1]
    n = n_z * across
    return call(
        lambda *refs: forward_kernel(n_z, n_rows, m, *refs),
        "forward_two",
        (shaped((rows // 2, span)), shaped((rows // 2, span), BF16), shaped((n, span), BF16)),
        [pl.BlockSpec(g_all[0].shape, lambda f: (0, 0, 0, 0))] * n_rows
        + [pl.BlockSpec((rows, across), lambda f: (0, 0))] * n_z
        + [pl.BlockSpec((LANES, wide), lambda f: (0, f))],
        (pl.BlockSpec((rows // 2, wide), lambda f: (0, f)),) * 2 + (pl.BlockSpec((n, wide), lambda f: (0, f)),),
        grid=(span // wide,),
        room=2 + 8 * across // 1024,
    )(*g_all, *strip, w_pad)


def one_hot(here, there):
    return jnp.where(here == there, 1.0, 0.0).astype(BF16)


def spread_kernel(n_m, n_blocks, *refs):
    near_parts, far_parts = refs[:n_m], refs[n_m : 2 * n_m]
    g_one_ref, w_ref, diag_ref, which_ref, gn_ref, gf_ref, g_ref = refs[2 * n_m :]
    ns = near_parts[0].shape[0]

    @pl.when(pl.program_id(0) == 0)
    def _():
        step = 256
        for at in range(0, HID, step):
            cut = slice(at, at + step)
            h = (0.5 * twice_gelu(mm(g_one_ref[...], w_ref[:, cut]))).astype(BF16)
            for m in range(n_m):
                g_ref[m * ns : (m + 1) * ns, cut] = (
                    near_parts[m][:, cut]
                    + far_parts[m][:, cut].astype(F32)
                    + LAMBDA * diag_ref[:, m : m + 1] * h[m * ns : (m + 1) * ns].astype(F32)
                ).astype(BF16)

    which = which_ref[...]
    hot = one_hot(lax.broadcasted_iota(jnp.int32, (HID, which.shape[1]), 0), which)
    out = mm(g_ref[...], hot).astype(BF16)

    @pl.when(pl.program_id(0) < n_blocks)
    def _():
        gn_ref[...] = out

    @pl.when(pl.program_id(0) >= n_blocks)
    def _():
        gf_ref[...] = out


def block_width(n):
    return 384 if n % 384 == 0 else LANES


def spread_two(near_parts, far_parts, g_one, w_pad, diag, which):
    ns = near_parts[0].shape[0]
    n_m = len(near_parts)
    n_near = which.shape[1] // 2
    rows = n_m * ns
    wide = block_width(n_near)
    n = n_near // wide
    whole = lambda k: (0, 0)
    out = shaped((rows, n_near), BF16)
    return call(
        lambda *refs: spread_kernel(n_m, n, *refs),
        "spread_two",
        (out, out),
        [pl.BlockSpec((ns, HID), whole)] * (2 * n_m)
        + [
            pl.BlockSpec((rows, LANES), whole),
            pl.BlockSpec((LANES, HID), whole),
            pl.BlockSpec((ns, n_m), whole),
            pl.BlockSpec((1, wide), lambda k: (0, k)),
        ],
        (
            pl.BlockSpec((rows, wide), lambda k: (0, jnp.minimum(k, n - 1))),
            pl.BlockSpec((rows, wide), lambda k: (0, jnp.maximum(k - n, 0))),
        ),
        grid=(2 * n,),
        scratch=[pltpu.VMEM((rows, HID), BF16)],
        room=8,
    )(*near_parts, *far_parts, g_one, w_pad, diag, which)


def layer_two_kernel(gn_ref, gf_ref, wn_ref, wf_ref, b_ref, w3_ref, here_ref, z_ref, h_ref, q_ref, sum_ref):
    ns = sum_ref.shape[0]

    @pl.when(pl.program_id(0) == 0)
    def _():
        sum_ref[...] = jnp.zeros_like(sum_ref)

    z = mm(gn_ref[...], wn_ref[...]) + mm(gf_ref[...], wf_ref[...]) + b_ref[...]
    z_ref[...] = z
    h = (0.5 * twice_gelu(z)).astype(BF16)
    h_ref[...] = h
    q = mm(h, w3_ref[...])
    lane = lane_of(sum_ref.shape)
    sum_ref[...] += jnp.where(lane < LANES // 2, q[:ns], q[ns:])

    @pl.when(pl.program_id(0) == pl.num_programs(0) - 1)
    def _():
        q_ref[...] = jnp.where(lane == LANES - 1, here_ref[...], sum_ref[...]).astype(BF16)


def layer_two(g_near, g_far, near, far, b_second, w3, here, wide=512):
    rows, n_near = g_near.shape
    ns = rows // MB
    whole = lambda f: (0, 0)
    return call(
        layer_two_kernel,
        "layer_two",
        (shaped((rows, HID)), shaped((rows, HID), BF16), shaped((ns, LANES), BF16)),
        [
            pl.BlockSpec((rows, n_near), whole),
            pl.BlockSpec((rows, n_near), whole),
            pl.BlockSpec((n_near, wide), lambda f: (0, f)),
            pl.BlockSpec((n_near, wide), lambda f: (0, f)),
            pl.BlockSpec((1, wide), lambda f: (0, f)),
            pl.BlockSpec((wide, LANES), lambda f: (f, 0)),
            pl.BlockSpec((1, LANES), whole),
        ],
        (
            pl.BlockSpec((rows, wide), lambda f: (0, f)),
            pl.BlockSpec((rows, wide), lambda f: (0, f)),
            pl.BlockSpec((ns, LANES), whole),
        ),
        grid=(HID // wide,),
        scratch=[pltpu.VMEM((ns, LANES), F32)],
    )(g_near, g_far, near, far, b_second, w3, here)


def logits_kernel(n_z, *refs):
    strips, q_refs, (near_ref, far_ref) = refs[: MB * n_z], refs[MB * n_z : -2], refs[-2:]
    half = near_ref.shape[0]
    lane = lane_of((2 * half, LANES))
    sums = [None] * MB
    for i in range(n_z):
        all_q = jnp.concatenate([q[i] for q in q_refs], 0)
        for m in range(MB):
            part = mm(strips[m * n_z + i][...], all_q)
            sums[m] = part if sums[m] is None else sums[m] + part
    out = jnp.where(lane < LANES // 2, sums[0], sums[1])
    count = sum(jnp.sum(q[:, 0:1, :].astype(F32), axis=0) for q in q_refs)
    out = jnp.where(lane == LANES - 1, count, out)
    near_ref[...] = out[:half]
    far_ref[...] = out[half:]


def logits_parts(strips, q_rows):
    n_z = len(strips[0])
    rows, across = strips[0][0].shape
    out = shaped((rows // 2, LANES))
    return call(
        lambda *refs: logits_kernel(n_z, *refs),
        "logits_parts",
        (out, out),
        [pl.BlockSpec((rows, across), lambda i: (0, 0))] * (MB * n_z) + [IN_VMEM] * len(q_rows),
        (IN_VMEM, IN_VMEM),
        grid=(1,),
    )(*strips[0], *strips[1], *q_rows)


def loss_kernel(near_ref, got_ref, q_ref, diag_ref, bias_ref, labels_ref, counted_ref, ds_ref, row_ref):
    total = near_ref[...] + got_ref[...]
    node_total = total[0:1, LANES - 1 :]
    lane = lane_of(total.shape)
    low = lane < LANES // 2
    at = jnp.where(low, lane, lane - LANES // 2)
    real = at < NCLS
    pick = lambda ref: jnp.where(low, ref[:, 0:1], ref[:, 1:2])
    logits = total + LAMBDA * pick(diag_ref) * q_ref[...].astype(F32) + bias_ref[...]
    least = jnp.float32(-3.0e38)
    hits = jnp.logical_and(real, at == pick(labels_ref))
    counted = pick(counted_ref)
    parts = []
    for side in (jnp.logical_and(real, low), jnp.logical_and(real, jnp.logical_not(low))):
        top = jnp.max(jnp.where(side, logits, least), axis=1, keepdims=True)
        powers = jnp.where(side, jnp.exp(jnp.where(side, logits - top, 0.0)), 0.0)
        parts.append((top, jnp.sum(powers, axis=1, keepdims=True)))
    log_total = jnp.where(
        low, parts[0][0] + jnp.log(parts[0][1]), parts[1][0] + jnp.log(parts[1][1])
    )
    loss = jnp.where(hits, counted * (log_total - logits), 0.0)
    soft = jnp.exp(jnp.where(real, logits - log_total, 0.0))
    d_logits = jnp.where(real, counted * (soft - hits.astype(F32)) / node_total, 0.0)
    ds_ref[...] = d_logits.astype(BF16)
    row_ref[0:1] = jnp.sum(d_logits, axis=0, keepdims=True)
    row_ref[1:2] = jnp.broadcast_to(jnp.sum(jnp.sum(loss, axis=0, keepdims=True), axis=1, keepdims=True), (1, LANES))
    row_ref[2:3] = jnp.broadcast_to(node_total, (1, LANES))
    row_ref[3:8] = jnp.zeros((5, LANES), F32)


def d_q_kernel(n_z, *refs):
    tile_refs, s_refs, out_refs = refs[: MB * n_z], refs[MB * n_z : (MB + 1) * n_z], refs[(MB + 1) * n_z :]
    side = out_refs[0].shape[0]
    lane = lane_of((side * len(out_refs), LANES))
    sums = [None] * MB
    for i in range(n_z):
        all_s = jnp.concatenate([s_refs[i][core] for core in (0, 1)], 0)
        for m in range(MB):
            part = mm_t(tile_refs[m * n_z + i][...], all_s)
            sums[m] = part if sums[m] is None else sums[m] + part
    out = jnp.where(lane < LANES // 2, sums[0], sums[1])
    for k, out_ref in enumerate(out_refs):
        out_ref[...] = out[k * side : (k + 1) * side]


def d_q_parts(tile, pieces):
    n_z = len(pieces)
    rows, across = tile[0][0].shape
    n = across // BLK
    return call(
        lambda *refs: d_q_kernel(n_z, *refs),
        "d_q_parts",
        (shaped((BLK, LANES)),) * n,
        [pl.BlockSpec((rows, across), lambda i: (0, 0))] * (MB * n_z) + [IN_VMEM] * n_z,
        (IN_VMEM,) * n,
        grid=(1,),
    )(*tile[0], *tile[1], *pieces)


def d_two_kernel(n_q, *refs):
    q_refs = refs[:n_q]
    ds_ref, diag_ref, z_ref, h_ref, w3_ref, g_ref, dz_ref, db_ref, dw3_ref, far_ref = refs[n_q:]
    ns = ds_ref.shape[0]
    d_q = q_refs[0][...]
    for q in q_refs[1:]:
        d_q = d_q + q[...]
    low = lane_of(d_q.shape) < LANES // 2
    d_q = d_q + LAMBDA * jnp.where(low, diag_ref[:, 0:1], diag_ref[:, 1:2]) * ds_ref[...].astype(F32)
    d_q = jnp.concatenate([jnp.where(low, d_q, 0.0), jnp.where(low, 0.0, d_q)], 0).astype(BF16)
    d_z = mm_nt(d_q, w3_ref[...]) * (0.5 * twice_gelu_both(z_ref[...])[1])
    db_ref[...] = jnp.sum(d_z.reshape(-1, 8, d_z.shape[1]), axis=0)
    d_zb = d_z.astype(BF16)
    dz_ref[...] = d_zb
    dw3_ref[...] = mm_t(h_ref[...], d_q)
    far_ref[...] = mm_t(g_ref[...], d_zb).astype(BF16)


def d_two(d_q, d_s, diag, z_two, h_two, w3, g_far, lo, hi, wide=256):
    rows = z_two.shape[0]
    ns, n_far = d_s.shape[0], g_far.shape[1]
    whole = lambda f: (0, 0)
    start = lo // wide
    small = pl.BlockSpec((ns, LANES), whole)
    column = pl.BlockSpec((rows, wide), lambda f: (0, start + f))
    span = hi - lo
    return call(
        lambda *refs: d_two_kernel(len(d_q), *refs),
        "d_two",
        (
            shaped((rows, span), BF16),
            shaped((8, span)),
            shaped((span, LANES)),
            shaped((n_far, span), BF16),
        ),
        [small] * (len(d_q) + 1)
        + [
            pl.BlockSpec((ns, MB), whole),
            column,
            column,
            pl.BlockSpec((wide, LANES), lambda f: (start + f, 0)),
            pl.BlockSpec((rows, n_far), whole),
        ],
        (
            pl.BlockSpec((rows, wide), lambda f: (0, f)),
            pl.BlockSpec((8, wide), lambda f: (0, f)),
            pl.BlockSpec((wide, LANES), lambda f: (f, 0)),
            pl.BlockSpec((n_far, wide), lambda f: (0, f)),
        ),
        grid=(span // wide,),
        room=4,
    )(*d_q, d_s, diag, z_two, h_two, w3, g_far)


def near_kernel(keep, send, rows, g_ref, dz_ref, got_ref, keep_ref, send_ref):
    total = mm_t(g_ref[...], dz_ref[...]) + got_ref[...].astype(F32)
    for out_ref, picks in ((keep_ref, keep), (send_ref, send)):
        for i, j in enumerate(picks):
            out_ref[i * rows : (i + 1) * rows] = total[j * rows : (j + 1) * rows].astype(out_ref.dtype)


def near_part(g_near, d_zb, got, n_rows, bit, wide=256):
    n_near, span = got.shape
    rows = n_near // n_rows
    keep = [j for j in range(n_rows) if not j & bit]
    send = [j | bit for j in keep]
    column = lambda n: pl.BlockSpec((n, wide), lambda f: (0, f))
    return call(
        lambda *refs: near_kernel(keep, send, rows, *refs),
        "near_part",
        (shaped((n_near // 2, span)), shaped((n_near // 2, span), BF16)),
        [pl.BlockSpec(g_near.shape, lambda f: (0, 0)), column(g_near.shape[0]), column(n_near)],
        (column(n_near // 2), column(n_near // 2)),
        grid=(span // wide,),
    )(g_near, d_zb, got)


def backward_kernel(n_z, n_rows, *refs):
    g_refs, strip_refs = refs[:n_rows], refs[n_rows : n_rows + MB * n_z]
    slope_refs, (dgn_ref, dgf_ref, diag_ref, dw_ref) = refs[-4 - MB : -4], refs[-4:]
    own = dgn_ref.shape[1]
    total = None
    for m in range(MB):
        d_g = jnp.concatenate([dgn_ref[m], dgf_ref[m]], 0)
        for i in range(n_z):
            d_h = mm_t(strip_refs[m * n_z + i][...], d_g)
            n = d_h.shape[0]
            if i == 0:
                more = LAMBDA * diag_ref[:, m : m + 1] * dgn_ref[m].astype(F32)
                d_h = jnp.concatenate([d_h[:own] + more, d_h[own:]], 0)
            g = jnp.concatenate([g_ref[i, m] for g_ref in g_refs], 0)
            d_z = d_h * slope_refs[m][i * n : (i + 1) * n].astype(F32)
            part = mm_t(g, d_z.astype(BF16))
            total = part if total is None else total + part
    dw_ref[...] = (0.5 * total).astype(BF16)


def backward_one(g_all, strips, slopes, d_g_near, d_g_far, diag, lo, hi, wide=256):
    n_rows, n_z = len(g_all), len(strips[0])
    rows, across = strips[0][0].shape
    span = hi - lo
    start = lo // wide
    column = pl.BlockSpec((MB, rows // 2, wide), lambda f: (0, 0, start + f))
    return call(
        lambda *refs: backward_kernel(n_z, n_rows, *refs),
        "backward_one",
        shaped((LANES, span), BF16),
        [pl.BlockSpec(g_all[0].shape, lambda f: (0, 0, 0, 0))] * n_rows
        + [pl.BlockSpec((rows, across), lambda f: (0, 0))] * (MB * n_z)
        + [pl.BlockSpec((n_z * across, wide), lambda f: (0, start + f))] * MB
        + [column, column, pl.BlockSpec((rows // 2, MB), lambda f: (0, 0))],
        pl.BlockSpec((LANES, wide), lambda f: (0, f)),
        grid=(span // wide,),
        room=2 + 8 * across // 1024,
    )(*g_all, *strips[0], *strips[1], *slopes, d_g_near, d_g_far, diag)


def d_g_kernel(n_blocks, cuts, *refs):
    dz_refs, (which_ref, wn_ref, wf_ref, out_ref, sum_ref) = refs[: len(cuts)], refs[len(cuts) :]
    step = pl.program_id(0)

    @pl.when(step == 0)
    def _():
        sum_ref[...] = jnp.zeros_like(sum_ref)

    def add(w_ref):
        part = sum(mm_nt(dz[...], w_ref[:, lo:hi]) for dz, (lo, hi) in zip(dz_refs, cuts)).astype(BF16)
        which = which_ref[...]
        hot = one_hot(lax.broadcasted_iota(jnp.int32, (which.shape[0], HID), 1), which)
        sum_ref[...] += mm(part, hot)

    @pl.when(step < n_blocks)
    def _():
        add(wn_ref)

    @pl.when(step >= n_blocks)
    def _():
        add(wf_ref)

    @pl.when(step == pl.num_programs(0) - 1)
    def _():
        out_ref[...] = sum_ref[...].astype(BF16)


def d_g_two(d_zb, cuts, which, near, far):
    rows, n_near = d_zb[0].shape[0], near.shape[0]
    wide = block_width(n_near)
    n = n_near // wide
    return call(
        lambda *refs: d_g_kernel(n, cuts, *refs),
        "d_g_two",
        shaped((rows, HID), BF16),
        [pl.BlockSpec(d.shape, lambda k: (0, 0)) for d in d_zb]
        + [
            pl.BlockSpec((wide, 1), lambda k: (k, 0)),
            pl.BlockSpec((wide, HID), lambda k: (jnp.minimum(k, n - 1), 0)),
            pl.BlockSpec((wide, HID), lambda k: (jnp.maximum(k - n, 0), 0)),
        ],
        pl.BlockSpec((rows, HID), lambda k: (0, 0)),
        grid=(2 * n,),
        scratch=[pltpu.VMEM((rows, HID), F32)],
        room=8,
    )(*d_zb, which, near, far)


def thirds_kernel(row_ref, out_ref):
    rest = row_ref[...]
    out_ref[...] = jnp.zeros_like(out_ref)
    for i in range(3):
        low = rest.astype(BF16)
        out_ref[i : i + 1] = low
        rest = rest - low.astype(F32)


def thirds(row):
    return call(thirds_kernel, "thirds", shaped((16, LANES), BF16), [IN_VMEM], IN_VMEM)(row)


def join_kernel(sizes, *refs):
    pieces, out_ref, sems = refs[: len(sizes)], refs[len(sizes)], refs[-1]
    at, copies = 0, []
    for i, (piece, size) in enumerate(zip(pieces, sizes)):
        copies.append(pltpu.make_async_copy(piece, out_ref.at[pl.ds(at, size)], sems.at[i]))
        copies[-1].start()
        at += size
    for copy in copies:
        copy.wait()


def join(pieces):
    sizes = [p.shape[0] for p in pieces]
    return call(
        lambda *refs: join_kernel(sizes, *refs),
        "join",
        shaped((sum(sizes),) + pieces[0].shape[1:], pieces[0].dtype),
        [ANYWHERE] * len(pieces),
        IN_VMEM,
        room=2,
        scratch=[pltpu.SemaphoreType.DMA((len(pieces),))],
    )(*pieces)


def per_device(features, adjacency, block_mask, diagonal, labels, train_mask, params, first_moment, second_moment):
    n_rows, n_cols = lax.axis_size("rows"), lax.axis_size("cols")
    n_z = n_cols // 2
    n_dev = n_rows * n_cols
    my_row, my_col = lax.axis_index("rows"), lax.axis_index("cols")
    me = my_row * n_cols + my_col
    ns = features.shape[1]
    z_bits, row_bits = bits_of(n_z), bits_of(n_rows)
    turned = row_bits[1:] + row_bits[:1]
    single = z_bits[::-1]
    several = [j for j in range(1, n_z) if j not in single]
    z_order = [0] + single + several

    def over_z(x):
        return [x] + [swap(x, "cols", 2 * j) for j in z_order[1:]]

    def over_rows(x):
        return [x] + [swap(x, "rows", j) for j in range(1, n_rows)]

    n_own = params.shape[0] // LANES
    slot = -(-((n_own + UNIT - 2) // UNIT + 1) // 8) * 8
    shift = lax.rem(n_own * me, UNIT)
    own = lax.dynamic_update_slice(
        jnp.zeros((slot * UNIT, LANES), BF16), params.reshape(n_own, LANES).astype(BF16), (shift, 0)
    ).reshape(1, slot, HID)
    wide_feats = jnp.pad(features, ((0, 0), (0, 0), (0, LANES - FIN)))
    ones = lax.broadcasted_iota(jnp.int32, (1, 1, LANES), 2) == FIN
    feats = over_rows(wide_feats)
    tile, leave = masked_tile(
        adjacency.reshape(MB, -1, n_rows, LANES), block_mask, [2 * j + core for j in z_order for core in (0, 1)], my_col, my_row
    )

    part_near, part_far = layer_one(tile, feats)
    own = after(own, part_far)
    by_z = {0: own}
    for j in single:
        by_z[j] = swap(own, "cols", 2 * j)
    partial = part_near + swap(part_far, "cols", 1)
    g_one = partial[0] + LAMBDA * diagonal[:, :, None] * wide_feats.astype(F32)
    low = partial.astype(BF16)
    for i, j in enumerate(z_order[1:], 1):
        g_one = g_one + swap(low[i], "cols", 2 * j).astype(F32)
    g_one = jnp.where(ones, 1.0, g_one).astype(BF16)

    def units_of(core):
        owner = (my_row ^ jnp.arange(n_rows))[:, None] * n_cols + (
            my_col ^ (2 * jnp.array(z_order) + core)
        )[None, :]
        start = (n_own * owner) // UNIT
        return (start[:, :, None] + jnp.arange(slot)[None, None, :]).reshape(-1)

    near_units = units_of(0)
    units = jnp.concatenate([near_units, units_of(1)])
    which = units - FIN

    middle = after(join([by_z[j] for j in single]), g_one)
    for j in several:
        bit = j & -j
        by_z[j] = swap(by_z[j - bit], "cols", 2 * bit)
    last = by_z[several[0]] if len(several) == 1 else join([by_z[j] for j in several])
    g_z = over_z(g_one)
    last = after(last, *g_z[1:])
    groups = [own, middle, last]
    g_all = over_rows(jnp.stack(g_z))
    strips = [[tile[m][0]] for m in range(MB)]
    for i, j in enumerate(z_order[1:]):
        strips[0].append(swap(after(leave[0][i], *g_all[1:]), "cols", 2 * j))
    passed = {0: groups}
    for j in range(1, n_rows):
        lowest = j & -j
        highest = 1 << (j.bit_length() - 1)
        hop = [passed[j - bit][i] for i, bit in enumerate((highest, lowest, highest))]
        if lowest != highest:
            hop = [after(h, *g_all[1:]) for h in hop]
        passed[j] = [swap(h, "rows", bit) for h, bit in zip(hop, (highest, lowest, highest))]
    for m in range(1, MB):
        for i, j in enumerate(z_order[1:]):
            strips[m].append(swap(after(leave[m][i], *strips[m - 1][1:]), "cols", 2 * j))
    passed[0][0] = after(passed[0][0], *strips[0][1:])
    near = join([g.reshape(-1, HID) for j in range(n_rows) for g in passed[j]])
    far = swap(near, "cols", 1)
    n_near = near.shape[0]

    per_small = -(-(FIN + NCLS + 3) // n_dev)
    n_small = per_small * n_dev
    small_unit = jnp.arange(n_small)
    small_unit = jnp.where(small_unit < FIN, small_unit, small_unit + HID)
    pick = (small_unit[:, None] == near_units[None, :]).astype(BF16)
    small = mm(pick, near).astype(BF16)
    small = small + swap(small, "cols", 1)
    w_pad = jnp.concatenate(
        [small[:FIN], small[FIN + NCLS : FIN + NCLS + 1], jnp.zeros((LANES - FIN - 1, HID), BF16)], 0
    )
    w_third = small[FIN : FIN + NCLS].reshape(HID, NCLS)
    gap = jnp.zeros((HID, LANES // 2 - NCLS), BF16)
    w_third = jnp.concatenate([w_third, gap, w_third, gap], 1)
    b_second = small[FIN + NCLS + 1].astype(F32)[None]
    b_third = small[FIN + NCLS + 2].astype(F32)[: LANES // 2]
    b_third = jnp.concatenate([b_third, b_third])[None]

    near_parts, far_parts, slopes = [], [], []
    for m in range(MB):
        if m == MB - 1:
            w_pad = after(w_pad, w_third)
        part_near, part_far, slope = forward_two(g_all, w_pad, strips[m], m)
        slopes.append(slope)
        near_parts.append(part_near)
        far_parts.append(swap(part_far, "cols", 1))

    diag = diagonal.T
    counted = train_mask.T.astype(F32)
    here = jnp.broadcast_to(jnp.sum(counted), (1, LANES))
    g_near, g_far = spread_two(
        near_parts, far_parts, g_one.reshape(MB * ns, LANES), w_pad, diag, which[None]
    )
    z_two, h_two, q = layer_two(g_near, g_far, near, far, b_second, w_third, here)

    part_near, part_far = logits_parts(strips, over_rows(jnp.stack(over_z(q))))
    d_s, sums = call(
        loss_kernel,
        "loss",
        (shaped((ns, LANES), BF16), shaped((8, LANES))),
        [IN_VMEM] * 7,
        (IN_VMEM, IN_VMEM),
    )(part_near, swap(part_far, "cols", 1), q, diag, b_third, labels.T, counted)
    d_bias_three = sums[0, :NCLS] + sums[0, LANES // 2 : LANES // 2 + NCLS]
    loss, node_total = sums[1, 0], sums[2, 0]

    d_q = d_q_parts(tile, over_z(jnp.stack([d_s, swap(d_s, "cols", 1)])))
    d_q = [d_q[0]] + [swap(d_q[j], "rows", j) for j in range(1, n_rows)]

    def split(item, axis, bit):
        dim = 0 if axis == "rows" else 1
        kept, send, item["orders"][axis] = split_bit(item["part"], dim, item["orders"][axis], bit)
        item["kept"], item["send"] = kept, send.astype(BF16)
        item["to"] = (axis, bit * (dim + 1))

    half = HID // 2
    work = []
    for k, bits in enumerate((row_bits, turned)):
        lo, hi = k * half, (k + 1) * half
        wait = d_s if k == 0 else after(d_s, work[0]["dz"])
        d_zb, d_b, d_w3, d_far = d_two(d_q, wait, diag, z_two, h_two, w_third, g_far, lo, hi)
        item = {"bits": bits, "dz": d_zb, "db": d_b, "dw3": d_w3}
        item["got"] = swap(d_far, "cols", 1)
        item["orders"] = {"rows": [j for j in range(n_rows) if not j & bits[0]], "cols": z_order}
        item["to"] = ("rows", bits[0])
        work.append(item)
    for item in work:
        kept, send = near_part(g_near, item["dz"], item["got"], n_rows, item["bits"][0])
        item["kept"], item["send"] = (x.reshape(n_rows // 2, n_z, slot, half) for x in (kept, send))
    d_zb = [item["dz"] for item in work]
    d_bias_two = jnp.concatenate([jnp.sum(item["db"], axis=0) for item in work])
    d_w_three = jnp.concatenate([item["dw3"] for item in work], 0)
    d_w_three = d_w_three[:, :NCLS] + d_w_three[:, LANES // 2 : LANES // 2 + NCLS]

    n_cuts = 3
    cuts = [0, 3 * (HID // 8), 6 * (HID // 8), HID]
    d_zb[0] = after(d_zb[0], *[item["send"] for item in work])
    d_g_near = d_g_two(d_zb, [(0, half), (half, HID)], which[:, None], near, far).reshape(MB, ns, HID)
    d_g_far = swap(d_g_near, "cols", 1)
    d_first = []

    def another_cut():
        i = len(d_first)
        if i < n_cuts:
            d_first.append(
                backward_one(g_all, strips, slopes, d_g_near, d_g_far, diag, cuts[i], cuts[i + 1])
            )

    for i in range(len(row_bits)):
        for item in work:
            item["part"] = item["kept"] + swap(item["send"], *item["to"]).astype(F32)
            if i + 1 < len(row_bits):
                split(item, "rows", item["bits"][i + 1])
        if i + 1 < len(row_bits):
            d_g_near = after(d_g_near, *[item["send"] for item in work])
            another_cut()
    item = {"orders": {"cols": z_order}, "part": jnp.concatenate([item["part"] for item in work], 3)}
    for bit in z_bits:
        split(item, "cols", bit)
        d_g_near = after(d_g_near, item["send"])
        another_cut()
        item["part"] = item["kept"] + swap(item["send"], *item["to"]).astype(F32)
    own_grad = item["part"][0, 0]
    d_first = jnp.concatenate(d_first, 1)
    d_w_one, d_bias_one = d_first[:FIN], d_first[FIN].astype(F32)

    d_small = jnp.concatenate(
        [
            d_w_one.astype(BF16),
            d_w_three.astype(BF16).reshape(NCLS, HID),
            jnp.stack([d_bias_one, d_bias_two, jnp.pad(d_bias_three, (0, HID - NCLS))]).astype(BF16),
            jnp.zeros((n_small - FIN - NCLS - 3, HID), BF16),
        ],
        0,
    )
    d_small = after(d_small.reshape(n_dev, per_small * UNIT, LANES), own_grad)
    got = lax.all_to_all(d_small, BOTH, split_axis=0, concat_axis=0, tiled=True)
    got = jnp.sum(got.astype(F32), axis=0)
    low = got.astype(BF16)

    own_flat = lax.dynamic_slice(own_grad.reshape(slot * UNIT, LANES), (shift, 0), (n_own, LANES))
    squares = jnp.sum(own_flat * own_flat) + jnp.sum(low.astype(F32) ** 2)
    row = jnp.concatenate([squares[None], loss[None], d_bias_three, jnp.zeros((LANES - NCLS - 2,), F32)])
    sent = jnp.concatenate([low, thirds(row[None])], 0)
    sent = jnp.broadcast_to(sent[None], (n_dev,) + sent.shape)
    got = lax.all_to_all(sent, BOTH, split_axis=0, concat_axis=0, tiled=True)
    d_small = got[:, : per_small * UNIT].reshape(n_small, HID)
    row = jnp.sum(got[:, per_small * UNIT : per_small * UNIT + 3].astype(F32), axis=(0, 1))
    squares, loss_sum, class_sum = row[0], row[1], row[2 : 2 + NCLS]

    mine = (n_own * me) // UNIT + jnp.arange(slot)
    place = (mine[:, None] == small_unit[None, :]).astype(BF16)
    small_flat = lax.dynamic_slice(
        mm(place, d_small).reshape(slot * UNIT, LANES), (shift, 0), (n_own, LANES)
    )
    reduced = (own_flat + small_flat).reshape(-1)

    grad_norm = jnp.sqrt(squares)
    clip_scale = jnp.minimum(1.0, CLIP_NORM / (grad_norm + 1e-06))
    clipped = reduced * clip_scale
    class_bias_grad = class_sum * clip_scale
    new_first = BETA_ONE * first_moment + (1.0 - BETA_ONE) * clipped
    new_second = BETA_TWO * second_moment + (1.0 - BETA_TWO) * clipped * clipped
    correct_one = 1.0 - BETA_ONE**STEP
    correct_two = 1.0 - BETA_TWO**STEP
    step_size = new_first / correct_one / (jnp.sqrt(new_second / correct_two) + EPSILON)
    new_params = params - LEARN_RATE * (step_size + WEIGHT_DECAY * params)
    return (new_params, new_first, new_second, grad_norm, loss_sum, node_total, class_bias_grad)


def solution(mesh):
    in_specs = (
        P(None, ("rows", "cols"), None),
        P(None, "rows", None, "cols", None),
        P(None, "rows", None, "cols", None),
        P(None, ("rows", "cols")),
        P(None, ("rows", "cols")),
        P(None, ("rows", "cols")),
        P(("rows", "cols")),
        P(("rows", "cols")),
        P(("rows", "cols")),
    )
    out_specs = (P(("rows", "cols")), P(("rows", "cols")), P(("rows", "cols")), P(), P(), P(), P())
    return jax.shard_map(
        per_device, mesh=mesh, in_specs=in_specs, out_specs=out_specs, check_vma=False
    )
```

```python
import math

import jax
import jax.numpy as jnp
from jax import lax
from jax.experimental import pallas as pl
from jax.experimental.pallas import tpu as pltpu
from jax.sharding import PartitionSpec as P

FIN = 100
HID = 2048
NCLS = 47
BLK = 128
MB = 2
STEP = 10
PARAMS = FIN * HID + HID * HID + HID * NCLS + 2 * HID + NCLS

LAMBDA = 1.0
CLIP_NORM = 0.01
BETA_ONE = 0.9
BETA_TWO = 0.95
EPSILON = 1e-08
WEIGHT_DECAY = 0.1
LEARN_RATE = 0.02

LANES = 128
UNIT = HID // LANES
BOTH = ("rows", "cols")
GELU_ONE = 0.7978845608028654
GELU_THREE = GELU_ONE * 0.044715
F32 = jnp.float32
FAR_BYTES = 1 << 17
BF16 = jnp.bfloat16


def swap(x, axis, bit):
    size = lax.axis_size(axis)
    return lax.ppermute(x, axis, [(i, i ^ bit) for i in range(size)])


def bits_of(size):
    return [1 << i for i in range(size.bit_length() - 1)]


def mm(left, right):
    return jnp.dot(left, right, preferred_element_type=F32)


def mm_t(left, right):
    return lax.dot_general(left, right, (((0,), (0,)), ((), ())), preferred_element_type=F32)


def mm_nt(left, right):
    return lax.dot_general(left, right, (((1,), (1,)), ((), ())), preferred_element_type=F32)


def take(x, axis, picks):
    return jnp.concatenate([lax.slice_in_dim(x, p, p + 1, axis=axis) for p in picks], axis)


def split_bit(x, axis, order, bit):
    keep = [j for j in order if not j & bit]
    run = next(i for i, j in enumerate(order) if j & bit)
    if any(bool(j & bit) != bool(i // run % 2) or j & ~bit != order[i - i // run % 2 * run] & ~bit for i, j in enumerate(order)):
        at = {j: i for i, j in enumerate(order)}
        return take(x, axis, [at[j] for j in keep]), take(x, axis, [at[j | bit] for j in keep]), keep
    shape = x.shape[:axis] + (len(order) // (2 * run), 2, run) + x.shape[axis + 1 :]
    kept_shape = x.shape[:axis] + (len(keep),) + x.shape[axis + 1 :]
    x = x.reshape(shape)
    pair = [lax.index_in_dim(x, i, axis + 1, keepdims=False).reshape(kept_shape) for i in (0, 1)]
    return pair[0], pair[1], keep


ANYWHERE = pl.BlockSpec(memory_space=pl.ANY)
IN_VMEM = pl.BlockSpec(memory_space=pltpu.VMEM)
IN_SMEM = pl.BlockSpec(memory_space=pltpu.SMEM)


def tip(x):
    while x.ndim > 2:
        x = x[0]
    return x[:8, :128].astype(F32)


def after_kernel(*refs):
    pass


def after(x, *earlier):
    earlier = [tip(e) for e in earlier]
    return pl.pallas_call(
        after_kernel,
        out_shape=jax.ShapeDtypeStruct(x.shape, x.dtype),
        in_specs=[ANYWHERE] * (1 + len(earlier)),
        out_specs=ANYWHERE,
        input_output_aliases={0: 0},
        name="after",
    )(x, *earlier)


def padded_bytes(shape, dtype):
    *front, rows, lanes = (1, 1, *shape)
    size = -(-rows // 16) * 16 * -(-lanes // LANES) * LANES * jnp.dtype(dtype).itemsize
    for n in front:
        size *= n
    return size


def call(kernel, name, out_shape, in_specs, out_specs, grid=None, room=4, scratch=()):
    more = {} if grid is None else {"grid": grid}

    def run(*args):
        outs = out_shape if isinstance(out_shape, tuple) else (out_shape,)
        specs = (*in_specs, *(out_specs if isinstance(out_specs, tuple) else (out_specs,)))
        total = room << 20
        for spec, x in zip(specs, (*args, *outs)):
            if spec.block_shape is not None:
                total += 2 * padded_bytes(spec.block_shape, x.dtype)
            elif spec.memory_space == pltpu.VMEM:
                total += padded_bytes(x.shape, x.dtype)
        large = lambda x: math.prod(x.shape) * x.dtype.itemsize >= FAR_BYTES
        args = [pltpu.with_memory_space_constraint(x, pltpu.HBM) if large(x) else x for x in args]
        placed = [
            pltpu.HBM(x.shape, x.dtype) if large(x) and spec.block_shape is not None else x
            for spec, x in zip(specs[len(args) :], outs)
        ]
        return pl.pallas_call(
            kernel,
            out_shape=tuple(placed) if isinstance(out_shape, tuple) else placed[0],
            in_specs=in_specs,
            out_specs=out_specs,
            scratch_shapes=list(scratch),
            compiler_params=pltpu.CompilerParams(vmem_limit_bytes=total),
            cost_estimate=pl.CostEstimate(flops=0, bytes_accessed=0, transcendentals=0),
            name=name,
            **more,
        )(*args)

    return run


def shaped(shape, dtype=F32):
    return jax.ShapeDtypeStruct(shape, dtype)


def lane_of(shape):
    return lax.broadcasted_iota(jnp.int32, shape, len(shape) - 1)


def masked_tile_kernel(row_order, n_across, n_pieces, where_ref, mask_ref, tile_ref, *refs):
    out_refs, wide_ref = refs[:-1], refs[-1]
    col, row = where_ref[0], where_ref[1]
    tall = BLK * n_across
    per_piece = len(row_order) // n_pieces
    for m in range(MB):
        for i, j in enumerate(row_order):
            block = col ^ j
            wide_ref[...] = tile_ref[m, pl.ds(pl.multiple_of(block * tall, tall), tall), :].astype(F32)
            piece, low = i // per_piece, i % per_piece * BLK
            for k in range(n_across):
                keep = mask_ref[(m * len(row_order) + block) * n_across + k].astype(F32)
                part = (wide_ref[pl.ds(k, BLK, n_across), :] * keep).astype(BF16)
                lanes = pl.ds(pl.multiple_of((row ^ k) * BLK, BLK), BLK)
                out_refs[m * n_pieces + piece][low : low + BLK, lanes] = part
                if piece:
                    at = MB * n_pieces + m * (n_pieces - 1) + piece - 1
                    out_refs[at][low : low + BLK, lanes] = part


def masked_tile(adjacency, block_mask, row_order, my_col, my_row):
    n_across = adjacency.shape[2]
    n_pieces = len(row_order) // 2
    piece = shaped((2 * BLK, n_across * BLK), BF16)
    n_out = MB * (2 * n_pieces - 1)
    out = call(
        lambda *refs: masked_tile_kernel(row_order, n_across, n_pieces, *refs),
        "masked_tile",
        (piece,) * n_out,
        [IN_SMEM, IN_SMEM, pl.BlockSpec((MB, adjacency.shape[1] * n_across, LANES), lambda i: (0, 0, 0))],
        (pl.BlockSpec((2 * BLK, n_across * BLK), lambda i: (0, 0)),) * n_out,
        grid=(1,),
        room=4,
        scratch=[pltpu.VMEM((n_across * BLK, LANES), F32)],
    )(
        jnp.stack([my_col, my_row]).astype(jnp.int32),
        block_mask.reshape(-1),
        adjacency.reshape(MB, -1, LANES),
    )
    tile = [out[m * n_pieces : (m + 1) * n_pieces] for m in range(MB)]
    leave = out[MB * n_pieces :]
    return tile, [leave[m * (n_pieces - 1) : (m + 1) * (n_pieces - 1)] for m in range(MB)]


def layer_one_kernel(n_z, *refs):
    tile_refs, feat_refs, (near_ref, far_ref) = refs[: MB * n_z], refs[MB * n_z : -2], refs[-2:]
    ns = near_ref.shape[2]
    for m in range(MB):
        feats = jnp.concatenate([f[m] for f in feat_refs], 0)
        for i in range(n_z):
            out = mm(tile_refs[m * n_z + i][...], feats)
            near_ref[i, m] = out[:ns]
            far_ref[i, m] = out[ns:]


def layer_one(tile, feats):
    n_z = len(tile[0])
    half, across = tile[0][0].shape
    out = shaped((n_z, MB, half // 2, LANES))
    return call(
        lambda *refs: layer_one_kernel(n_z, *refs),
        "layer_one",
        (out, out),
        [pl.BlockSpec((half, across), lambda i: (0, 0))] * (MB * n_z) + [IN_VMEM] * len(feats),
        (IN_VMEM, IN_VMEM),
        grid=(1,),
    )(*tile[0], *tile[1], *feats)


def twice_gelu(z):
    return z + z * jnp.tanh(z * (GELU_ONE + GELU_THREE * (z * z)))


def twice_gelu_both(z):
    square = z * z
    t = jnp.tanh(z * (GELU_ONE + GELU_THREE * square))
    slope = z * (GELU_ONE + (3 * GELU_THREE) * square)
    return z + z * t, (1.0 + t) * (1.0 + (1.0 - t) * slope)


def forward_kernel(n_z, n_rows, m, *refs):
    g_refs, strip_refs = refs[:n_rows], refs[n_rows : n_rows + n_z]
    w_ref, near_ref, far_ref, slope_ref = refs[n_rows + n_z :]
    half = near_ref.shape[0]
    total = None
    for i in range(n_z):
        g = jnp.concatenate([g_ref[i, m] for g_ref in g_refs], 0)
        h, slope = twice_gelu_both(mm(g, w_ref[...]))
        n = g.shape[0]
        slope_ref[i * n : (i + 1) * n] = slope.astype(BF16)
        part = mm(strip_refs[i][...], h.astype(BF16))
        total = part if total is None else total + part
    near_ref[...] = 0.5 * total[:half]
    far_ref[...] = (0.5 * total[half:]).astype(BF16)


def forward_two(g_all, w_pad, strip, m, wide=256):
    n_rows, n_z = len(g_all), len(strip)
    rows, across = strip[0].shape
    span = w_pad.shape[1]
    n = n_z * across
    return call(
        lambda *refs: forward_kernel(n_z, n_rows, m, *refs),
        "forward_two",
        (shaped((rows // 2, span)), shaped((rows // 2, span), BF16), shaped((n, span), BF16)),
        [pl.BlockSpec(g_all[0].shape, lambda f: (0, 0, 0, 0))] * n_rows
        + [pl.BlockSpec((rows, across), lambda f: (0, 0))] * n_z
        + [pl.BlockSpec((LANES, wide), lambda f: (0, f))],
        (pl.BlockSpec((rows // 2, wide), lambda f: (0, f)),) * 2 + (pl.BlockSpec((n, wide), lambda f: (0, f)),),
        grid=(span // wide,),
        room=2 + 8 * across // 1024,
    )(*g_all, *strip, w_pad)


def one_hot(here, there):
    return jnp.where(here == there, 1.0, 0.0).astype(BF16)


def spread_kernel(n_m, n_blocks, *refs):
    near_parts, far_parts = refs[:n_m], refs[n_m : 2 * n_m]
    g_one_ref, w_ref, diag_ref, which_ref, gn_ref, gf_ref, g_ref = refs[2 * n_m :]
    ns = near_parts[0].shape[0]

    @pl.when(pl.program_id(0) == 0)
    def _():
        step = 256
        for at in range(0, HID, step):
            cut = slice(at, at + step)
            h = (0.5 * twice_gelu(mm(g_one_ref[...], w_ref[:, cut]))).astype(BF16)
            for m in range(n_m):
                g_ref[m * ns : (m + 1) * ns, cut] = (
                    near_parts[m][:, cut]
                    + far_parts[m][:, cut].astype(F32)
                    + LAMBDA * diag_ref[:, m : m + 1] * h[m * ns : (m + 1) * ns].astype(F32)
                ).astype(BF16)

    which = which_ref[...]
    hot = one_hot(lax.broadcasted_iota(jnp.int32, (HID, which.shape[1]), 0), which)
    out = mm(g_ref[...], hot).astype(BF16)

    @pl.when(pl.program_id(0) < n_blocks)
    def _():
        gn_ref[...] = out

    @pl.when(pl.program_id(0) >= n_blocks)
    def _():
        gf_ref[...] = out


def block_width(n):
    return 384 if n % 384 == 0 else LANES


def spread_two(near_parts, far_parts, g_one, w_pad, diag, which):
    ns = near_parts[0].shape[0]
    n_m = len(near_parts)
    n_near = which.shape[1] // 2
    rows = n_m * ns
    wide = block_width(n_near)
    n = n_near // wide
    whole = lambda k: (0, 0)
    out = shaped((rows, n_near), BF16)
    return call(
        lambda *refs: spread_kernel(n_m, n, *refs),
        "spread_two",
        (out, out),
        [pl.BlockSpec((ns, HID), whole)] * (2 * n_m)
        + [
            pl.BlockSpec((rows, LANES), whole),
            pl.BlockSpec((LANES, HID), whole),
            pl.BlockSpec((ns, n_m), whole),
            pl.BlockSpec((1, wide), lambda k: (0, k)),
        ],
        (
            pl.BlockSpec((rows, wide), lambda k: (0, jnp.minimum(k, n - 1))),
            pl.BlockSpec((rows, wide), lambda k: (0, jnp.maximum(k - n, 0))),
        ),
        grid=(2 * n,),
        scratch=[pltpu.VMEM((rows, HID), BF16)],
        room=8,
    )(*near_parts, *far_parts, g_one, w_pad, diag, which)


def layer_two_kernel(gn_ref, gf_ref, wn_ref, wf_ref, b_ref, w3_ref, here_ref, z_ref, h_ref, q_ref, sum_ref):
    ns = sum_ref.shape[0]

    @pl.when(pl.program_id(0) == 0)
    def _():
        sum_ref[...] = jnp.zeros_like(sum_ref)

    z = mm(gn_ref[...], wn_ref[...]) + mm(gf_ref[...], wf_ref[...]) + b_ref[...]
    z_ref[...] = z
    h = (0.5 * twice_gelu(z)).astype(BF16)
    h_ref[...] = h
    q = mm(h, w3_ref[...])
    lane = lane_of(sum_ref.shape)
    sum_ref[...] += jnp.where(lane < LANES // 2, q[:ns], q[ns:])

    @pl.when(pl.program_id(0) == pl.num_programs(0) - 1)
    def _():
        q_ref[...] = jnp.where(lane == LANES - 1, here_ref[...], sum_ref[...]).astype(BF16)


def layer_two(g_near, g_far, near, far, b_second, w3, here, wide=512):
    rows, n_near = g_near.shape
    ns = rows // MB
    whole = lambda f: (0, 0)
    return call(
        layer_two_kernel,
        "layer_two",
        (shaped((rows, HID)), shaped((rows, HID), BF16), shaped((ns, LANES), BF16)),
        [
            pl.BlockSpec((rows, n_near), whole),
            pl.BlockSpec((rows, n_near), whole),
            pl.BlockSpec((n_near, wide), lambda f: (0, f)),
            pl.BlockSpec((n_near, wide), lambda f: (0, f)),
            pl.BlockSpec((1, wide), lambda f: (0, f)),
            pl.BlockSpec((wide, LANES), lambda f: (f, 0)),
            pl.BlockSpec((1, LANES), whole),
        ],
        (
            pl.BlockSpec((rows, wide), lambda f: (0, f)),
            pl.BlockSpec((rows, wide), lambda f: (0, f)),
            pl.BlockSpec((ns, LANES), whole),
        ),
        grid=(HID // wide,),
        scratch=[pltpu.VMEM((ns, LANES), F32)],
    )(g_near, g_far, near, far, b_second, w3, here)


def logits_kernel(n_z, *refs):
    strips, q_refs, (near_ref, far_ref) = refs[: MB * n_z], refs[MB * n_z : -2], refs[-2:]
    half = near_ref.shape[0]
    lane = lane_of((2 * half, LANES))
    sums = [None] * MB
    for i in range(n_z):
        all_q = jnp.concatenate([q[i] for q in q_refs], 0)
        for m in range(MB):
            part = mm(strips[m * n_z + i][...], all_q)
            sums[m] = part if sums[m] is None else sums[m] + part
    out = jnp.where(lane < LANES // 2, sums[0], sums[1])
    count = sum(jnp.sum(q[:, 0:1, :].astype(F32), axis=0) for q in q_refs)
    out = jnp.where(lane == LANES - 1, count, out)
    near_ref[...] = out[:half]
    far_ref[...] = out[half:]


def logits_parts(strips, q_rows):
    n_z = len(strips[0])
    rows, across = strips[0][0].shape
    out = shaped((rows // 2, LANES))
    return call(
        lambda *refs: logits_kernel(n_z, *refs),
        "logits_parts",
        (out, out),
        [pl.BlockSpec((rows, across), lambda i: (0, 0))] * (MB * n_z) + [IN_VMEM] * len(q_rows),
        (IN_VMEM, IN_VMEM),
        grid=(1,),
    )(*strips[0], *strips[1], *q_rows)


def loss_kernel(near_ref, got_ref, q_ref, diag_ref, bias_ref, labels_ref, counted_ref, ds_ref, row_ref):
    total = near_ref[...] + got_ref[...]
    node_total = total[0:1, LANES - 1 :]
    lane = lane_of(total.shape)
    low = lane < LANES // 2
    at = jnp.where(low, lane, lane - LANES // 2)
    real = at < NCLS
    pick = lambda ref: jnp.where(low, ref[:, 0:1], ref[:, 1:2])
    logits = total + LAMBDA * pick(diag_ref) * q_ref[...].astype(F32) + bias_ref[...]
    least = jnp.float32(-3.0e38)
    hits = jnp.logical_and(real, at == pick(labels_ref))
    counted = pick(counted_ref)
    parts = []
    for side in (jnp.logical_and(real, low), jnp.logical_and(real, jnp.logical_not(low))):
        top = jnp.max(jnp.where(side, logits, least), axis=1, keepdims=True)
        powers = jnp.where(side, jnp.exp(jnp.where(side, logits - top, 0.0)), 0.0)
        parts.append((top, jnp.sum(powers, axis=1, keepdims=True)))
    log_total = jnp.where(
        low, parts[0][0] + jnp.log(parts[0][1]), parts[1][0] + jnp.log(parts[1][1])
    )
    loss = jnp.where(hits, counted * (log_total - logits), 0.0)
    soft = jnp.exp(jnp.where(real, logits - log_total, 0.0))
    d_logits = jnp.where(real, counted * (soft - hits.astype(F32)) / node_total, 0.0)
    ds_ref[...] = d_logits.astype(BF16)
    row_ref[0:1] = jnp.sum(d_logits, axis=0, keepdims=True)
    row_ref[1:2] = jnp.broadcast_to(jnp.sum(jnp.sum(loss, axis=0, keepdims=True), axis=1, keepdims=True), (1, LANES))
    row_ref[2:3] = jnp.broadcast_to(node_total, (1, LANES))
    row_ref[3:8] = jnp.zeros((5, LANES), F32)


def d_q_kernel(n_z, *refs):
    tile_refs, s_refs, out_refs = refs[: MB * n_z], refs[MB * n_z : (MB + 1) * n_z], refs[(MB + 1) * n_z :]
    side = out_refs[0].shape[0]
    lane = lane_of((side * len(out_refs), LANES))
    sums = [None] * MB
    for i in range(n_z):
        all_s = jnp.concatenate([s_refs[i][core] for core in (0, 1)], 0)
        for m in range(MB):
            part = mm_t(tile_refs[m * n_z + i][...], all_s)
            sums[m] = part if sums[m] is None else sums[m] + part
    out = jnp.where(lane < LANES // 2, sums[0], sums[1])
    for k, out_ref in enumerate(out_refs):
        out_ref[...] = out[k * side : (k + 1) * side]


def d_q_parts(tile, pieces):
    n_z = len(pieces)
    rows, across = tile[0][0].shape
    n = across // BLK
    return call(
        lambda *refs: d_q_kernel(n_z, *refs),
        "d_q_parts",
        (shaped((BLK, LANES)),) * n,
        [pl.BlockSpec((rows, across), lambda i: (0, 0))] * (MB * n_z) + [IN_VMEM] * n_z,
        (IN_VMEM,) * n,
        grid=(1,),
    )(*tile[0], *tile[1], *pieces)


def d_two_kernel(n_q, *refs):
    q_refs = refs[:n_q]
    ds_ref, diag_ref, z_ref, h_ref, w3_ref, g_ref, dz_ref, db_ref, dw3_ref, far_ref = refs[n_q:]
    ns = ds_ref.shape[0]
    d_q = q_refs[0][...]
    for q in q_refs[1:]:
        d_q = d_q + q[...]
    low = lane_of(d_q.shape) < LANES // 2
    d_q = d_q + LAMBDA * jnp.where(low, diag_ref[:, 0:1], diag_ref[:, 1:2]) * ds_ref[...].astype(F32)
    d_q = jnp.concatenate([jnp.where(low, d_q, 0.0), jnp.where(low, 0.0, d_q)], 0).astype(BF16)
    d_z = mm_nt(d_q, w3_ref[...]) * (0.5 * twice_gelu_both(z_ref[...])[1])
    db_ref[...] = jnp.sum(d_z.reshape(-1, 8, d_z.shape[1]), axis=0)
    d_zb = d_z.astype(BF16)
    dz_ref[...] = d_zb
    dw3_ref[...] = mm_t(h_ref[...], d_q)
    far_ref[...] = mm_t(g_ref[...], d_zb).astype(BF16)


def d_two(d_q, d_s, diag, z_two, h_two, w3, g_far, lo, hi, wide=256):
    rows = z_two.shape[0]
    ns, n_far = d_s.shape[0], g_far.shape[1]
    whole = lambda f: (0, 0)
    start = lo // wide
    small = pl.BlockSpec((ns, LANES), whole)
    column = pl.BlockSpec((rows, wide), lambda f: (0, start + f))
    span = hi - lo
    return call(
        lambda *refs: d_two_kernel(len(d_q), *refs),
        "d_two",
        (
            shaped((rows, span), BF16),
            shaped((8, span)),
            shaped((span, LANES)),
            shaped((n_far, span), BF16),
        ),
        [small] * (len(d_q) + 1)
        + [
            pl.BlockSpec((ns, MB), whole),
            column,
            column,
            pl.BlockSpec((wide, LANES), lambda f: (start + f, 0)),
            pl.BlockSpec((rows, n_far), whole),
        ],
        (
            pl.BlockSpec((rows, wide), lambda f: (0, f)),
            pl.BlockSpec((8, wide), lambda f: (0, f)),
            pl.BlockSpec((wide, LANES), lambda f: (f, 0)),
            pl.BlockSpec((n_far, wide), lambda f: (0, f)),
        ),
        grid=(span // wide,),
        room=4,
    )(*d_q, d_s, diag, z_two, h_two, w3, g_far)


def near_kernel(keep, send, rows, g_ref, dz_ref, got_ref, keep_ref, send_ref):
    total = mm_t(g_ref[...], dz_ref[...]) + got_ref[...].astype(F32)
    for out_ref, picks in ((keep_ref, keep), (send_ref, send)):
        for i, j in enumerate(picks):
            out_ref[i * rows : (i + 1) * rows] = total[j * rows : (j + 1) * rows].astype(out_ref.dtype)


def near_part(g_near, d_zb, got, n_rows, bit, wide=256):
    n_near, span = got.shape
    rows = n_near // n_rows
    keep = [j for j in range(n_rows) if not j & bit]
    send = [j | bit for j in keep]
    column = lambda n: pl.BlockSpec((n, wide), lambda f: (0, f))
    return call(
        lambda *refs: near_kernel(keep, send, rows, *refs),
        "near_part",
        (shaped((n_near // 2, span)), shaped((n_near // 2, span), BF16)),
        [pl.BlockSpec(g_near.shape, lambda f: (0, 0)), column(g_near.shape[0]), column(n_near)],
        (column(n_near // 2), column(n_near // 2)),
        grid=(span // wide,),
    )(g_near, d_zb, got)


def backward_kernel(n_z, n_rows, *refs):
    g_refs, strip_refs = refs[:n_rows], refs[n_rows : n_rows + MB * n_z]
    slope_refs, (dgn_ref, dgf_ref, diag_ref, dw_ref) = refs[-4 - MB : -4], refs[-4:]
    own = dgn_ref.shape[1]
    total = None
    for m in range(MB):
        d_g = jnp.concatenate([dgn_ref[m], dgf_ref[m]], 0)
        for i in range(n_z):
            d_h = mm_t(strip_refs[m * n_z + i][...], d_g)
            n = d_h.shape[0]
            if i == 0:
                more = LAMBDA * diag_ref[:, m : m + 1] * dgn_ref[m].astype(F32)
                d_h = jnp.concatenate([d_h[:own] + more, d_h[own:]], 0)
            g = jnp.concatenate([g_ref[i, m] for g_ref in g_refs], 0)
            d_z = d_h * slope_refs[m][i * n : (i + 1) * n].astype(F32)
            part = mm_t(g, d_z.astype(BF16))
            total = part if total is None else total + part
    dw_ref[...] = (0.5 * total).astype(BF16)


def backward_one(g_all, strips, slopes, d_g_near, d_g_far, diag, lo, hi, wide=256):
    n_rows, n_z = len(g_all), len(strips[0])
    rows, across = strips[0][0].shape
    span = hi - lo
    start = lo // wide
    column = pl.BlockSpec((MB, rows // 2, wide), lambda f: (0, 0, start + f))
    return call(
        lambda *refs: backward_kernel(n_z, n_rows, *refs),
        "backward_one",
        shaped((LANES, span), BF16),
        [pl.BlockSpec(g_all[0].shape, lambda f: (0, 0, 0, 0))] * n_rows
        + [pl.BlockSpec((rows, across), lambda f: (0, 0))] * (MB * n_z)
        + [pl.BlockSpec((n_z * across, wide), lambda f: (0, start + f))] * MB
        + [column, column, pl.BlockSpec((rows // 2, MB), lambda f: (0, 0))],
        pl.BlockSpec((LANES, wide), lambda f: (0, f)),
        grid=(span // wide,),
        room=2 + 8 * across // 1024,
    )(*g_all, *strips[0], *strips[1], *slopes, d_g_near, d_g_far, diag)


def d_g_kernel(n_blocks, cuts, *refs):
    dz_refs, (which_ref, wn_ref, wf_ref, out_ref, sum_ref) = refs[: len(cuts)], refs[len(cuts) :]
    step = pl.program_id(0)

    @pl.when(step == 0)
    def _():
        sum_ref[...] = jnp.zeros_like(sum_ref)

    def add(w_ref):
        part = sum(mm_nt(dz[...], w_ref[:, lo:hi]) for dz, (lo, hi) in zip(dz_refs, cuts)).astype(BF16)
        which = which_ref[...]
        hot = one_hot(lax.broadcasted_iota(jnp.int32, (which.shape[0], HID), 1), which)
        sum_ref[...] += mm(part, hot)

    @pl.when(step < n_blocks)
    def _():
        add(wn_ref)

    @pl.when(step >= n_blocks)
    def _():
        add(wf_ref)

    @pl.when(step == pl.num_programs(0) - 1)
    def _():
        out_ref[...] = sum_ref[...].astype(BF16)


def d_g_two(d_zb, cuts, which, near, far):
    rows, n_near = d_zb[0].shape[0], near.shape[0]
    wide = block_width(n_near)
    n = n_near // wide
    return call(
        lambda *refs: d_g_kernel(n, cuts, *refs),
        "d_g_two",
        shaped((rows, HID), BF16),
        [pl.BlockSpec(d.shape, lambda k: (0, 0)) for d in d_zb]
        + [
            pl.BlockSpec((wide, 1), lambda k: (k, 0)),
            pl.BlockSpec((wide, HID), lambda k: (jnp.minimum(k, n - 1), 0)),
            pl.BlockSpec((wide, HID), lambda k: (jnp.maximum(k - n, 0), 0)),
        ],
        pl.BlockSpec((rows, HID), lambda k: (0, 0)),
        grid=(2 * n,),
        scratch=[pltpu.VMEM((rows, HID), F32)],
        room=8,
    )(*d_zb, which, near, far)


def thirds_kernel(row_ref, out_ref):
    rest = row_ref[...]
    out_ref[...] = jnp.zeros_like(out_ref)
    for i in range(3):
        low = rest.astype(BF16)
        out_ref[i : i + 1] = low
        rest = rest - low.astype(F32)


def thirds(row):
    return call(thirds_kernel, "thirds", shaped((16, LANES), BF16), [IN_VMEM], IN_VMEM)(row)


def join_kernel(sizes, *refs):
    pieces, out_ref, sems = refs[: len(sizes)], refs[len(sizes)], refs[-1]
    at, copies = 0, []
    for i, (piece, size) in enumerate(zip(pieces, sizes)):
        copies.append(pltpu.make_async_copy(piece, out_ref.at[pl.ds(at, size)], sems.at[i]))
        copies[-1].start()
        at += size
    for copy in copies:
        copy.wait()


def join(pieces):
    sizes = [p.shape[0] for p in pieces]
    return call(
        lambda *refs: join_kernel(sizes, *refs),
        "join",
        shaped((sum(sizes),) + pieces[0].shape[1:], pieces[0].dtype),
        [ANYWHERE] * len(pieces),
        IN_VMEM,
        room=2,
        scratch=[pltpu.SemaphoreType.DMA((len(pieces),))],
    )(*pieces)


def per_device(features, adjacency, block_mask, diagonal, labels, train_mask, params, first_moment, second_moment):
    n_rows, n_cols = lax.axis_size("rows"), lax.axis_size("cols")
    n_z = n_cols // 2
    n_dev = n_rows * n_cols
    my_row, my_col = lax.axis_index("rows"), lax.axis_index("cols")
    me = my_row * n_cols + my_col
    ns = features.shape[1]
    z_bits, row_bits = bits_of(n_z), bits_of(n_rows)
    turned = row_bits[1:] + row_bits[:1]
    single = z_bits[::-1]
    several = [j for j in range(1, n_z) if j not in single]
    z_order = [0] + single + several

    def over_z(x):
        return [x] + [swap(x, "cols", 2 * j) for j in z_order[1:]]

    def over_rows(x):
        return [x] + [swap(x, "rows", j) for j in range(1, n_rows)]

    n_own = params.shape[0] // LANES
    slot = -(-((n_own + UNIT - 2) // UNIT + 1) // 8) * 8
    shift = lax.rem(n_own * me, UNIT)
    own = lax.dynamic_update_slice(
        jnp.zeros((slot * UNIT, LANES), BF16), params.reshape(n_own, LANES).astype(BF16), (shift, 0)
    ).reshape(1, slot, HID)
    wide_feats = jnp.pad(features, ((0, 0), (0, 0), (0, LANES - FIN)))
    ones = lax.broadcasted_iota(jnp.int32, (1, 1, LANES), 2) == FIN
    feats = over_rows(wide_feats)
    tile, leave = masked_tile(
        adjacency.reshape(MB, -1, n_rows, LANES), block_mask, [2 * j + core for j in z_order for core in (0, 1)], my_col, my_row
    )

    part_near, part_far = layer_one(tile, feats)
    own = after(own, part_far)
    by_z = {0: own}
    for j in single:
        by_z[j] = swap(own, "cols", 2 * j)
    partial = part_near + swap(part_far, "cols", 1)
    g_one = partial[0] + LAMBDA * diagonal[:, :, None] * wide_feats.astype(F32)
    low = partial.astype(BF16)
    for i, j in enumerate(z_order[1:], 1):
        g_one = g_one + swap(low[i], "cols", 2 * j).astype(F32)
    g_one = jnp.where(ones, 1.0, g_one).astype(BF16)

    def units_of(core):
        owner = (my_row ^ jnp.arange(n_rows))[:, None] * n_cols + (
            my_col ^ (2 * jnp.array(z_order) + core)
        )[None, :]
        start = (n_own * owner) // UNIT
        return (start[:, :, None] + jnp.arange(slot)[None, None, :]).reshape(-1)

    near_units = units_of(0)
    units = jnp.concatenate([near_units, units_of(1)])
    which = units - FIN

    middle = after(join([by_z[j] for j in single]), g_one)
    for j in several:
        bit = j & -j
        by_z[j] = swap(by_z[j - bit], "cols", 2 * bit)
    last = by_z[several[0]] if len(several) == 1 else join([by_z[j] for j in several])
    g_z = over_z(g_one)
    last = after(last, *g_z[1:])
    groups = [own, middle, last]
    g_all = over_rows(jnp.stack(g_z))
    strips = [[tile[m][0]] for m in range(MB)]
    for i, j in enumerate(z_order[1:]):
        strips[0].append(swap(after(leave[0][i], *g_all[1:]), "cols", 2 * j))
    passed = {0: groups}
    for j in range(1, n_rows):
        lowest = j & -j
        highest = 1 << (j.bit_length() - 1)
        hop = [passed[j - bit][i] for i, bit in enumerate((highest, lowest, highest))]
        if lowest != highest:
            once = [x for i in passed if i for x in passed[i]]
            hop = [after(h, *g_all[1:], *[x for x in once if x is not h]) for h in hop]
        passed[j] = [swap(h, "rows", bit) for h, bit in zip(hop, (highest, lowest, highest))]
    for m in range(1, MB):
        for i, j in enumerate(z_order[1:]):
            strips[m].append(swap(after(leave[m][i], *strips[m - 1][1:]), "cols", 2 * j))
    passed[0][0] = after(passed[0][0], *strips[0][1:])
    near = join([g.reshape(-1, HID) for j in range(n_rows) for g in passed[j]])
    far = swap(near, "cols", 1)
    n_near = near.shape[0]

    per_small = -(-(FIN + NCLS + 3) // n_dev)
    n_small = per_small * n_dev
    small_unit = jnp.arange(n_small)
    small_unit = jnp.where(small_unit < FIN, small_unit, small_unit + HID)
    pick = (small_unit[:, None] == near_units[None, :]).astype(BF16)
    small = mm(pick, near).astype(BF16)
    small = small + swap(small, "cols", 1)
    w_pad = jnp.concatenate(
        [small[:FIN], small[FIN + NCLS : FIN + NCLS + 1], jnp.zeros((LANES - FIN - 1, HID), BF16)], 0
    )
    w_third = small[FIN : FIN + NCLS].reshape(HID, NCLS)
    gap = jnp.zeros((HID, LANES // 2 - NCLS), BF16)
    w_third = jnp.concatenate([w_third, gap, w_third, gap], 1)
    b_second = small[FIN + NCLS + 1].astype(F32)[None]
    b_third = small[FIN + NCLS + 2].astype(F32)[: LANES // 2]
    b_third = jnp.concatenate([b_third, b_third])[None]

    near_parts, far_parts, slopes = [], [], []
    for m in range(MB):
        if m == MB - 1:
            w_pad = after(w_pad, w_third)
        part_near, part_far, slope = forward_two(g_all, w_pad, strips[m], m)
        slopes.append(slope)
        near_parts.append(part_near)
        far_parts.append(swap(part_far, "cols", 1))

    diag = diagonal.T
    counted = train_mask.T.astype(F32)
    here = jnp.broadcast_to(jnp.sum(counted), (1, LANES))
    g_near, g_far = spread_two(
        near_parts, far_parts, g_one.reshape(MB * ns, LANES), w_pad, diag, which[None]
    )
    z_two, h_two, q = layer_two(g_near, g_far, near, far, b_second, w_third, here)

    part_near, part_far = logits_parts(strips, over_rows(jnp.stack(over_z(q))))
    d_s, sums = call(
        loss_kernel,
        "loss",
        (shaped((ns, LANES), BF16), shaped((8, LANES))),
        [IN_VMEM] * 7,
        (IN_VMEM, IN_VMEM),
    )(part_near, swap(part_far, "cols", 1), q, diag, b_third, labels.T, counted)
    d_bias_three = sums[0, :NCLS] + sums[0, LANES // 2 : LANES // 2 + NCLS]
    loss, node_total = sums[1, 0], sums[2, 0]

    d_q = d_q_parts(tile, over_z(jnp.stack([d_s, swap(d_s, "cols", 1)])))
    d_q = [d_q[0]] + [swap(d_q[j], "rows", j) for j in range(1, n_rows)]

    def split(item, axis, bit):
        dim = 0 if axis == "rows" else 1
        kept, send, item["orders"][axis] = split_bit(item["part"], dim, item["orders"][axis], bit)
        item["kept"], item["send"] = kept, send.astype(BF16)
        item["to"] = (axis, bit * (dim + 1))

    half = HID // 2
    work = []
    for k, bits in enumerate((row_bits, turned)):
        lo, hi = k * half, (k + 1) * half
        wait = d_s if k == 0 else after(d_s, work[0]["dz"])
        d_zb, d_b, d_w3, d_far = d_two(d_q, wait, diag, z_two, h_two, w_third, g_far, lo, hi)
        item = {"bits": bits, "dz": d_zb, "db": d_b, "dw3": d_w3}
        item["got"] = swap(d_far, "cols", 1)
        item["orders"] = {"rows": [j for j in range(n_rows) if not j & bits[0]], "cols": z_order}
        item["to"] = ("rows", bits[0])
        work.append(item)
    for item in work:
        kept, send = near_part(g_near, item["dz"], item["got"], n_rows, item["bits"][0])
        item["kept"], item["send"] = (x.reshape(n_rows // 2, n_z, slot, half) for x in (kept, send))
    d_zb = [item["dz"] for item in work]
    d_bias_two = jnp.concatenate([jnp.sum(item["db"], axis=0) for item in work])
    d_w_three = jnp.concatenate([item["dw3"] for item in work], 0)
    d_w_three = d_w_three[:, :NCLS] + d_w_three[:, LANES // 2 : LANES // 2 + NCLS]

    n_cuts = 3
    cuts = [0, 3 * (HID // 8), 6 * (HID // 8), HID]
    d_zb[0] = after(d_zb[0], *[item["send"] for item in work])
    d_g_near = d_g_two(d_zb, [(0, half), (half, HID)], which[:, None], near, far).reshape(MB, ns, HID)
    d_g_far = swap(d_g_near, "cols", 1)
    d_first = []

    def another_cut():
        i = len(d_first)
        if i < n_cuts:
            d_first.append(
                backward_one(g_all, strips, slopes, d_g_near, d_g_far, diag, cuts[i], cuts[i + 1])
            )

    for i in range(len(row_bits)):
        for item in work:
            item["part"] = item["kept"] + swap(item["send"], *item["to"]).astype(F32)
            if i + 1 < len(row_bits):
                split(item, "rows", item["bits"][i + 1])
        if i + 1 < len(row_bits):
            d_g_near = after(d_g_near, *[item["send"] for item in work])
            another_cut()
    item = {"orders": {"cols": z_order}, "part": jnp.concatenate([item["part"] for item in work], 3)}
    for bit in z_bits:
        split(item, "cols", bit)
        d_g_near = after(d_g_near, item["send"])
        another_cut()
        item["part"] = item["kept"] + swap(item["send"], *item["to"]).astype(F32)
    own_grad = item["part"][0, 0]
    d_first = jnp.concatenate(d_first, 1)
    d_w_one, d_bias_one = d_first[:FIN], d_first[FIN].astype(F32)

    d_small = jnp.concatenate(
        [
            d_w_one.astype(BF16),
            d_w_three.astype(BF16).reshape(NCLS, HID),
            jnp.stack([d_bias_one, d_bias_two, jnp.pad(d_bias_three, (0, HID - NCLS))]).astype(BF16),
            jnp.zeros((n_small - FIN - NCLS - 3, HID), BF16),
        ],
        0,
    )
    d_small = after(d_small.reshape(n_dev, per_small * UNIT, LANES), own_grad)
    got = lax.all_to_all(d_small, BOTH, split_axis=0, concat_axis=0, tiled=True)
    got = jnp.sum(got.astype(F32), axis=0)
    low = got.astype(BF16)

    own_flat = lax.dynamic_slice(own_grad.reshape(slot * UNIT, LANES), (shift, 0), (n_own, LANES))
    squares = jnp.sum(own_flat * own_flat) + jnp.sum(low.astype(F32) ** 2)
    row = jnp.concatenate([squares[None], loss[None], d_bias_three, jnp.zeros((LANES - NCLS - 2,), F32)])
    sent = jnp.concatenate([low, thirds(row[None])], 0)
    sent = jnp.broadcast_to(sent[None], (n_dev,) + sent.shape)
    got = lax.all_to_all(sent, BOTH, split_axis=0, concat_axis=0, tiled=True)
    d_small = got[:, : per_small * UNIT].reshape(n_small, HID)
    row = jnp.sum(got[:, per_small * UNIT : per_small * UNIT + 3].astype(F32), axis=(0, 1))
    squares, loss_sum, class_sum = row[0], row[1], row[2 : 2 + NCLS]

    mine = (n_own * me) // UNIT + jnp.arange(slot)
    place = (mine[:, None] == small_unit[None, :]).astype(BF16)
    small_flat = lax.dynamic_slice(
        mm(place, d_small).reshape(slot * UNIT, LANES), (shift, 0), (n_own, LANES)
    )
    reduced = (own_flat + small_flat).reshape(-1)

    grad_norm = jnp.sqrt(squares)
    clip_scale = jnp.minimum(1.0, CLIP_NORM / (grad_norm + 1e-06))
    clipped = reduced * clip_scale
    class_bias_grad = class_sum * clip_scale
    new_first = BETA_ONE * first_moment + (1.0 - BETA_ONE) * clipped
    new_second = BETA_TWO * second_moment + (1.0 - BETA_TWO) * clipped * clipped
    correct_one = 1.0 - BETA_ONE**STEP
    correct_two = 1.0 - BETA_TWO**STEP
    step_size = new_first / correct_one / (jnp.sqrt(new_second / correct_two) + EPSILON)
    new_params = params - LEARN_RATE * (step_size + WEIGHT_DECAY * params)
    return (new_params, new_first, new_second, grad_norm, loss_sum, node_total, class_bias_grad)


def solution(mesh):
    in_specs = (
        P(None, ("rows", "cols"), None),
        P(None, "rows", None, "cols", None),
        P(None, "rows", None, "cols", None),
        P(None, ("rows", "cols")),
        P(None, ("rows", "cols")),
        P(None, ("rows", "cols")),
        P(("rows", "cols")),
        P(("rows", "cols")),
        P(("rows", "cols")),
    )
    out_specs = (P(("rows", "cols")), P(("rows", "cols")), P(("rows", "cols")), P(), P(), P(), P())
    return jax.shard_map(
        per_device, mesh=mesh, in_specs=in_specs, out_specs=out_specs, check_vma=False
    )
```

```python
import math

import jax
import jax.numpy as jnp
from jax import lax
from jax.experimental import pallas as pl
from jax.experimental.pallas import tpu as pltpu
from jax.sharding import PartitionSpec as P

FIN = 100
HID = 2048
NCLS = 47
BLK = 128
MB = 2
STEP = 10
PARAMS = FIN * HID + HID * HID + HID * NCLS + 2 * HID + NCLS

LAMBDA = 1.0
CLIP_NORM = 0.01
BETA_ONE = 0.9
BETA_TWO = 0.95
EPSILON = 1e-08
WEIGHT_DECAY = 0.1
LEARN_RATE = 0.02

LANES = 128
UNIT = HID // LANES
BOTH = ("rows", "cols")
GELU_ONE = 0.7978845608028654
GELU_THREE = GELU_ONE * 0.044715
F32 = jnp.float32
FAR_BYTES = 1 << 17
BF16 = jnp.bfloat16


def swap(x, axis, bit):
    size = lax.axis_size(axis)
    return lax.ppermute(x, axis, [(i, i ^ bit) for i in range(size)])


def bits_of(size):
    return [1 << i for i in range(size.bit_length() - 1)]


def mm(left, right):
    return jnp.dot(left, right, preferred_element_type=F32)


def mm_t(left, right):
    return lax.dot_general(left, right, (((0,), (0,)), ((), ())), preferred_element_type=F32)


def mm_nt(left, right):
    return lax.dot_general(left, right, (((1,), (1,)), ((), ())), preferred_element_type=F32)


def take(x, axis, picks):
    return jnp.concatenate([lax.slice_in_dim(x, p, p + 1, axis=axis) for p in picks], axis)


def split_bit(x, axis, order, bit):
    keep = [j for j in order if not j & bit]
    run = next(i for i, j in enumerate(order) if j & bit)
    if any(bool(j & bit) != bool(i // run % 2) or j & ~bit != order[i - i // run % 2 * run] & ~bit for i, j in enumerate(order)):
        at = {j: i for i, j in enumerate(order)}
        return take(x, axis, [at[j] for j in keep]), take(x, axis, [at[j | bit] for j in keep]), keep
    shape = x.shape[:axis] + (len(order) // (2 * run), 2, run) + x.shape[axis + 1 :]
    kept_shape = x.shape[:axis] + (len(keep),) + x.shape[axis + 1 :]
    x = x.reshape(shape)
    pair = [lax.index_in_dim(x, i, axis + 1, keepdims=False).reshape(kept_shape) for i in (0, 1)]
    return pair[0], pair[1], keep


ANYWHERE = pl.BlockSpec(memory_space=pl.ANY)
IN_VMEM = pl.BlockSpec(memory_space=pltpu.VMEM)
IN_SMEM = pl.BlockSpec(memory_space=pltpu.SMEM)


def tip(x):
    while x.ndim > 2:
        x = x[0]
    return x[:8, :128].astype(F32)


def after_kernel(*refs):
    pass


def after(x, *earlier):
    earlier = [tip(e) for e in earlier]
    return pl.pallas_call(
        after_kernel,
        out_shape=jax.ShapeDtypeStruct(x.shape, x.dtype),
        in_specs=[ANYWHERE] * (1 + len(earlier)),
        out_specs=ANYWHERE,
        input_output_aliases={0: 0},
        name="after",
    )(x, *earlier)


def padded_bytes(shape, dtype):
    *front, rows, lanes = (1, 1, *shape)
    size = -(-rows // 16) * 16 * -(-lanes // LANES) * LANES * jnp.dtype(dtype).itemsize
    for n in front:
        size *= n
    return size


def call(kernel, name, out_shape, in_specs, out_specs, grid=None, room=4, scratch=()):
    more = {} if grid is None else {"grid": grid}

    def run(*args):
        outs = out_shape if isinstance(out_shape, tuple) else (out_shape,)
        specs = (*in_specs, *(out_specs if isinstance(out_specs, tuple) else (out_specs,)))
        total = room << 20
        for spec, x in zip(specs, (*args, *outs)):
            if spec.block_shape is not None:
                total += 2 * padded_bytes(spec.block_shape, x.dtype)
            elif spec.memory_space == pltpu.VMEM:
                total += padded_bytes(x.shape, x.dtype)
        large = lambda x: math.prod(x.shape) * x.dtype.itemsize >= FAR_BYTES
        args = [pltpu.with_memory_space_constraint(x, pltpu.HBM) if large(x) else x for x in args]
        placed = [
            pltpu.HBM(x.shape, x.dtype) if large(x) and spec.block_shape is not None else x
            for spec, x in zip(specs[len(args) :], outs)
        ]
        return pl.pallas_call(
            kernel,
            out_shape=tuple(placed) if isinstance(out_shape, tuple) else placed[0],
            in_specs=in_specs,
            out_specs=out_specs,
            scratch_shapes=list(scratch),
            compiler_params=pltpu.CompilerParams(vmem_limit_bytes=total),
            cost_estimate=pl.CostEstimate(flops=0, bytes_accessed=0, transcendentals=0),
            name=name,
            **more,
        )(*args)

    return run


def shaped(shape, dtype=F32):
    return jax.ShapeDtypeStruct(shape, dtype)


def lane_of(shape):
    return lax.broadcasted_iota(jnp.int32, shape, len(shape) - 1)


def masked_tile_kernel(row_order, n_across, n_pieces, where_ref, mask_ref, tile_ref, *refs):
    out_refs, wide_ref = refs[:-1], refs[-1]
    col, row = where_ref[0], where_ref[1]
    tall = BLK * n_across
    per_piece = len(row_order) // n_pieces
    for m in range(MB):
        for i, j in enumerate(row_order):
            block = col ^ j
            wide_ref[...] = tile_ref[m, pl.ds(pl.multiple_of(block * tall, tall), tall), :].astype(F32)
            piece, low = i // per_piece, i % per_piece * BLK
            for k in range(n_across):
                keep = mask_ref[(m * len(row_order) + block) * n_across + k].astype(F32)
                part = (wide_ref[pl.ds(k, BLK, n_across), :] * keep).astype(BF16)
                lanes = pl.ds(pl.multiple_of((row ^ k) * BLK, BLK), BLK)
                out_refs[m * n_pieces + piece][low : low + BLK, lanes] = part
                if piece:
                    at = MB * n_pieces + m * (n_pieces - 1) + piece - 1
                    out_refs[at][low : low + BLK, lanes] = part


def masked_tile(adjacency, block_mask, row_order, my_col, my_row):
    n_across = adjacency.shape[2]
    n_pieces = len(row_order) // 2
    piece = shaped((2 * BLK, n_across * BLK), BF16)
    n_out = MB * (2 * n_pieces - 1)
    out = call(
        lambda *refs: masked_tile_kernel(row_order, n_across, n_pieces, *refs),
        "masked_tile",
        (piece,) * n_out,
        [IN_SMEM, IN_SMEM, pl.BlockSpec((MB, adjacency.shape[1] * n_across, LANES), lambda i: (0, 0, 0))],
        (pl.BlockSpec((2 * BLK, n_across * BLK), lambda i: (0, 0)),) * n_out,
        grid=(1,),
        room=4,
        scratch=[pltpu.VMEM((n_across * BLK, LANES), F32)],
    )(
        jnp.stack([my_col, my_row]).astype(jnp.int32),
        block_mask.reshape(-1),
        adjacency.reshape(MB, -1, LANES),
    )
    tile = [out[m * n_pieces : (m + 1) * n_pieces] for m in range(MB)]
    leave = out[MB * n_pieces :]
    return tile, [leave[m * (n_pieces - 1) : (m + 1) * (n_pieces - 1)] for m in range(MB)]


def layer_one_kernel(n_z, *refs):
    tile_refs, feat_refs, (near_ref, far_ref) = refs[: MB * n_z], refs[MB * n_z : -2], refs[-2:]
    ns = near_ref.shape[2]
    for m in range(MB):
        feats = jnp.concatenate([f[m] for f in feat_refs], 0)
        for i in range(n_z):
            out = mm(tile_refs[m * n_z + i][...], feats)
            near_ref[i, m] = out[:ns]
            far_ref[i, m] = out[ns:]


def layer_one(tile, feats):
    n_z = len(tile[0])
    half, across = tile[0][0].shape
    out = shaped((n_z, MB, half // 2, LANES))
    return call(
        lambda *refs: layer_one_kernel(n_z, *refs),
        "layer_one",
        (out, out),
        [pl.BlockSpec((half, across), lambda i: (0, 0))] * (MB * n_z) + [IN_VMEM] * len(feats),
        (IN_VMEM, IN_VMEM),
        grid=(1,),
    )(*tile[0], *tile[1], *feats)


def twice_gelu(z):
    return z + z * jnp.tanh(z * (GELU_ONE + GELU_THREE * (z * z)))


def twice_gelu_both(z):
    square = z * z
    t = jnp.tanh(z * (GELU_ONE + GELU_THREE * square))
    slope = z * (GELU_ONE + (3 * GELU_THREE) * square)
    above = 1.0 + t
    return z * above, above * (1.0 + (1.0 - t) * slope)


def forward_kernel(n_z, n_rows, m, *refs):
    g_refs, strip_refs = refs[:n_rows], refs[n_rows : n_rows + n_z]
    w_ref, near_ref, far_ref, slope_ref = refs[n_rows + n_z :]
    half = near_ref.shape[0]
    total = None
    for i in range(n_z):
        g = jnp.concatenate([g_ref[i, m] for g_ref in g_refs], 0)
        h, slope = twice_gelu_both(mm(g, w_ref[...]))
        n = g.shape[0]
        slope_ref[i * n : (i + 1) * n] = slope.astype(BF16)
        part = mm(strip_refs[i][...], h.astype(BF16))
        total = part if total is None else total + part
    near_ref[...] = 0.5 * total[:half]
    far_ref[...] = (0.5 * total[half:]).astype(BF16)


def forward_two(g_all, w_pad, strip, m, wide=256):
    n_rows, n_z = len(g_all), len(strip)
    rows, across = strip[0].shape
    span = w_pad.shape[1]
    n = n_z * across
    return call(
        lambda *refs: forward_kernel(n_z, n_rows, m, *refs),
        "forward_two",
        (shaped((rows // 2, span)), shaped((rows // 2, span), BF16), shaped((n, span), BF16)),
        [pl.BlockSpec(g_all[0].shape, lambda f: (0, 0, 0, 0))] * n_rows
        + [pl.BlockSpec((rows, across), lambda f: (0, 0))] * n_z
        + [pl.BlockSpec((LANES, wide), lambda f: (0, f))],
        (pl.BlockSpec((rows // 2, wide), lambda f: (0, f)),) * 2 + (pl.BlockSpec((n, wide), lambda f: (0, f)),),
        grid=(span // wide,),
        room=2 + 8 * across // 1024,
    )(*g_all, *strip, w_pad)


def one_hot(here, there):
    return jnp.where(here == there, 1.0, 0.0).astype(BF16)


def spread_kernel(n_m, n_blocks, *refs):
    near_parts, far_parts = refs[:n_m], refs[n_m : 2 * n_m]
    g_one_ref, w_ref, diag_ref, which_ref, gn_ref, gf_ref, g_ref = refs[2 * n_m :]
    ns = near_parts[0].shape[0]

    @pl.when(pl.program_id(0) == 0)
    def _():
        step = 256
        for at in range(0, HID, step):
            cut = slice(at, at + step)
            h = (0.5 * twice_gelu(mm(g_one_ref[...], w_ref[:, cut]))).astype(BF16)
            for m in range(n_m):
                g_ref[m * ns : (m + 1) * ns, cut] = (
                    near_parts[m][:, cut]
                    + far_parts[m][:, cut].astype(F32)
                    + LAMBDA * diag_ref[:, m : m + 1] * h[m * ns : (m + 1) * ns].astype(F32)
                ).astype(BF16)

    which = which_ref[...]
    hot = one_hot(lax.broadcasted_iota(jnp.int32, (HID, which.shape[1]), 0), which)
    out = mm(g_ref[...], hot).astype(BF16)

    @pl.when(pl.program_id(0) < n_blocks)
    def _():
        gn_ref[...] = out

    @pl.when(pl.program_id(0) >= n_blocks)
    def _():
        gf_ref[...] = out


def block_width(n):
    return 384 if n % 384 == 0 else LANES


def spread_two(near_parts, far_parts, g_one, w_pad, diag, which):
    ns = near_parts[0].shape[0]
    n_m = len(near_parts)
    n_near = which.shape[1] // 2
    rows = n_m * ns
    wide = block_width(n_near)
    n = n_near // wide
    whole = lambda k: (0, 0)
    out = shaped((rows, n_near), BF16)
    return call(
        lambda *refs: spread_kernel(n_m, n, *refs),
        "spread_two",
        (out, out),
        [pl.BlockSpec((ns, HID), whole)] * (2 * n_m)
        + [
            pl.BlockSpec((rows, LANES), whole),
            pl.BlockSpec((LANES, HID), whole),
            pl.BlockSpec((ns, n_m), whole),
            pl.BlockSpec((1, wide), lambda k: (0, k)),
        ],
        (
            pl.BlockSpec((rows, wide), lambda k: (0, jnp.minimum(k, n - 1))),
            pl.BlockSpec((rows, wide), lambda k: (0, jnp.maximum(k - n, 0))),
        ),
        grid=(2 * n,),
        scratch=[pltpu.VMEM((rows, HID), BF16)],
        room=8,
    )(*near_parts, *far_parts, g_one, w_pad, diag, which)


def layer_two_kernel(gn_ref, gf_ref, wn_ref, wf_ref, b_ref, w3_ref, here_ref, z_ref, h_ref, q_ref, sum_ref):
    ns = sum_ref.shape[0]

    @pl.when(pl.program_id(0) == 0)
    def _():
        sum_ref[...] = jnp.zeros_like(sum_ref)

    z = mm(gn_ref[...], wn_ref[...]) + mm(gf_ref[...], wf_ref[...]) + b_ref[...]
    z_ref[...] = z
    h = (0.5 * twice_gelu(z)).astype(BF16)
    h_ref[...] = h
    q = mm(h, w3_ref[...])
    lane = lane_of(sum_ref.shape)
    sum_ref[...] += jnp.where(lane < LANES // 2, q[:ns], q[ns:])

    @pl.when(pl.program_id(0) == pl.num_programs(0) - 1)
    def _():
        q_ref[...] = jnp.where(lane == LANES - 1, here_ref[...], sum_ref[...]).astype(BF16)


def layer_two(g_near, g_far, near, far, b_second, w3, here, wide=512):
    rows, n_near = g_near.shape
    ns = rows // MB
    whole = lambda f: (0, 0)
    return call(
        layer_two_kernel,
        "layer_two",
        (shaped((rows, HID)), shaped((rows, HID), BF16), shaped((ns, LANES), BF16)),
        [
            pl.BlockSpec((rows, n_near), whole),
            pl.BlockSpec((rows, n_near), whole),
            pl.BlockSpec((n_near, wide), lambda f: (0, f)),
            pl.BlockSpec((n_near, wide), lambda f: (0, f)),
            pl.BlockSpec((1, wide), lambda f: (0, f)),
            pl.BlockSpec((wide, LANES), lambda f: (f, 0)),
            pl.BlockSpec((1, LANES), whole),
        ],
        (
            pl.BlockSpec((rows, wide), lambda f: (0, f)),
            pl.BlockSpec((rows, wide), lambda f: (0, f)),
            pl.BlockSpec((ns, LANES), whole),
        ),
        grid=(HID // wide,),
        scratch=[pltpu.VMEM((ns, LANES), F32)],
    )(g_near, g_far, near, far, b_second, w3, here)


def logits_kernel(n_z, *refs):
    strips, q_refs, (near_ref, far_ref) = refs[: MB * n_z], refs[MB * n_z : -2], refs[-2:]
    half = near_ref.shape[0]
    lane = lane_of((2 * half, LANES))
    sums = [None] * MB
    for i in range(n_z):
        all_q = jnp.concatenate([q[i] for q in q_refs], 0)
        for m in range(MB):
            part = mm(strips[m * n_z + i][...], all_q)
            sums[m] = part if sums[m] is None else sums[m] + part
    out = jnp.where(lane < LANES // 2, sums[0], sums[1])
    count = sum(jnp.sum(q[:, 0:1, :].astype(F32), axis=0) for q in q_refs)
    out = jnp.where(lane == LANES - 1, count, out)
    near_ref[...] = out[:half]
    far_ref[...] = out[half:]


def logits_parts(strips, q_rows):
    n_z = len(strips[0])
    rows, across = strips[0][0].shape
    out = shaped((rows // 2, LANES))
    return call(
        lambda *refs: logits_kernel(n_z, *refs),
        "logits_parts",
        (out, out),
        [pl.BlockSpec((rows, across), lambda i: (0, 0))] * (MB * n_z) + [IN_VMEM] * len(q_rows),
        (IN_VMEM, IN_VMEM),
        grid=(1,),
    )(*strips[0], *strips[1], *q_rows)


def loss_kernel(near_ref, got_ref, q_ref, diag_ref, bias_ref, labels_ref, counted_ref, ds_ref, row_ref):
    total = near_ref[...] + got_ref[...]
    node_total = total[0:1, LANES - 1 :]
    lane = lane_of(total.shape)
    low = lane < LANES // 2
    at = jnp.where(low, lane, lane - LANES // 2)
    real = at < NCLS
    pick = lambda ref: jnp.where(low, ref[:, 0:1], ref[:, 1:2])
    logits = total + LAMBDA * pick(diag_ref) * q_ref[...].astype(F32) + bias_ref[...]
    least = jnp.float32(-3.0e38)
    hits = jnp.logical_and(real, at == pick(labels_ref))
    counted = pick(counted_ref)
    parts = []
    for side in (jnp.logical_and(real, low), jnp.logical_and(real, jnp.logical_not(low))):
        top = jnp.max(jnp.where(side, logits, least), axis=1, keepdims=True)
        powers = jnp.where(side, jnp.exp(jnp.where(side, logits - top, 0.0)), 0.0)
        parts.append((top, jnp.sum(powers, axis=1, keepdims=True)))
    log_total = jnp.where(
        low, parts[0][0] + jnp.log(parts[0][1]), parts[1][0] + jnp.log(parts[1][1])
    )
    loss = jnp.where(hits, counted * (log_total - logits), 0.0)
    soft = jnp.exp(jnp.where(real, logits - log_total, 0.0))
    d_logits = jnp.where(real, counted * (soft - hits.astype(F32)) / node_total, 0.0)
    ds_ref[...] = d_logits.astype(BF16)
    row_ref[0:1] = jnp.sum(d_logits, axis=0, keepdims=True)
    row_ref[1:2] = jnp.broadcast_to(jnp.sum(jnp.sum(loss, axis=0, keepdims=True), axis=1, keepdims=True), (1, LANES))
    row_ref[2:3] = jnp.broadcast_to(node_total, (1, LANES))
    row_ref[3:8] = jnp.zeros((5, LANES), F32)


def d_q_kernel(n_z, *refs):
    tile_refs, s_refs, out_refs = refs[: MB * n_z], refs[MB * n_z : (MB + 1) * n_z], refs[(MB + 1) * n_z :]
    side = out_refs[0].shape[0]
    lane = lane_of((side * len(out_refs), LANES))
    sums = [None] * MB
    for i in range(n_z):
        all_s = jnp.concatenate([s_refs[i][core] for core in (0, 1)], 0)
        for m in range(MB):
            part = mm_t(tile_refs[m * n_z + i][...], all_s)
            sums[m] = part if sums[m] is None else sums[m] + part
    out = jnp.where(lane < LANES // 2, sums[0], sums[1])
    for k, out_ref in enumerate(out_refs):
        out_ref[...] = out[k * side : (k + 1) * side]


def d_q_parts(tile, pieces):
    n_z = len(pieces)
    rows, across = tile[0][0].shape
    n = across // BLK
    return call(
        lambda *refs: d_q_kernel(n_z, *refs),
        "d_q_parts",
        (shaped((BLK, LANES)),) * n,
        [pl.BlockSpec((rows, across), lambda i: (0, 0))] * (MB * n_z) + [IN_VMEM] * n_z,
        (IN_VMEM,) * n,
        grid=(1,),
    )(*tile[0], *tile[1], *pieces)


def d_two_kernel(n_q, *refs):
    q_refs = refs[:n_q]
    ds_ref, diag_ref, z_ref, h_ref, w3_ref, g_ref, dz_ref, db_ref, dw3_ref, far_ref = refs[n_q:]
    ns = ds_ref.shape[0]
    d_q = q_refs[0][...]
    for q in q_refs[1:]:
        d_q = d_q + q[...]
    low = lane_of(d_q.shape) < LANES // 2
    d_q = d_q + LAMBDA * jnp.where(low, diag_ref[:, 0:1], diag_ref[:, 1:2]) * ds_ref[...].astype(F32)
    d_q = jnp.concatenate([jnp.where(low, d_q, 0.0), jnp.where(low, 0.0, d_q)], 0).astype(BF16)
    d_z = mm_nt(d_q, w3_ref[...]) * (0.5 * twice_gelu_both(z_ref[...])[1])
    db_ref[...] = jnp.sum(d_z.reshape(-1, 8, d_z.shape[1]), axis=0)
    d_zb = d_z.astype(BF16)
    dz_ref[...] = d_zb
    dw3_ref[...] = mm_t(h_ref[...], d_q)
    far_ref[...] = mm_t(g_ref[...], d_zb).astype(BF16)


def d_two(d_q, d_s, diag, z_two, h_two, w3, g_far, lo, hi, wide=256):
    rows = z_two.shape[0]
    ns, n_far = d_s.shape[0], g_far.shape[1]
    whole = lambda f: (0, 0)
    start = lo // wide
    small = pl.BlockSpec((ns, LANES), whole)
    column = pl.BlockSpec((rows, wide), lambda f: (0, start + f))
    span = hi - lo
    return call(
        lambda *refs: d_two_kernel(len(d_q), *refs),
        "d_two",
        (
            shaped((rows, span), BF16),
            shaped((8, span)),
            shaped((span, LANES)),
            shaped((n_far, span), BF16),
        ),
        [small] * (len(d_q) + 1)
        + [
            pl.BlockSpec((ns, MB), whole),
            column,
            column,
            pl.BlockSpec((wide, LANES), lambda f: (start + f, 0)),
            pl.BlockSpec((rows, n_far), whole),
        ],
        (
            pl.BlockSpec((rows, wide), lambda f: (0, f)),
            pl.BlockSpec((8, wide), lambda f: (0, f)),
            pl.BlockSpec((wide, LANES), lambda f: (f, 0)),
            pl.BlockSpec((n_far, wide), lambda f: (0, f)),
        ),
        grid=(span // wide,),
        room=4,
    )(*d_q, d_s, diag, z_two, h_two, w3, g_far)


def near_kernel(keep, send, rows, g_ref, dz_ref, got_ref, keep_ref, send_ref, done_ref):
    done_ref[...] = jnp.zeros_like(done_ref)
    total = mm_t(g_ref[...], dz_ref[...]) + got_ref[...].astype(F32)
    for out_ref, picks in ((keep_ref, keep), (send_ref, send)):
        for i, j in enumerate(picks):
            out_ref[i * rows : (i + 1) * rows] = total[j * rows : (j + 1) * rows].astype(out_ref.dtype)


def near_part(g_near, d_zb, got, n_rows, bit, wide=256):
    n_near, span = got.shape
    rows = n_near // n_rows
    keep = [j for j in range(n_rows) if not j & bit]
    send = [j | bit for j in keep]
    column = lambda n: pl.BlockSpec((n, wide), lambda f: (0, f))
    return call(
        lambda *refs: near_kernel(keep, send, rows, *refs),
        "near_part",
        (shaped((n_near // 2, span)), shaped((n_near // 2, span), BF16), shaped((8, LANES))),
        [pl.BlockSpec(g_near.shape, lambda f: (0, 0)), column(g_near.shape[0]), column(n_near)],
        (column(n_near // 2), column(n_near // 2), pl.BlockSpec((8, LANES), lambda f: (0, 0))),
        grid=(span // wide,),
    )(g_near, d_zb, got)


def backward_kernel(n_z, n_rows, *refs):
    g_refs, strip_refs = refs[:n_rows], refs[n_rows : n_rows + MB * n_z]
    slope_refs, (dgn_ref, dgf_ref, diag_ref, dw_ref) = refs[-4 - MB : -4], refs[-4:]
    own = dgn_ref.shape[1]
    total = None
    for m in range(MB):
        d_g = jnp.concatenate([dgn_ref[m], dgf_ref[m]], 0)
        for i in range(n_z):
            d_h = mm_t(strip_refs[m * n_z + i][...], d_g)
            n = d_h.shape[0]
            if i == 0:
                more = LAMBDA * diag_ref[:, m : m + 1] * dgn_ref[m].astype(F32)
                d_h = jnp.concatenate([d_h[:own] + more, d_h[own:]], 0)
            g = jnp.concatenate([g_ref[i, m] for g_ref in g_refs], 0)
            d_z = d_h * slope_refs[m][i * n : (i + 1) * n].astype(F32)
            part = mm_t(g, d_z.astype(BF16))
            total = part if total is None else total + part
    dw_ref[...] = (0.5 * total).astype(BF16)


def backward_one(g_all, strips, slopes, d_g_near, d_g_far, diag, lo, hi, wide=256):
    n_rows, n_z = len(g_all), len(strips[0])
    rows, across = strips[0][0].shape
    span = hi - lo
    start = lo // wide
    column = pl.BlockSpec((MB, rows // 2, wide), lambda f: (0, 0, start + f))
    return call(
        lambda *refs: backward_kernel(n_z, n_rows, *refs),
        "backward_one",
        shaped((LANES, span), BF16),
        [pl.BlockSpec(g_all[0].shape, lambda f: (0, 0, 0, 0))] * n_rows
        + [pl.BlockSpec((rows, across), lambda f: (0, 0))] * (MB * n_z)
        + [pl.BlockSpec((n_z * across, wide), lambda f: (0, start + f))] * MB
        + [column, column, pl.BlockSpec((rows // 2, MB), lambda f: (0, 0))],
        pl.BlockSpec((LANES, wide), lambda f: (0, f)),
        grid=(span // wide,),
        room=2 + 8 * across // 1024,
    )(*g_all, *strips[0], *strips[1], *slopes, d_g_near, d_g_far, diag)


def d_g_kernel(n_blocks, cuts, *refs):
    dz_refs, (which_ref, wn_ref, wf_ref, out_ref, sum_ref) = refs[: len(cuts)], refs[len(cuts) :]
    step = pl.program_id(0)

    @pl.when(step == 0)
    def _():
        sum_ref[...] = jnp.zeros_like(sum_ref)

    def add(w_ref):
        part = sum(mm_nt(dz[...], w_ref[:, lo:hi]) for dz, (lo, hi) in zip(dz_refs, cuts)).astype(BF16)
        which = which_ref[...]
        hot = one_hot(lax.broadcasted_iota(jnp.int32, (which.shape[0], HID), 1), which)
        sum_ref[...] += mm(part, hot)

    @pl.when(step < n_blocks)
    def _():
        add(wn_ref)

    @pl.when(step >= n_blocks)
    def _():
        add(wf_ref)

    @pl.when(step == pl.num_programs(0) - 1)
    def _():
        out_ref[...] = sum_ref[...].astype(BF16)


def d_g_two(d_zb, cuts, which, near, far):
    rows, n_near = d_zb[0].shape[0], near.shape[0]
    wide = block_width(n_near)
    n = n_near // wide
    return call(
        lambda *refs: d_g_kernel(n, cuts, *refs),
        "d_g_two",
        shaped((rows, HID), BF16),
        [pl.BlockSpec(d.shape, lambda k: (0, 0)) for d in d_zb]
        + [
            pl.BlockSpec((wide, 1), lambda k: (k, 0)),
            pl.BlockSpec((wide, HID), lambda k: (jnp.minimum(k, n - 1), 0)),
            pl.BlockSpec((wide, HID), lambda k: (jnp.maximum(k - n, 0), 0)),
        ],
        pl.BlockSpec((rows, HID), lambda k: (0, 0)),
        grid=(2 * n,),
        scratch=[pltpu.VMEM((rows, HID), F32)],
        room=8,
    )(*d_zb, which, near, far)


def thirds_kernel(row_ref, out_ref):
    rest = row_ref[...]
    out_ref[...] = jnp.zeros_like(out_ref)
    for i in range(3):
        low = rest.astype(BF16)
        out_ref[i : i + 1] = low
        rest = rest - low.astype(F32)


def thirds(row):
    return call(thirds_kernel, "thirds", shaped((16, LANES), BF16), [IN_VMEM], IN_VMEM)(row)


def join_kernel(sizes, *refs):
    pieces, out_ref, sems = refs[: len(sizes)], refs[len(sizes)], refs[-1]
    at, copies = 0, []
    for i, (piece, size) in enumerate(zip(pieces, sizes)):
        copies.append(pltpu.make_async_copy(piece, out_ref.at[pl.ds(at, size)], sems.at[i]))
        copies[-1].start()
        at += size
    for copy in copies:
        copy.wait()


def join(pieces):
    sizes = [p.shape[0] for p in pieces]
    return call(
        lambda *refs: join_kernel(sizes, *refs),
        "join",
        shaped((sum(sizes),) + pieces[0].shape[1:], pieces[0].dtype),
        [ANYWHERE] * len(pieces),
        IN_VMEM,
        room=2,
        scratch=[pltpu.SemaphoreType.DMA((len(pieces),))],
    )(*pieces)


def per_device(features, adjacency, block_mask, diagonal, labels, train_mask, params, first_moment, second_moment):
    n_rows, n_cols = lax.axis_size("rows"), lax.axis_size("cols")
    n_z = n_cols // 2
    n_dev = n_rows * n_cols
    my_row, my_col = lax.axis_index("rows"), lax.axis_index("cols")
    me = my_row * n_cols + my_col
    ns = features.shape[1]
    z_bits, row_bits = bits_of(n_z), bits_of(n_rows)
    turned = row_bits[1:] + row_bits[:1]
    single = z_bits[::-1]
    several = [j for j in range(1, n_z) if j not in single]
    z_order = [0] + single + several

    def over_z(x):
        return [x] + [swap(x, "cols", 2 * j) for j in z_order[1:]]

    def over_rows(x):
        return [x] + [swap(x, "rows", j) for j in range(1, n_rows)]

    n_own = params.shape[0] // LANES
    slot = -(-((n_own + UNIT - 2) // UNIT + 1) // 8) * 8
    shift = lax.rem(n_own * me, UNIT)
    own = lax.dynamic_update_slice(
        jnp.zeros((slot * UNIT, LANES), BF16), params.reshape(n_own, LANES).astype(BF16), (shift, 0)
    ).reshape(1, slot, HID)
    wide_feats = jnp.pad(features, ((0, 0), (0, 0), (0, LANES - FIN)))
    ones = lax.broadcasted_iota(jnp.int32, (1, 1, LANES), 2) == FIN
    feats = over_rows(wide_feats)
    tile, leave = masked_tile(
        adjacency.reshape(MB, -1, n_rows, LANES), block_mask, [2 * j + core for j in z_order for core in (0, 1)], my_col, my_row
    )

    part_near, part_far = layer_one(tile, feats)
    own = after(own, part_far)
    by_z = {0: own}
    for j in single:
        by_z[j] = swap(own, "cols", 2 * j)
    partial = part_near + swap(part_far, "cols", 1)
    g_one = partial[0] + LAMBDA * diagonal[:, :, None] * wide_feats.astype(F32)
    low = partial.astype(BF16)
    for i, j in enumerate(z_order[1:], 1):
        g_one = g_one + swap(low[i], "cols", 2 * j).astype(F32)
    g_one = jnp.where(ones, 1.0, g_one).astype(BF16)

    def units_of(core):
        owner = (my_row ^ jnp.arange(n_rows))[:, None] * n_cols + (
            my_col ^ (2 * jnp.array(z_order) + core)
        )[None, :]
        start = (n_own * owner) // UNIT
        return (start[:, :, None] + jnp.arange(slot)[None, None, :]).reshape(-1)

    near_units = units_of(0)
    units = jnp.concatenate([near_units, units_of(1)])
    which = units - FIN

    middle = after(join([by_z[j] for j in single]), g_one)
    for j in several:
        bit = j & -j
        by_z[j] = swap(by_z[j - bit], "cols", 2 * bit)
    last = by_z[several[0]] if len(several) == 1 else join([by_z[j] for j in several])
    g_z = over_z(g_one)
    last = after(last, *g_z[1:])
    groups = [own, middle, last]
    g_all = over_rows(jnp.stack(g_z))
    strips = [[tile[m][0]] for m in range(MB)]
    for i, j in enumerate(z_order[1:]):
        strips[0].append(swap(after(leave[0][i], *g_all[1:]), "cols", 2 * j))
    passed = {0: groups}
    for j in range(1, n_rows):
        lowest = j & -j
        highest = 1 << (j.bit_length() - 1)
        hop = [passed[j - bit][i] for i, bit in enumerate((highest, lowest, highest))]
        if lowest != highest:
            once = [x for i in passed if i for x in passed[i]]
            hop = [after(h, *g_all[1:], *[x for x in once if x is not h]) for h in hop]
        passed[j] = [swap(h, "rows", bit) for h, bit in zip(hop, (highest, lowest, highest))]
    for m in range(1, MB):
        for i, j in enumerate(z_order[1:]):
            strips[m].append(swap(after(leave[m][i], *strips[m - 1][1:]), "cols", 2 * j))
    passed[0][0] = after(passed[0][0], *strips[0][1:])
    near = join([g.reshape(-1, HID) for j in range(n_rows) for g in passed[j]])
    far = swap(near, "cols", 1)
    n_near = near.shape[0]

    per_small = -(-(FIN + NCLS + 3) // n_dev)
    n_small = per_small * n_dev
    small_unit = jnp.arange(n_small)
    small_unit = jnp.where(small_unit < FIN, small_unit, small_unit + HID)
    pick = (small_unit[:, None] == near_units[None, :]).astype(BF16)
    small = mm(pick, near).astype(BF16)
    small = small + swap(small, "cols", 1)
    w_pad = jnp.concatenate(
        [small[:FIN], small[FIN + NCLS : FIN + NCLS + 1], jnp.zeros((LANES - FIN - 1, HID), BF16)], 0
    )
    w_third = small[FIN : FIN + NCLS].reshape(HID, NCLS)
    gap = jnp.zeros((HID, LANES // 2 - NCLS), BF16)
    w_third = jnp.concatenate([w_third, gap, w_third, gap], 1)
    b_second = small[FIN + NCLS + 1].astype(F32)[None]
    b_third = small[FIN + NCLS + 2].astype(F32)[: LANES // 2]
    b_third = jnp.concatenate([b_third, b_third])[None]

    near_parts, far_parts, slopes = [], [], []
    for m in range(MB):
        if m == MB - 1:
            w_pad = after(w_pad, w_third)
        part_near, part_far, slope = forward_two(g_all, w_pad, strips[m], m)
        slopes.append(slope)
        near_parts.append(part_near)
        far_parts.append(swap(part_far, "cols", 1))

    diag = diagonal.T
    counted = train_mask.T.astype(F32)
    here = jnp.broadcast_to(jnp.sum(counted), (1, LANES))
    g_near, g_far = spread_two(
        near_parts, far_parts, g_one.reshape(MB * ns, LANES), w_pad, diag, which[None]
    )
    z_two, h_two, q = layer_two(g_near, g_far, near, far, b_second, w_third, here)

    part_near, part_far = logits_parts(strips, over_rows(jnp.stack(over_z(q))))
    d_s, sums = call(
        loss_kernel,
        "loss",
        (shaped((ns, LANES), BF16), shaped((8, LANES))),
        [IN_VMEM] * 7,
        (IN_VMEM, IN_VMEM),
    )(part_near, swap(part_far, "cols", 1), q, diag, b_third, labels.T, counted)
    d_bias_three = sums[0, :NCLS] + sums[0, LANES // 2 : LANES // 2 + NCLS]
    loss, node_total = sums[1, 0], sums[2, 0]

    d_q = d_q_parts(tile, over_z(jnp.stack([d_s, swap(d_s, "cols", 1)])))
    d_q = [d_q[0]] + [swap(d_q[j], "rows", j) for j in range(1, n_rows)]

    def split(item, axis, bit):
        dim = 0 if axis == "rows" else 1
        kept, send, item["orders"][axis] = split_bit(item["part"], dim, item["orders"][axis], bit)
        item["kept"], item["send"] = kept, send.astype(BF16)
        item["to"] = (axis, bit * (dim + 1))

    half = HID // 2
    work = []
    for k, bits in enumerate((row_bits, turned)):
        lo, hi = k * half, (k + 1) * half
        d_zb, d_b, d_w3, d_far = d_two(d_q, d_s, diag, z_two, h_two, w_third, g_far, lo, hi)
        item = {"bits": bits, "dz": d_zb, "db": d_b, "dw3": d_w3}
        item["got"] = swap(d_far, "cols", 1)
        item["orders"] = {"rows": [j for j in range(n_rows) if not j & bits[0]], "cols": z_order}
        item["to"] = ("rows", bits[0])
        work.append(item)
    for item in work:
        kept, send, item["done"] = near_part(g_near, item["dz"], item["got"], n_rows, item["bits"][0])
        item["kept"], item["send"] = (x.reshape(n_rows // 2, n_z, slot, half) for x in (kept, send))
    d_zb = [item["dz"] for item in work]
    d_bias_two = jnp.concatenate([jnp.sum(item["db"], axis=0) for item in work])
    d_w_three = jnp.concatenate([item["dw3"] for item in work], 0)
    d_w_three = d_w_three[:, :NCLS] + d_w_three[:, LANES // 2 : LANES // 2 + NCLS]

    n_cuts = 3
    cuts = [0, 3 * (HID // 8), 6 * (HID // 8), HID]
    d_zb[0] = after(d_zb[0], *[item["done"] for item in work])
    d_g_near = d_g_two(d_zb, [(0, half), (half, HID)], which[:, None], near, far).reshape(MB, ns, HID)
    d_g_far = swap(d_g_near, "cols", 1)
    d_first = []

    def another_cut():
        i = len(d_first)
        if i < n_cuts:
            d_first.append(
                backward_one(g_all, strips, slopes, d_g_near, d_g_far, diag, cuts[i], cuts[i + 1])
            )

    for i in range(len(row_bits)):
        for item in work:
            item["part"] = item["kept"] + swap(item["send"], *item["to"]).astype(F32)
            if i + 1 < len(row_bits):
                split(item, "rows", item["bits"][i + 1])
        if i + 1 < len(row_bits):
            d_g_near = after(d_g_near, *[item["send"] for item in work])
            another_cut()
    item = {"orders": {"cols": z_order}, "part": jnp.concatenate([item["part"] for item in work], 3)}
    for bit in z_bits:
        split(item, "cols", bit)
        d_g_near = after(d_g_near, item["send"])
        another_cut()
        item["part"] = item["kept"] + swap(item["send"], *item["to"]).astype(F32)
    own_grad = item["part"][0, 0]
    d_first = jnp.concatenate(d_first, 1)
    d_w_one, d_bias_one = d_first[:FIN], d_first[FIN].astype(F32)

    d_small = jnp.concatenate(
        [
            d_w_one.astype(BF16),
            d_w_three.astype(BF16).reshape(NCLS, HID),
            jnp.stack([d_bias_one, d_bias_two, jnp.pad(d_bias_three, (0, HID - NCLS))]).astype(BF16),
            jnp.zeros((n_small - FIN - NCLS - 3, HID), BF16),
        ],
        0,
    )
    d_small = after(d_small.reshape(n_dev, per_small * UNIT, LANES), own_grad)
    got = lax.all_to_all(d_small, BOTH, split_axis=0, concat_axis=0, tiled=True)
    got = jnp.sum(got.astype(F32), axis=0)
    low = got.astype(BF16)

    own_flat = lax.dynamic_slice(own_grad.reshape(slot * UNIT, LANES), (shift, 0), (n_own, LANES))
    squares = jnp.sum(own_flat * own_flat) + jnp.sum(low.astype(F32) ** 2)
    row = jnp.concatenate([squares[None], loss[None], d_bias_three, jnp.zeros((LANES - NCLS - 2,), F32)])
    sent = jnp.concatenate([low, thirds(row[None])], 0)
    sent = jnp.broadcast_to(sent[None], (n_dev,) + sent.shape)
    got = lax.all_to_all(sent, BOTH, split_axis=0, concat_axis=0, tiled=True)
    d_small = got[:, : per_small * UNIT].reshape(n_small, HID)
    row = jnp.sum(got[:, per_small * UNIT : per_small * UNIT + 3].astype(F32), axis=(0, 1))
    squares, loss_sum, class_sum = row[0], row[1], row[2 : 2 + NCLS]

    mine = (n_own * me) // UNIT + jnp.arange(slot)
    place = (mine[:, None] == small_unit[None, :]).astype(BF16)
    small_flat = lax.dynamic_slice(
        mm(place, d_small).reshape(slot * UNIT, LANES), (shift, 0), (n_own, LANES)
    )
    reduced = (own_flat + small_flat).reshape(-1)

    grad_norm = jnp.sqrt(squares)
    clip_scale = jnp.minimum(1.0, CLIP_NORM / (grad_norm + 1e-06))
    clipped = reduced * clip_scale
    class_bias_grad = class_sum * clip_scale
    new_first = BETA_ONE * first_moment + (1.0 - BETA_ONE) * clipped
    new_second = BETA_TWO * second_moment + (1.0 - BETA_TWO) * clipped * clipped
    correct_one = 1.0 - BETA_ONE**STEP
    correct_two = 1.0 - BETA_TWO**STEP
    step_size = new_first / correct_one / (jnp.sqrt(new_second / correct_two) + EPSILON)
    new_params = params - LEARN_RATE * (step_size + WEIGHT_DECAY * params)
    return (new_params, new_first, new_second, grad_norm, loss_sum, node_total, class_bias_grad)


def solution(mesh):
    in_specs = (
        P(None, ("rows", "cols"), None),
        P(None, "rows", None, "cols", None),
        P(None, "rows", None, "cols", None),
        P(None, ("rows", "cols")),
        P(None, ("rows", "cols")),
        P(None, ("rows", "cols")),
        P(("rows", "cols")),
        P(("rows", "cols")),
        P(("rows", "cols")),
    )
    out_specs = (P(("rows", "cols")), P(("rows", "cols")), P(("rows", "cols")), P(), P(), P(), P())
    return jax.shard_map(
        per_device, mesh=mesh, in_specs=in_specs, out_specs=out_specs, check_vma=False
    )
```

```python
import math

import jax
import jax.numpy as jnp
from jax import lax
from jax.experimental import pallas as pl
from jax.experimental.pallas import tpu as pltpu
from jax.sharding import PartitionSpec as P

FIN = 100
HID = 2048
NCLS = 47
BLK = 128
MB = 2
STEP = 10
PARAMS = FIN * HID + HID * HID + HID * NCLS + 2 * HID + NCLS

LAMBDA = 1.0
CLIP_NORM = 0.01
BETA_ONE = 0.9
BETA_TWO = 0.95
EPSILON = 1e-08
WEIGHT_DECAY = 0.1
LEARN_RATE = 0.02

LANES = 128
UNIT = HID // LANES
BOTH = ("rows", "cols")
GELU_ONE = 0.7978845608028654
GELU_THREE = GELU_ONE * 0.044715
F32 = jnp.float32
FAR_BYTES = 1 << 17
BF16 = jnp.bfloat16


def swap(x, axis, bit):
    size = lax.axis_size(axis)
    return lax.ppermute(x, axis, [(i, i ^ bit) for i in range(size)])


def bits_of(size):
    return [1 << i for i in range(size.bit_length() - 1)]


def mm(left, right):
    return jnp.dot(left, right, preferred_element_type=F32)


def mm_t(left, right):
    return lax.dot_general(left, right, (((0,), (0,)), ((), ())), preferred_element_type=F32)


def mm_nt(left, right):
    return lax.dot_general(left, right, (((1,), (1,)), ((), ())), preferred_element_type=F32)


def take(x, axis, picks):
    return jnp.concatenate([lax.slice_in_dim(x, p, p + 1, axis=axis) for p in picks], axis)


def split_bit(x, axis, order, bit):
    keep = [j for j in order if not j & bit]
    run = next(i for i, j in enumerate(order) if j & bit)
    if any(bool(j & bit) != bool(i // run % 2) or j & ~bit != order[i - i // run % 2 * run] & ~bit for i, j in enumerate(order)):
        at = {j: i for i, j in enumerate(order)}
        return take(x, axis, [at[j] for j in keep]), take(x, axis, [at[j | bit] for j in keep]), keep
    shape = x.shape[:axis] + (len(order) // (2 * run), 2, run) + x.shape[axis + 1 :]
    kept_shape = x.shape[:axis] + (len(keep),) + x.shape[axis + 1 :]
    x = x.reshape(shape)
    pair = [lax.index_in_dim(x, i, axis + 1, keepdims=False).reshape(kept_shape) for i in (0, 1)]
    return pair[0], pair[1], keep


ANYWHERE = pl.BlockSpec(memory_space=pl.ANY)
IN_VMEM = pl.BlockSpec(memory_space=pltpu.VMEM)
IN_SMEM = pl.BlockSpec(memory_space=pltpu.SMEM)


def tip(x):
    while x.ndim > 2:
        x = x[0]
    return x[:8, :128].astype(F32)


def after_kernel(*refs):
    pass


def after(x, *earlier):
    earlier = [tip(e) for e in earlier]
    return pl.pallas_call(
        after_kernel,
        out_shape=jax.ShapeDtypeStruct(x.shape, x.dtype),
        in_specs=[ANYWHERE] * (1 + len(earlier)),
        out_specs=ANYWHERE,
        input_output_aliases={0: 0},
        name="after",
    )(x, *earlier)


def padded_bytes(shape, dtype):
    *front, rows, lanes = (1, 1, *shape)
    size = -(-rows // 16) * 16 * -(-lanes // LANES) * LANES * jnp.dtype(dtype).itemsize
    for n in front:
        size *= n
    return size


def call(kernel, name, out_shape, in_specs, out_specs, grid=None, room=4, scratch=()):
    more = {} if grid is None else {"grid": grid}

    def run(*args):
        outs = out_shape if isinstance(out_shape, tuple) else (out_shape,)
        specs = (*in_specs, *(out_specs if isinstance(out_specs, tuple) else (out_specs,)))
        total = room << 20
        for spec, x in zip(specs, (*args, *outs)):
            if spec.block_shape is not None:
                total += 2 * padded_bytes(spec.block_shape, x.dtype)
            elif spec.memory_space == pltpu.VMEM:
                total += padded_bytes(x.shape, x.dtype)
        large = lambda x: math.prod(x.shape) * x.dtype.itemsize >= FAR_BYTES
        args = [pltpu.with_memory_space_constraint(x, pltpu.HBM) if large(x) else x for x in args]
        placed = [
            pltpu.HBM(x.shape, x.dtype) if large(x) and spec.block_shape is not None else x
            for spec, x in zip(specs[len(args) :], outs)
        ]
        return pl.pallas_call(
            kernel,
            out_shape=tuple(placed) if isinstance(out_shape, tuple) else placed[0],
            in_specs=in_specs,
            out_specs=out_specs,
            scratch_shapes=list(scratch),
            compiler_params=pltpu.CompilerParams(vmem_limit_bytes=total),
            cost_estimate=pl.CostEstimate(flops=0, bytes_accessed=0, transcendentals=0),
            name=name,
            **more,
        )(*args)

    return run


def shaped(shape, dtype=F32):
    return jax.ShapeDtypeStruct(shape, dtype)


def lane_of(shape):
    return lax.broadcasted_iota(jnp.int32, shape, len(shape) - 1)


def masked_tile_kernel(row_order, n_across, n_pieces, where_ref, mask_ref, tile_ref, *refs):
    out_refs, wide_ref = refs[:-1], refs[-1]
    col, row = where_ref[0], where_ref[1]
    tall = BLK * n_across
    per_piece = len(row_order) // n_pieces
    for m in range(MB):
        for i, j in enumerate(row_order):
            block = col ^ j
            wide_ref[...] = tile_ref[m, pl.ds(pl.multiple_of(block * tall, tall), tall), :].astype(F32)
            piece, low = i // per_piece, i % per_piece * BLK
            for k in range(n_across):
                keep = mask_ref[(m * len(row_order) + block) * n_across + k].astype(F32)
                part = (wide_ref[pl.ds(k, BLK, n_across), :] * keep).astype(BF16)
                lanes = pl.ds(pl.multiple_of((row ^ k) * BLK, BLK), BLK)
                out_refs[m * n_pieces + piece][low : low + BLK, lanes] = part
                if piece:
                    at = MB * n_pieces + m * (n_pieces - 1) + piece - 1
                    out_refs[at][low : low + BLK, lanes] = part


def masked_tile(adjacency, block_mask, row_order, my_col, my_row):
    n_across = adjacency.shape[2]
    n_pieces = len(row_order) // 2
    piece = shaped((2 * BLK, n_across * BLK), BF16)
    n_out = MB * (2 * n_pieces - 1)
    out = call(
        lambda *refs: masked_tile_kernel(row_order, n_across, n_pieces, *refs),
        "masked_tile",
        (piece,) * n_out,
        [IN_SMEM, IN_SMEM, pl.BlockSpec((MB, adjacency.shape[1] * n_across, LANES), lambda i: (0, 0, 0))],
        (pl.BlockSpec((2 * BLK, n_across * BLK), lambda i: (0, 0)),) * n_out,
        grid=(1,),
        room=4,
        scratch=[pltpu.VMEM((n_across * BLK, LANES), F32)],
    )(
        jnp.stack([my_col, my_row]).astype(jnp.int32),
        block_mask.reshape(-1),
        adjacency.reshape(MB, -1, LANES),
    )
    tile = [out[m * n_pieces : (m + 1) * n_pieces] for m in range(MB)]
    leave = out[MB * n_pieces :]
    return tile, [leave[m * (n_pieces - 1) : (m + 1) * (n_pieces - 1)] for m in range(MB)]


def layer_one_kernel(n_z, *refs):
    tile_refs, feat_refs, (near_ref, far_ref) = refs[: MB * n_z], refs[MB * n_z : -2], refs[-2:]
    ns = near_ref.shape[2]
    for m in range(MB):
        feats = jnp.concatenate([f[m] for f in feat_refs], 0)
        for i in range(n_z):
            out = mm(tile_refs[m * n_z + i][...], feats)
            near_ref[i, m] = out[:ns]
            far_ref[i, m] = out[ns:]


def layer_one(tile, feats):
    n_z = len(tile[0])
    half, across = tile[0][0].shape
    out = shaped((n_z, MB, half // 2, LANES))
    return call(
        lambda *refs: layer_one_kernel(n_z, *refs),
        "layer_one",
        (out, out),
        [pl.BlockSpec((half, across), lambda i: (0, 0))] * (MB * n_z) + [IN_VMEM] * len(feats),
        (IN_VMEM, IN_VMEM),
        grid=(1,),
    )(*tile[0], *tile[1], *feats)


def twice_gelu(z):
    return z + z * jnp.tanh(z * (GELU_ONE + GELU_THREE * (z * z)))


def twice_gelu_both(z):
    square = z * z
    t = jnp.tanh(z * (GELU_ONE + GELU_THREE * square))
    slope = z * (GELU_ONE + (3 * GELU_THREE) * square)
    above = 1.0 + t
    return z * above, above * (1.0 + (1.0 - t) * slope)


def forward_kernel(n_z, n_rows, m, *refs):
    g_refs, strip_refs = refs[:n_rows], refs[n_rows : n_rows + n_z]
    w_ref, near_ref, far_ref, slope_ref = refs[n_rows + n_z :]
    half = near_ref.shape[0]
    total = None
    for i in range(n_z):
        g = jnp.concatenate([g_ref[i, m] for g_ref in g_refs], 0)
        h, slope = twice_gelu_both(mm(g, w_ref[...]))
        n = g.shape[0]
        slope_ref[i * n : (i + 1) * n] = slope.astype(BF16)
        part = mm(strip_refs[i][...], h.astype(BF16))
        total = part if total is None else total + part
    near_ref[...] = 0.5 * total[:half]
    far_ref[...] = (0.5 * total[half:]).astype(BF16)


def forward_two(g_all, w_pad, strip, m, wide=256):
    n_rows, n_z = len(g_all), len(strip)
    rows, across = strip[0].shape
    span = w_pad.shape[1]
    n = n_z * across
    return call(
        lambda *refs: forward_kernel(n_z, n_rows, m, *refs),
        "forward_two",
        (shaped((rows // 2, span)), shaped((rows // 2, span), BF16), shaped((n, span), BF16)),
        [pl.BlockSpec(g_all[0].shape, lambda f: (0, 0, 0, 0))] * n_rows
        + [pl.BlockSpec((rows, across), lambda f: (0, 0))] * n_z
        + [pl.BlockSpec((LANES, wide), lambda f: (0, f))],
        (pl.BlockSpec((rows // 2, wide), lambda f: (0, f)),) * 2 + (pl.BlockSpec((n, wide), lambda f: (0, f)),),
        grid=(span // wide,),
        room=2 + 8 * across // 1024,
    )(*g_all, *strip, w_pad)


def one_hot(here, there):
    return jnp.where(here == there, 1.0, 0.0).astype(BF16)


def spread_kernel(n_m, n_blocks, *refs):
    near_parts, far_parts = refs[:n_m], refs[n_m : 2 * n_m]
    g_one_ref, w_ref, diag_ref, which_ref, gn_ref, gf_ref, g_ref = refs[2 * n_m :]
    ns = near_parts[0].shape[0]

    @pl.when(pl.program_id(0) == 0)
    def _():
        step = 256
        for at in range(0, HID, step):
            cut = slice(at, at + step)
            h = (0.5 * twice_gelu(mm(g_one_ref[...], w_ref[:, cut]))).astype(BF16)
            for m in range(n_m):
                g_ref[m * ns : (m + 1) * ns, cut] = (
                    near_parts[m][:, cut]
                    + far_parts[m][:, cut].astype(F32)
                    + LAMBDA * diag_ref[:, m : m + 1] * h[m * ns : (m + 1) * ns].astype(F32)
                ).astype(BF16)

    which = which_ref[...]
    hot = one_hot(lax.broadcasted_iota(jnp.int32, (HID, which.shape[1]), 0), which)
    out = mm(g_ref[...], hot).astype(BF16)

    @pl.when(pl.program_id(0) < n_blocks)
    def _():
        gn_ref[...] = out

    @pl.when(pl.program_id(0) >= n_blocks)
    def _():
        gf_ref[...] = out


def block_width(n):
    return 384 if n % 384 == 0 else LANES


def spread_two(near_parts, far_parts, g_one, w_pad, diag, which):
    ns = near_parts[0].shape[0]
    n_m = len(near_parts)
    n_near = which.shape[1] // 2
    rows = n_m * ns
    wide = block_width(n_near)
    n = n_near // wide
    whole = lambda k: (0, 0)
    out = shaped((rows, n_near), BF16)
    return call(
        lambda *refs: spread_kernel(n_m, n, *refs),
        "spread_two",
        (out, out),
        [pl.BlockSpec((ns, HID), whole)] * (2 * n_m)
        + [
            pl.BlockSpec((rows, LANES), whole),
            pl.BlockSpec((LANES, HID), whole),
            pl.BlockSpec((ns, n_m), whole),
            pl.BlockSpec((1, wide), lambda k: (0, k)),
        ],
        (
            pl.BlockSpec((rows, wide), lambda k: (0, jnp.minimum(k, n - 1))),
            pl.BlockSpec((rows, wide), lambda k: (0, jnp.maximum(k - n, 0))),
        ),
        grid=(2 * n,),
        scratch=[pltpu.VMEM((rows, HID), BF16)],
        room=8,
    )(*near_parts, *far_parts, g_one, w_pad, diag, which)


def layer_two_kernel(gn_ref, gf_ref, wn_ref, wf_ref, b_ref, w3_ref, here_ref, z_ref, h_ref, q_ref, sum_ref):
    ns = sum_ref.shape[0]

    @pl.when(pl.program_id(0) == 0)
    def _():
        sum_ref[...] = jnp.zeros_like(sum_ref)

    z = mm(gn_ref[...], wn_ref[...]) + mm(gf_ref[...], wf_ref[...]) + b_ref[...]
    z_ref[...] = z
    h = (0.5 * twice_gelu(z)).astype(BF16)
    h_ref[...] = h
    q = mm(h, w3_ref[...])
    lane = lane_of(sum_ref.shape)
    sum_ref[...] += jnp.where(lane < LANES // 2, q[:ns], q[ns:])

    @pl.when(pl.program_id(0) == pl.num_programs(0) - 1)
    def _():
        q_ref[...] = jnp.where(lane == LANES - 1, here_ref[...], sum_ref[...]).astype(BF16)


def layer_two(g_near, g_far, near, far, b_second, w3, here, wide=512):
    rows, n_near = g_near.shape
    ns = rows // MB
    whole = lambda f: (0, 0)
    return call(
        layer_two_kernel,
        "layer_two",
        (shaped((rows, HID)), shaped((rows, HID), BF16), shaped((ns, LANES), BF16)),
        [
            pl.BlockSpec((rows, n_near), whole),
            pl.BlockSpec((rows, n_near), whole),
            pl.BlockSpec((n_near, wide), lambda f: (0, f)),
            pl.BlockSpec((n_near, wide), lambda f: (0, f)),
            pl.BlockSpec((1, wide), lambda f: (0, f)),
            pl.BlockSpec((wide, LANES), lambda f: (f, 0)),
            pl.BlockSpec((1, LANES), whole),
        ],
        (
            pl.BlockSpec((rows, wide), lambda f: (0, f)),
            pl.BlockSpec((rows, wide), lambda f: (0, f)),
            pl.BlockSpec((ns, LANES), whole),
        ),
        grid=(HID // wide,),
        scratch=[pltpu.VMEM((ns, LANES), F32)],
    )(g_near, g_far, near, far, b_second, w3, here)


def logits_kernel(n_z, *refs):
    strips, q_refs, (near_ref, far_ref) = refs[: MB * n_z], refs[MB * n_z : -2], refs[-2:]
    half = near_ref.shape[0]
    lane = lane_of((2 * half, LANES))
    sums = [None] * MB
    for i in range(n_z):
        all_q = jnp.concatenate([q[i] for q in q_refs], 0)
        for m in range(MB):
            part = mm(strips[m * n_z + i][...], all_q)
            sums[m] = part if sums[m] is None else sums[m] + part
    out = jnp.where(lane < LANES // 2, sums[0], sums[1])
    count = sum(jnp.sum(q[:, 0:1, :].astype(F32), axis=0) for q in q_refs)
    out = jnp.where(lane == LANES - 1, count, out)
    near_ref[...] = out[:half]
    far_ref[...] = out[half:]


def logits_parts(strips, q_rows):
    n_z = len(strips[0])
    rows, across = strips[0][0].shape
    out = shaped((rows // 2, LANES))
    return call(
        lambda *refs: logits_kernel(n_z, *refs),
        "logits_parts",
        (out, out),
        [pl.BlockSpec((rows, across), lambda i: (0, 0))] * (MB * n_z) + [IN_VMEM] * len(q_rows),
        (IN_VMEM, IN_VMEM),
        grid=(1,),
    )(*strips[0], *strips[1], *q_rows)


def loss_kernel(near_ref, got_ref, q_ref, diag_ref, bias_ref, labels_ref, counted_ref, ds_ref, row_ref):
    total = near_ref[...] + got_ref[...]
    node_total = total[0:1, LANES - 1 :]
    lane = lane_of(total.shape)
    low = lane < LANES // 2
    at = jnp.where(low, lane, lane - LANES // 2)
    real = at < NCLS
    pick = lambda ref: jnp.where(low, ref[:, 0:1], ref[:, 1:2])
    logits = total + LAMBDA * pick(diag_ref) * q_ref[...].astype(F32) + bias_ref[...]
    least = jnp.float32(-3.0e38)
    hits = jnp.logical_and(real, at == pick(labels_ref))
    counted = pick(counted_ref)
    parts = []
    for side in (jnp.logical_and(real, low), jnp.logical_and(real, jnp.logical_not(low))):
        top = jnp.max(jnp.where(side, logits, least), axis=1, keepdims=True)
        powers = jnp.where(side, jnp.exp(jnp.where(side, logits - top, 0.0)), 0.0)
        parts.append((top, jnp.sum(powers, axis=1, keepdims=True)))
    log_total = jnp.where(
        low, parts[0][0] + jnp.log(parts[0][1]), parts[1][0] + jnp.log(parts[1][1])
    )
    loss = jnp.where(hits, counted * (log_total - logits), 0.0)
    soft = jnp.exp(jnp.where(real, logits - log_total, 0.0))
    d_logits = jnp.where(real, counted * (soft - hits.astype(F32)) / node_total, 0.0)
    ds_ref[...] = d_logits.astype(BF16)
    row_ref[0:1] = jnp.sum(d_logits, axis=0, keepdims=True)
    row_ref[1:2] = jnp.broadcast_to(jnp.sum(jnp.sum(loss, axis=0, keepdims=True), axis=1, keepdims=True), (1, LANES))
    row_ref[2:3] = jnp.broadcast_to(node_total, (1, LANES))
    row_ref[3:8] = jnp.zeros((5, LANES), F32)


def d_q_kernel(n_z, *refs):
    tile_refs, s_refs, out_refs = refs[: MB * n_z], refs[MB * n_z : (MB + 1) * n_z], refs[(MB + 1) * n_z :]
    side = out_refs[0].shape[0]
    lane = lane_of((side * len(out_refs), LANES))
    sums = [None] * MB
    for i in range(n_z):
        all_s = jnp.concatenate([s_refs[i][core] for core in (0, 1)], 0)
        for m in range(MB):
            part = mm_t(tile_refs[m * n_z + i][...], all_s)
            sums[m] = part if sums[m] is None else sums[m] + part
    out = jnp.where(lane < LANES // 2, sums[0], sums[1])
    for k, out_ref in enumerate(out_refs):
        out_ref[...] = out[k * side : (k + 1) * side]


def d_q_parts(tile, pieces):
    n_z = len(pieces)
    rows, across = tile[0][0].shape
    n = across // BLK
    return call(
        lambda *refs: d_q_kernel(n_z, *refs),
        "d_q_parts",
        (shaped((BLK, LANES)),) * n,
        [pl.BlockSpec((rows, across), lambda i: (0, 0))] * (MB * n_z) + [IN_VMEM] * n_z,
        (IN_VMEM,) * n,
        grid=(1,),
    )(*tile[0], *tile[1], *pieces)


def d_two_kernel(n_q, *refs):
    q_refs = refs[:n_q]
    ds_ref, diag_ref, z_ref, h_ref, w3_ref, g_ref, dz_ref, db_ref, dw3_ref, far_ref = refs[n_q:]
    ns = ds_ref.shape[0]
    d_q = q_refs[0][...]
    for q in q_refs[1:]:
        d_q = d_q + q[...]
    low = lane_of(d_q.shape) < LANES // 2
    d_q = d_q + LAMBDA * jnp.where(low, diag_ref[:, 0:1], diag_ref[:, 1:2]) * ds_ref[...].astype(F32)
    d_q = jnp.concatenate([jnp.where(low, d_q, 0.0), jnp.where(low, 0.0, d_q)], 0).astype(BF16)
    d_z = mm_nt(d_q, w3_ref[...]) * (0.5 * twice_gelu_both(z_ref[...])[1])
    db_ref[...] = jnp.sum(d_z.reshape(-1, 8, d_z.shape[1]), axis=0)
    d_zb = d_z.astype(BF16)
    dz_ref[...] = d_zb
    dw3_ref[...] = mm_t(h_ref[...], d_q)
    far_ref[...] = mm_t(g_ref[...], d_zb).astype(BF16)


def d_two(d_q, d_s, diag, z_two, h_two, w3, g_far, lo, hi, wide=256):
    rows = z_two.shape[0]
    ns, n_far = d_s.shape[0], g_far.shape[1]
    whole = lambda f: (0, 0)
    start = lo // wide
    small = pl.BlockSpec((ns, LANES), whole)
    column = pl.BlockSpec((rows, wide), lambda f: (0, start + f))
    span = hi - lo
    return call(
        lambda *refs: d_two_kernel(len(d_q), *refs),
        "d_two",
        (
            shaped((rows, span), BF16),
            shaped((8, span)),
            shaped((span, LANES)),
            shaped((n_far, span), BF16),
        ),
        [small] * (len(d_q) + 1)
        + [
            pl.BlockSpec((ns, MB), whole),
            column,
            column,
            pl.BlockSpec((wide, LANES), lambda f: (start + f, 0)),
            pl.BlockSpec((rows, n_far), whole),
        ],
        (
            pl.BlockSpec((rows, wide), lambda f: (0, f)),
            pl.BlockSpec((8, wide), lambda f: (0, f)),
            pl.BlockSpec((wide, LANES), lambda f: (f, 0)),
            pl.BlockSpec((n_far, wide), lambda f: (0, f)),
        ),
        grid=(span // wide,),
        room=4,
    )(*d_q, d_s, diag, z_two, h_two, w3, g_far)


def near_kernel(keep, send, rows, g_ref, dz_ref, got_ref, keep_ref, send_ref, done_ref):
    done_ref[...] = jnp.zeros_like(done_ref)
    total = mm_t(g_ref[...], dz_ref[...]) + got_ref[...].astype(F32)
    for out_ref, picks in ((keep_ref, keep), (send_ref, send)):
        for i, j in enumerate(picks):
            out_ref[i * rows : (i + 1) * rows] = total[j * rows : (j + 1) * rows].astype(out_ref.dtype)


def near_part(g_near, d_zb, got, n_rows, bit, wide=256):
    n_near, span = got.shape
    rows = n_near // n_rows
    keep = [j for j in range(n_rows) if not j & bit]
    send = [j | bit for j in keep]
    column = lambda n: pl.BlockSpec((n, wide), lambda f: (0, f))
    return call(
        lambda *refs: near_kernel(keep, send, rows, *refs),
        "near_part",
        (shaped((n_near // 2, span)), shaped((n_near // 2, span), BF16), shaped((8, LANES))),
        [pl.BlockSpec(g_near.shape, lambda f: (0, 0)), column(g_near.shape[0]), column(n_near)],
        (column(n_near // 2), column(n_near // 2), pl.BlockSpec((8, LANES), lambda f: (0, 0))),
        grid=(span // wide,),
    )(g_near, d_zb, got)


def backward_kernel(n_z, n_rows, *refs):
    g_refs, strip_refs = refs[:n_rows], refs[n_rows : n_rows + MB * n_z]
    slope_refs, (dgn_ref, dgf_ref, diag_ref, dw_ref) = refs[-4 - MB : -4], refs[-4:]
    own = dgn_ref.shape[1]
    total = None
    for m in range(MB):
        d_g = jnp.concatenate([dgn_ref[m], dgf_ref[m]], 0)
        for i in range(n_z):
            d_h = mm_t(strip_refs[m * n_z + i][...], d_g)
            n = d_h.shape[0]
            if i == 0:
                more = LAMBDA * diag_ref[:, m : m + 1] * dgn_ref[m].astype(F32)
                d_h = jnp.concatenate([d_h[:own] + more, d_h[own:]], 0)
            g = jnp.concatenate([g_ref[i, m] for g_ref in g_refs], 0)
            d_z = d_h * slope_refs[m][i * n : (i + 1) * n].astype(F32)
            part = mm_t(g, d_z.astype(BF16))
            total = part if total is None else total + part
    dw_ref[...] = (0.5 * total).astype(BF16)


def backward_one(g_all, strips, slopes, d_g_near, d_g_far, diag, lo, hi, wide=256):
    n_rows, n_z = len(g_all), len(strips[0])
    rows, across = strips[0][0].shape
    span = hi - lo
    start = lo // wide
    column = pl.BlockSpec((MB, rows // 2, wide), lambda f: (0, 0, start + f))
    return call(
        lambda *refs: backward_kernel(n_z, n_rows, *refs),
        "backward_one",
        shaped((LANES, span), BF16),
        [pl.BlockSpec(g_all[0].shape, lambda f: (0, 0, 0, 0))] * n_rows
        + [pl.BlockSpec((rows, across), lambda f: (0, 0))] * (MB * n_z)
        + [pl.BlockSpec((n_z * across, wide), lambda f: (0, start + f))] * MB
        + [column, column, pl.BlockSpec((rows // 2, MB), lambda f: (0, 0))],
        pl.BlockSpec((LANES, wide), lambda f: (0, f)),
        grid=(span // wide,),
        room=2 + 8 * across // 1024,
    )(*g_all, *strips[0], *strips[1], *slopes, d_g_near, d_g_far, diag)


def d_g_kernel(n_blocks, cuts, *refs):
    dz_refs, (which_ref, wn_ref, wf_ref, out_ref, sum_ref) = refs[: len(cuts)], refs[len(cuts) :]
    step = pl.program_id(0)

    @pl.when(step == 0)
    def _():
        sum_ref[...] = jnp.zeros_like(sum_ref)

    def add(w_ref):
        part = sum(mm_nt(dz[...], w_ref[:, lo:hi]) for dz, (lo, hi) in zip(dz_refs, cuts)).astype(BF16)
        which = which_ref[...]
        hot = one_hot(lax.broadcasted_iota(jnp.int32, (which.shape[0], HID), 1), which)
        sum_ref[...] += mm(part, hot)

    @pl.when(step < n_blocks)
    def _():
        add(wn_ref)

    @pl.when(step >= n_blocks)
    def _():
        add(wf_ref)

    @pl.when(step == pl.num_programs(0) - 1)
    def _():
        out_ref[...] = sum_ref[...].astype(BF16)


def d_g_two(d_zb, cuts, which, near, far):
    rows, n_near = d_zb[0].shape[0], near.shape[0]
    wide = block_width(n_near)
    n = n_near // wide
    return call(
        lambda *refs: d_g_kernel(n, cuts, *refs),
        "d_g_two",
        shaped((rows, HID), BF16),
        [pl.BlockSpec(d.shape, lambda k: (0, 0)) for d in d_zb]
        + [
            pl.BlockSpec((wide, 1), lambda k: (k, 0)),
            pl.BlockSpec((wide, HID), lambda k: (jnp.minimum(k, n - 1), 0)),
            pl.BlockSpec((wide, HID), lambda k: (jnp.maximum(k - n, 0), 0)),
        ],
        pl.BlockSpec((rows, HID), lambda k: (0, 0)),
        grid=(2 * n,),
        scratch=[pltpu.VMEM((rows, HID), F32)],
        room=8,
    )(*d_zb, which, near, far)


def thirds_kernel(row_ref, out_ref):
    rest = row_ref[...]
    out_ref[...] = jnp.zeros_like(out_ref)
    for i in range(3):
        low = rest.astype(BF16)
        out_ref[i : i + 1] = low
        rest = rest - low.astype(F32)


def thirds(row):
    return call(thirds_kernel, "thirds", shaped((16, LANES), BF16), [IN_VMEM], IN_VMEM)(row)


def join_kernel(sizes, *refs):
    pieces, out_ref, sems = refs[: len(sizes)], refs[len(sizes)], refs[-1]
    at, copies = 0, []
    for i, (piece, size) in enumerate(zip(pieces, sizes)):
        copies.append(pltpu.make_async_copy(piece, out_ref.at[pl.ds(at, size)], sems.at[i]))
        copies[-1].start()
        at += size
    for copy in copies:
        copy.wait()


def join(pieces):
    sizes = [p.shape[0] for p in pieces]
    return call(
        lambda *refs: join_kernel(sizes, *refs),
        "join",
        shaped((sum(sizes),) + pieces[0].shape[1:], pieces[0].dtype),
        [ANYWHERE] * len(pieces),
        IN_VMEM,
        room=2,
        scratch=[pltpu.SemaphoreType.DMA((len(pieces),))],
    )(*pieces)


def per_device(features, adjacency, block_mask, diagonal, labels, train_mask, params, first_moment, second_moment):
    n_rows, n_cols = lax.axis_size("rows"), lax.axis_size("cols")
    n_z = n_cols // 2
    n_dev = n_rows * n_cols
    my_row, my_col = lax.axis_index("rows"), lax.axis_index("cols")
    me = my_row * n_cols + my_col
    ns = features.shape[1]
    z_bits, row_bits = bits_of(n_z), bits_of(n_rows)
    turned = row_bits[1:] + row_bits[:1]
    single = z_bits[::-1]
    several = [j for j in range(1, n_z) if j not in single]
    z_order = [0] + single + several

    def over_z(x):
        return [x] + [swap(x, "cols", 2 * j) for j in z_order[1:]]

    def over_rows(x):
        return [x] + [swap(x, "rows", j) for j in range(1, n_rows)]

    n_own = params.shape[0] // LANES
    slot = -(-((n_own + UNIT - 2) // UNIT + 1) // 8) * 8
    shift = lax.rem(n_own * me, UNIT)
    own = lax.dynamic_update_slice(
        jnp.zeros((slot * UNIT, LANES), BF16), params.reshape(n_own, LANES).astype(BF16), (shift, 0)
    ).reshape(1, slot, HID)
    wide_feats = jnp.pad(features, ((0, 0), (0, 0), (0, LANES - FIN)))
    ones = lax.broadcasted_iota(jnp.int32, (1, 1, LANES), 2) == FIN
    feats = over_rows(wide_feats)
    tile, leave = masked_tile(
        adjacency.reshape(MB, -1, n_rows, LANES), block_mask, [2 * j + core for j in z_order for core in (0, 1)], my_col, my_row
    )

    part_near, part_far = layer_one(tile, feats)
    own = after(own, part_far)
    by_z = {0: own}
    for j in single:
        by_z[j] = swap(own, "cols", 2 * j)
    partial = part_near + swap(part_far, "cols", 1)
    g_one = partial[0] + LAMBDA * diagonal[:, :, None] * wide_feats.astype(F32)
    low = partial.astype(BF16)
    for i, j in enumerate(z_order[1:], 1):
        g_one = g_one + swap(low[i], "cols", 2 * j).astype(F32)
    g_one = jnp.where(ones, 1.0, g_one).astype(BF16)

    def units_of(core):
        owner = (my_row ^ jnp.arange(n_rows))[:, None] * n_cols + (
            my_col ^ (2 * jnp.array(z_order) + core)
        )[None, :]
        start = (n_own * owner) // UNIT
        return (start[:, :, None] + jnp.arange(slot)[None, None, :]).reshape(-1)

    near_units = units_of(0)
    units = jnp.concatenate([near_units, units_of(1)])
    which = units - FIN

    middle = after(join([by_z[j] for j in single]), g_one)
    for j in several:
        bit = j & -j
        by_z[j] = swap(by_z[j - bit], "cols", 2 * bit)
    last = by_z[several[0]] if len(several) == 1 else join([by_z[j] for j in several])
    g_z = over_z(g_one)
    last = after(last, *g_z[1:])
    groups = [own, middle, last]
    g_all = over_rows(jnp.stack(g_z))
    strips = [[tile[m][0]] for m in range(MB)]
    for i, j in enumerate(z_order[1:]):
        strips[0].append(swap(after(leave[0][i], *g_all[1:]), "cols", 2 * j))
    passed = {0: groups}
    for j in range(1, n_rows):
        lowest = j & -j
        highest = 1 << (j.bit_length() - 1)
        hop = [passed[j - bit][i] for i, bit in enumerate((highest, lowest, highest))]
        if lowest != highest:
            once = [x for i in passed if i for x in passed[i]]
            hop = [after(h, *g_all[1:], *[x for x in once if x is not h]) for h in hop]
        passed[j] = [swap(h, "rows", bit) for h, bit in zip(hop, (highest, lowest, highest))]
    for m in range(1, MB):
        for i, j in enumerate(z_order[1:]):
            strips[m].append(swap(after(leave[m][i], strips[m - 1][1]), "cols", 2 * j))
    passed[0][0] = after(passed[0][0], *strips[0][1:])
    near = join([g.reshape(-1, HID) for j in range(n_rows) for g in passed[j]])
    far = swap(near, "cols", 1)
    n_near = near.shape[0]

    per_small = -(-(FIN + NCLS + 3) // n_dev)
    n_small = per_small * n_dev
    small_unit = jnp.arange(n_small)
    small_unit = jnp.where(small_unit < FIN, small_unit, small_unit + HID)
    pick = (small_unit[:, None] == near_units[None, :]).astype(BF16)
    small = mm(pick, near).astype(BF16)
    small = small + swap(small, "cols", 1)
    w_pad = jnp.concatenate(
        [small[:FIN], small[FIN + NCLS : FIN + NCLS + 1], jnp.zeros((LANES - FIN - 1, HID), BF16)], 0
    )
    w_third = small[FIN : FIN + NCLS].reshape(HID, NCLS)
    gap = jnp.zeros((HID, LANES // 2 - NCLS), BF16)
    w_third = jnp.concatenate([w_third, gap, w_third, gap], 1)
    b_second = small[FIN + NCLS + 1].astype(F32)[None]
    b_third = small[FIN + NCLS + 2].astype(F32)[: LANES // 2]
    b_third = jnp.concatenate([b_third, b_third])[None]

    near_parts, far_parts, slopes = [], [], []
    for m in range(MB):
        if m == MB - 1:
            w_pad = after(w_pad, w_third)
        part_near, part_far, slope = forward_two(g_all, w_pad, strips[m], m)
        slopes.append(slope)
        near_parts.append(part_near)
        far_parts.append(swap(part_far, "cols", 1))

    diag = diagonal.T
    counted = train_mask.T.astype(F32)
    here = jnp.broadcast_to(jnp.sum(counted), (1, LANES))
    g_near, g_far = spread_two(
        near_parts, far_parts, g_one.reshape(MB * ns, LANES), w_pad, diag, which[None]
    )
    z_two, h_two, q = layer_two(g_near, g_far, near, far, b_second, w_third, here)

    part_near, part_far = logits_parts(strips, over_rows(jnp.stack(over_z(q))))
    d_s, sums = call(
        loss_kernel,
        "loss",
        (shaped((ns, LANES), BF16), shaped((8, LANES))),
        [IN_VMEM] * 7,
        (IN_VMEM, IN_VMEM),
    )(part_near, swap(part_far, "cols", 1), q, diag, b_third, labels.T, counted)
    d_bias_three = sums[0, :NCLS] + sums[0, LANES // 2 : LANES // 2 + NCLS]
    loss, node_total = sums[1, 0], sums[2, 0]

    d_q = d_q_parts(tile, over_z(jnp.stack([d_s, swap(d_s, "cols", 1)])))
    d_q = [d_q[0]] + [swap(d_q[j], "rows", j) for j in range(1, n_rows)]

    def split(item, axis, bit):
        dim = 0 if axis == "rows" else 1
        kept, send, item["orders"][axis] = split_bit(item["part"], dim, item["orders"][axis], bit)
        item["kept"], item["send"] = kept, send.astype(BF16)
        item["to"] = (axis, bit * (dim + 1))

    half = HID // 2
    work = []
    for k, bits in enumerate((row_bits, turned)):
        lo, hi = k * half, (k + 1) * half
        d_zb, d_b, d_w3, d_far = d_two(d_q, d_s, diag, z_two, h_two, w_third, g_far, lo, hi)
        item = {"bits": bits, "dz": d_zb, "db": d_b, "dw3": d_w3}
        item["got"] = swap(d_far, "cols", 1)
        item["orders"] = {"rows": [j for j in range(n_rows) if not j & bits[0]], "cols": z_order}
        item["to"] = ("rows", bits[0])
        work.append(item)
    for item in work:
        kept, send, item["done"] = near_part(g_near, item["dz"], item["got"], n_rows, item["bits"][0])
        item["kept"], item["send"] = (x.reshape(n_rows // 2, n_z, slot, half) for x in (kept, send))
    d_zb = [item["dz"] for item in work]
    d_bias_two = jnp.concatenate([jnp.sum(item["db"], axis=0) for item in work])
    d_w_three = jnp.concatenate([item["dw3"] for item in work], 0)
    d_w_three = d_w_three[:, :NCLS] + d_w_three[:, LANES // 2 : LANES // 2 + NCLS]

    n_cuts = 3
    cuts = [0, 3 * (HID // 8), 6 * (HID // 8), HID]
    d_zb[0] = after(d_zb[0], *[item["done"] for item in work])
    d_g_near = d_g_two(d_zb, [(0, half), (half, HID)], which[:, None], near, far).reshape(MB, ns, HID)
    d_g_far = swap(d_g_near, "cols", 1)
    d_first = []

    def another_cut():
        i = len(d_first)
        if i < n_cuts:
            d_first.append(
                backward_one(g_all, strips, slopes, d_g_near, d_g_far, diag, cuts[i], cuts[i + 1])
            )

    for i in range(len(row_bits)):
        for item in work:
            item["part"] = item["kept"] + swap(item["send"], *item["to"]).astype(F32)
            if i + 1 < len(row_bits):
                split(item, "rows", item["bits"][i + 1])
        if i + 1 < len(row_bits):
            d_g_near = after(d_g_near, *[item["send"] for item in work])
            another_cut()
    item = {"orders": {"cols": z_order}, "part": jnp.concatenate([item["part"] for item in work], 3)}
    for bit in z_bits:
        split(item, "cols", bit)
        d_g_near = after(d_g_near, item["send"])
        another_cut()
        item["part"] = item["kept"] + swap(item["send"], *item["to"]).astype(F32)
    own_grad = item["part"][0, 0]
    d_first = jnp.concatenate(d_first, 1)
    d_w_one, d_bias_one = d_first[:FIN], d_first[FIN].astype(F32)

    d_small = jnp.concatenate(
        [
            d_w_one.astype(BF16),
            d_w_three.astype(BF16).reshape(NCLS, HID),
            jnp.stack([d_bias_one, d_bias_two, jnp.pad(d_bias_three, (0, HID - NCLS))]).astype(BF16),
            jnp.zeros((n_small - FIN - NCLS - 3, HID), BF16),
        ],
        0,
    )
    d_small = after(d_small.reshape(n_dev, per_small * UNIT, LANES), own_grad)
    got = lax.all_to_all(d_small, BOTH, split_axis=0, concat_axis=0, tiled=True)
    got = jnp.sum(got.astype(F32), axis=0)
    low = got.astype(BF16)

    own_flat = lax.dynamic_slice(own_grad.reshape(slot * UNIT, LANES), (shift, 0), (n_own, LANES))
    squares = jnp.sum(own_flat * own_flat) + jnp.sum(low.astype(F32) ** 2)
    row = jnp.concatenate([squares[None], loss[None], d_bias_three, jnp.zeros((LANES - NCLS - 2,), F32)])
    sent = jnp.concatenate([low, thirds(row[None])], 0)
    sent = jnp.broadcast_to(sent[None], (n_dev,) + sent.shape)
    got = lax.all_to_all(sent, BOTH, split_axis=0, concat_axis=0, tiled=True)
    d_small = got[:, : per_small * UNIT].reshape(n_small, HID)
    row = jnp.sum(got[:, per_small * UNIT : per_small * UNIT + 3].astype(F32), axis=(0, 1))
    squares, loss_sum, class_sum = row[0], row[1], row[2 : 2 + NCLS]

    mine = (n_own * me) // UNIT + jnp.arange(slot)
    place = (mine[:, None] == small_unit[None, :]).astype(BF16)
    small_flat = lax.dynamic_slice(
        mm(place, d_small).reshape(slot * UNIT, LANES), (shift, 0), (n_own, LANES)
    )
    reduced = (own_flat + small_flat).reshape(-1)

    grad_norm = jnp.sqrt(squares)
    clip_scale = jnp.minimum(1.0, CLIP_NORM / (grad_norm + 1e-06))
    clipped = reduced * clip_scale
    class_bias_grad = class_sum * clip_scale
    new_first = BETA_ONE * first_moment + (1.0 - BETA_ONE) * clipped
    new_second = BETA_TWO * second_moment + (1.0 - BETA_TWO) * clipped * clipped
    correct_one = 1.0 - BETA_ONE**STEP
    correct_two = 1.0 - BETA_TWO**STEP
    step_size = new_first / correct_one / (jnp.sqrt(new_second / correct_two) + EPSILON)
    new_params = params - LEARN_RATE * (step_size + WEIGHT_DECAY * params)
    return (new_params, new_first, new_second, grad_norm, loss_sum, node_total, class_bias_grad)


def solution(mesh):
    in_specs = (
        P(None, ("rows", "cols"), None),
        P(None, "rows", None, "cols", None),
        P(None, "rows", None, "cols", None),
        P(None, ("rows", "cols")),
        P(None, ("rows", "cols")),
        P(None, ("rows", "cols")),
        P(("rows", "cols")),
        P(("rows", "cols")),
        P(("rows", "cols")),
    )
    out_specs = (P(("rows", "cols")), P(("rows", "cols")), P(("rows", "cols")), P(), P(), P(), P())
    return jax.shard_map(
        per_device, mesh=mesh, in_specs=in_specs, out_specs=out_specs, check_vma=False
    )
```
